32 devices in a mesh: dp: 2 (over x), expert: 16 (over z, y, core).
Axes of the slice: x: 2, y: 2, z: 4, core: 2. Of those that a mesh axis runs over, the one named last changes fastest.
Arguments:
- hidden_in: bfloat16 [48, 4096], P('dp'), may hold values from -6 to 6
- norm_gain: float32 [4096], replicated, may hold values from 0.1 to 1.9
- route_ids: int32 [48, 8], P('dp'), may hold values from 0 to 15, all different within a row; in each aligned block of 24 rows (0 to 23, 24 to 47, ...) at most 24 rows name the same one
- route_gates: float32 [48, 8], P('dp'), may hold values from 0.05 to 0.5
- w_gate: bfloat16 [16, 4096, 1536], P('expert', None, 'dp'), may hold values from -0.09375 to 0.09375
- w_up: bfloat16 [16, 4096, 1536], P('expert', None, 'dp'), may hold values from -0.09375 to 0.09375
- w_down: bfloat16 [16, 1536, 4096], P('expert', 'dp'), may hold values from -0.15625 to 0.15625
- context: bfloat16 [48, 2048], P('dp', 'expert'), may hold values from -6 to 6
- w_out: bfloat16 [2048, 4096], P('expert'), may hold values from -0.125 to 0.125
- grad_out: bfloat16 [48, 4096], P('dp'), may hold values from -6 to 6
Outputs:
- output: bfloat16 [48, 4096], P('dp')
- d_hidden: bfloat16 [48, 4096], P('dp')
- d_context: bfloat16 [48, 2048], P('dp', 'expert')
- d_w_out: bfloat16 [2048, 4096], P('expert', 'dp')
The draws below stay inside these ranges and needn't reach their ends.
Inputs may be any that keep to these rules, and one draw needn't show every extreme that they name: `route_ids`: each token names 8 different experts. Among the 24 tokens of one index of dp no expert is named by more than 24 of them, and in every draw some expert is named by exactly 24.
All inputs are finite; a program needn't handle non-finite values.
Results may differ from the reference program's by a relative error of at most 0.013.
Values may be sent and summed in bfloat16 or wider, within the bound.
No kernel may reach another device: no remote copies, remote signals or barrier semaphores. Data moves between devices by JAX's collectives and lax.ppermute only.
A program may use at most 64 MiB of HBM per device.

```python
import math
import jax
import jax.numpy as jnp
import numpy as np
from jax import lax

D = 4096
FF = 1536
TOPK = 8
HD = 128
TOK_ROW = 24
EXPERTS = 16
HEADS = 16
MOST = 24
TOKENS = 48
N_DP = 2


def level_of(own_key, dims, shards, least, largest):
    loudness, own = 1.0, jax.random.fold_in(own_key, 6)
    for axis_at, parts in shards:
        heights = jnp.exp(jax.random.uniform(jax.random.fold_in(own, axis_at), (parts,), jnp.float32, least / len(shards), largest / len(shards)))
        loudness = loudness * jnp.repeat(heights, dims[axis_at] // parts).reshape([-1 if axis == axis_at else 1 for axis in range(len(dims))])
    return loudness


def shared_out(own_key, own, number, rows, amount, top, reach, lean):
    order = jax.random.permutation(own_key, amount)
    crowded, common = shares(amount, rows * top, reach, lean, True), shares(amount, rows * top, reach, lean, False)
    places = jnp.arange(amount)

    def named(lengths, turn):
        used = int((lengths > 0).sum())
        fixed = max(1, used // 4)
        shifted = fixed + (places - fixed + turn * (used - fixed)) % max(1, amount - fixed)
        return jnp.zeros((amount,), jnp.int32).at[order[jnp.where(places < fixed, places, shifted)]].set(jnp.asarray(lengths, jnp.int32))

    lengths = jnp.where(number % 4 == 0, named(crowded, number // 4), named(common, number - number // 4 - 1))
    mixed = jax.random.permutation(jax.random.fold_in(own, 3), amount)
    source_of, sink = mixed[0:amount // 2 * 2:2], mixed[1:amount // 2 * 2:2]
    room = jnp.minimum(lengths[source_of] - 1, reach - lengths[sink]) // 2
    room = jnp.where((source_of == order[0]) | (sink == order[0]) | (lengths[sink] == 0), 0, jnp.maximum(room, 0))
    shifted = jax.random.randint(jax.random.fold_in(own, 4), (amount // 2,), 0, 1 << 20) % (room + 1)
    lengths = lengths.at[source_of].add(-shifted).at[sink].add(shifted)
    members = jnp.searchsorted(jnp.cumsum(lengths), jnp.arange(rows * top), side="right").astype(jnp.int32)
    listing = members.reshape(top, rows).T
    listing = listing[jax.random.permutation(jax.random.fold_in(own, 1), rows)]
    turn = jax.random.randint(jax.random.fold_in(own, 2), (rows, 1), 0, top)
    return jnp.take_along_axis(listing, (jnp.arange(top)[None, :] + turn) % top, axis=1)


def shares(number_of, total, limit, slope, full):
    weights = [(1 << 20) // math.isqrt(rank ** slope) + 1 for rank in range(1, number_of + 1)]
    largest = limit if full else min(limit, max(-(-total // number_of), total * weights[0] // sum(weights)))
    least = 1 if total - largest >= number_of - 1 else 0
    counts, surplus = [largest] + [least] * (number_of - 1), total - largest - least * (number_of - 1)
    while surplus > 0:
        movable = [i for i in range(1, number_of) if counts[i] < largest] or [i for i in range(1, number_of) if counts[i] < limit]
        pool, remaining = sum([weights[i] for i in movable]), surplus
        for i in movable:
            more = min(limit - counts[i], max(1, remaining * weights[i] // pool), surplus)
            counts[i] = counts[i] + more
            surplus = surplus - more
    return np.array(counts)


def centred(key, dims, scale, bound, split=(), kind=jnp.bfloat16):
    level = level_of(key, dims, split, -0.22, 0.18) if split else 1.0
    array = jax.random.normal(key, dims, jnp.float32) * scale * level
    return jnp.minimum(jnp.maximum(array, -bound), bound).astype(kind)


def setup_inputs(seed: int = 0) -> dict:
    streams_of = jax.random.split(jax.random.key(seed), 11)
    hidden_in = centred(streams_of[0], (TOKENS, D), 1.0, 6.0, ((0, 2),))
    norm_gain = jnp.clip(1.0 + 0.18 * jax.random.normal(streams_of[1], (D,), jnp.float32), 0.1, 1.9)
    route_ids_keys = jax.random.split(jax.random.fold_in(streams_of[2], 1), TOKENS // TOK_ROW)
    route_ids_turns = jax.random.permutation(jax.random.fold_in(streams_of[2], 3), TOKENS // TOK_ROW)
    route_ids = jax.vmap(lambda own, number: shared_out(jax.random.fold_in(streams_of[2], 2), own, number, TOK_ROW, EXPERTS, TOPK, MOST, 2))(route_ids_keys, route_ids_turns).reshape((TOKENS, TOPK))
    route_gates = jnp.clip(jnp.exp(math.log(0.5) - 2.3025851 * jax.random.uniform(streams_of[3], (TOKENS, TOPK), jnp.float32) ** level_of(streams_of[3], (TOKENS, TOPK), ((0, 2),), -0.2, 0.2)), 0.05, 0.5)
    w_gate = centred(streams_of[4], (EXPERTS, D, FF), D ** -0.5, 0.09375, ((0, 16), (2, 2)))
    w_up = centred(streams_of[5], (EXPERTS, D, FF), D ** -0.5, 0.09375, ((0, 16), (2, 2)))
    w_down = centred(streams_of[6], (EXPERTS, FF, D), FF ** -0.5, 0.15625, ((0, 16), (1, 2)))
    context = centred(streams_of[7], (TOKENS, HEADS * HD), 1.0, 6.0, ((0, 2), (1, 16)))
    w_out = centred(streams_of[8], (HEADS * HD, D), (HEADS * HD) ** -0.5, 0.125, ((0, 16),))
    grad_out = centred(streams_of[9], (TOKENS, D), 1.0, 6.0, ((0, 2),))
    return {"hidden_in": hidden_in, "norm_gain": norm_gain, "route_ids": route_ids, "route_gates": route_gates, "w_gate": w_gate, "w_up": w_up, "w_down": w_down, "context": context, "w_out": w_out, "grad_out": grad_out}


EPSILON = 1e-06
EXACT = lax.Precision.HIGHEST

def rounded(values):
    return lax.optimization_barrier(values.astype(jnp.bfloat16)).astype(jnp.float32)

def reference(hidden_in, norm_gain, route_ids, route_gates, w_gate, w_up, w_down, context, w_out, grad_out):
    hidden32 = hidden_in.astype(jnp.float32)
    scale_inv = lax.rsqrt(lax.optimization_barrier(jnp.mean(hidden32 * hidden32, axis=1, keepdims=True)) + EPSILON)
    unit_rows = hidden32 * scale_inv
    normed = (unit_rows * norm_gain).astype(jnp.bfloat16)
    grad32 = grad_out.astype(jnp.float32)
    ids_rows = route_ids.reshape(N_DP, TOK_ROW, TOPK)
    gates_rows = route_gates.reshape(N_DP, TOK_ROW, TOPK)
    normed_rows = normed.astype(jnp.float32).reshape(N_DP, TOK_ROW, D)
    grad_rows = grad32.reshape(N_DP, TOK_ROW, D)
    block_width = FF // N_DP
    slot_index = jnp.arange(MOST, dtype=jnp.int32)

    def expert_step(carry, expert):
        matches = ids_rows == expert
        chosen = jnp.any(matches, axis=2)
        gate_sel = lax.optimization_barrier(jnp.sum(jnp.where(matches, gates_rows, jnp.float32(0.0)), axis=2))
        rank_rows = jnp.cumsum(chosen.astype(jnp.int32), axis=1) - 1
        places = jnp.where(chosen, rank_rows, -1)
        picker = (places[:, None, :] == slot_index[None, :, None]).astype(jnp.float32)
        rows_in = jnp.einsum('rst,rtd->rsd', picker, normed_rows, precision=EXACT).astype(jnp.bfloat16)
        gate_slot = jnp.einsum('rst,rt->rs', picker, gate_sel, precision=EXACT)
        grad_slot = jnp.einsum('rst,rtd->rsd', picker, grad_rows, precision=EXACT)
        rows_grad = (gate_slot[:, :, None] * grad_slot).astype(jnp.bfloat16)
        gate_w = w_gate[expert].astype(jnp.float32).reshape(D, N_DP, block_width)
        up_w = w_up[expert].astype(jnp.float32).reshape(D, N_DP, block_width)
        down_w = w_down[expert].astype(jnp.float32).reshape(N_DP, block_width, D)
        flat_in = rows_in.astype(jnp.float32).reshape(N_DP * MOST, D)
        flat_grad = rows_grad.astype(jnp.float32).reshape(N_DP * MOST, D)
        pre_gate = jnp.einsum('nd,dbf->nbf', flat_in, gate_w)
        pre_up = jnp.einsum('nd,dbf->nbf', flat_in, up_w)
        sig = jax.nn.sigmoid(pre_gate)
        act = rounded(pre_gate * sig * pre_up)
        out_part = rounded(jnp.einsum('nbf,bfd->nbd', act, down_w))
        expert_out = lax.optimization_barrier(jnp.sum(out_part, axis=1)).reshape(N_DP, MOST, D)
        back_act = jnp.einsum('nd,bfd->nbf', flat_grad, down_w)
        grad_gate = rounded(back_act * pre_up * sig * (1.0 + pre_gate * (1.0 - sig)))
        grad_up = rounded(back_act * pre_gate * sig)
        in_part = rounded(jnp.einsum('nbf,dbf->nbd', grad_gate, gate_w) + jnp.einsum('nbf,dbf->nbd', grad_up, up_w))
        expert_back = lax.optimization_barrier(jnp.sum(in_part, axis=1)).reshape(N_DP, MOST, D)
        moe_add = jnp.einsum('rst,rsd->rtd', picker * gate_slot[:, :, None], expert_out, precision=EXACT)
        back_add = jnp.einsum('rst,rsd->rtd', picker, expert_back, precision=EXACT)
        return ((carry[0] + moe_add, carry[1] + back_add), None)
    start_sums = (jnp.zeros((N_DP, TOK_ROW, D), jnp.float32), jnp.zeros((N_DP, TOK_ROW, D), jnp.float32))
    (moe_sum, normed_grad), _ = lax.scan(expert_step, start_sums, jnp.arange(EXPERTS, dtype=jnp.int32))
    moe_sum = moe_sum.reshape(TOKENS, D)
    normed_grad = normed_grad.reshape(TOKENS, D)
    output = (hidden32 + moe_sum).astype(jnp.bfloat16)
    scaled = normed_grad * norm_gain
    centre = lax.optimization_barrier(jnp.mean(scaled * unit_rows, axis=1, keepdims=True))
    d_hidden = (grad32 + scale_inv * (scaled - unit_rows * centre)).astype(jnp.bfloat16)
    d_context = jnp.dot(d_hidden, w_out.T, preferred_element_type=jnp.float32).astype(jnp.bfloat16)
    d_w_out = jnp.dot(context.T, d_hidden, preferred_element_type=jnp.float32).astype(jnp.bfloat16)
    return (output, d_hidden, d_context, d_w_out)
```

```python
import jax
import jax.numpy as jnp
from jax import lax
from jax.sharding import PartitionSpec as P

EPSILON = 1e-06
F32 = jnp.float32
BF16 = jnp.bfloat16


def from_ahead(value, step, count):
    return lax.ppermute(value, "dp", [((i + step) % count, i) for i in range(count)])


def blocks_of(value, count):
    return jnp.stack([value] + [from_ahead(value, k, count) for k in range(1, count)])


def reduce_all(part, n_dp, n_e):
    rows, width = part.shape[0] // n_dp, part.shape[1] // n_e
    shares = part.reshape(n_dp, rows, n_e, width).transpose(0, 2, 1, 3).reshape(n_dp * n_e, rows, width)
    arrived = lax.all_to_all(shares, ("dp", "expert"), 0, 0, tiled=True)
    total = jnp.sum(arrived.astype(F32), axis=0).astype(BF16)
    spread = lax.all_gather(total, "expert", axis=0, tiled=False)
    return spread.transpose(1, 0, 2).reshape(rows, part.shape[1])


def per_device(
    hidden_in, norm_gain, route_ids, route_gates, w_gate, w_up, w_down, context, w_out, grad_out
):
    n_dp, n_e = lax.axis_size("dp"), lax.axis_size("expert")
    me = lax.axis_index("dp")
    rows, width = hidden_in.shape
    expert = lax.axis_index("expert")
    gate_own = jnp.sum(jnp.where(route_ids == expert, route_gates, 0.0), axis=1, keepdims=True)
    order = lambda blocks: jnp.roll(blocks, me, axis=0).reshape((n_dp * rows,) + blocks.shape[2:])
    hidden = order(blocks_of(hidden_in, n_dp)).astype(F32)
    grads = order(blocks_of(grad_out, n_dp)).astype(F32)
    gates = order(blocks_of(gate_own, n_dp))
    contexts = blocks_of(context, n_dp).reshape(n_dp * rows, -1)

    scale_inv = lax.rsqrt(jnp.mean(hidden * hidden, axis=1, keepdims=True) + EPSILON)
    normed = (hidden * scale_inv * norm_gain).astype(BF16)
    rows_grad = (gates * grads).astype(BF16)
    dot = lambda a, b, dims: lax.dot_general(a, b, (dims, ((), ())), preferred_element_type=F32)
    wg, wu, wd = w_gate[0], w_up[0], w_down[0]
    pre_gate = dot(normed, wg, ((1,), (0,)))
    pre_up = dot(normed, wu, ((1,), (0,)))
    back_act = dot(rows_grad, wd, ((1,), (1,)))
    sig = jax.nn.sigmoid(pre_gate)
    grad_gate = (back_act * pre_up * sig * (1.0 + pre_gate * (1.0 - sig))).astype(BF16)
    grad_up = (back_act * pre_gate * sig).astype(BF16)
    in_part = dot(grad_gate, wg, ((1,), (1,))) + dot(grad_up, wu, ((1,), (1,)))
    normed_grad = reduce_all(in_part.astype(BF16), n_dp, n_e).astype(F32)
    act = (pre_gate * sig * pre_up).astype(BF16)
    out_part = gates * dot(act, wd, ((1,), (0,)))
    moe_sum = reduce_all(out_part.astype(BF16), n_dp, n_e).astype(F32)

    own = hidden_in.astype(F32)
    own_scale = lax.rsqrt(jnp.mean(own * own, axis=1, keepdims=True) + EPSILON)
    unit_rows = own * own_scale
    output = (own + moe_sum).astype(BF16)
    scaled = normed_grad * norm_gain
    centre = jnp.mean(scaled * unit_rows, axis=1, keepdims=True)
    d_hidden = (grad_out.astype(F32) + own_scale * (scaled - unit_rows * centre)).astype(BF16)
    d_context = dot(d_hidden, w_out, ((1,), (1,))).astype(BF16)
    part = width // n_dp
    columns = lambda k: lax.dynamic_slice_in_dim(d_hidden, ((me + k) % n_dp) * part, part, 1)
    pieces = [columns(0)]
    for k in range(1, n_dp):
        pieces.append(from_ahead(columns(n_dp - k), k, n_dp))
    d_w_out = dot(contexts, jnp.concatenate(pieces, axis=0), ((0,), (0,))).astype(BF16)
    return (output, d_hidden, d_context, d_w_out)


def solution(mesh):
    return jax.shard_map(
        per_device,
        mesh=mesh,
        in_specs=(
            P("dp", None),
            P(),
            P("dp", None),
            P("dp", None),
            P("expert", None, "dp"),
            P("expert", None, "dp"),
            P("expert", "dp", None),
            P("dp", "expert"),
            P("expert", None),
            P("dp", None),
        ),
        out_specs=(P("dp", None), P("dp", None), P("dp", "expert"), P("expert", "dp")),
        check_vma=False,
    )
```

```python
import jax
import jax.numpy as jnp
from jax import lax
from jax.sharding import PartitionSpec as P

EPSILON = 1e-06
F32 = jnp.float32
BF16 = jnp.bfloat16


def from_ahead(value, step, count):
    return lax.ppermute(value, "dp", [((i + step) % count, i) for i in range(count)])


def blocks_of(value, count):
    return jnp.stack([value] + [from_ahead(value, k, count) for k in range(1, count)])


def plane_sum(part, n_dp, n_lo):
    rows, width = part.shape[0] // n_dp, part.shape[1] // n_lo
    shares = part.reshape(n_dp, rows, n_lo, width).transpose(0, 2, 1, 3).reshape(n_dp * n_lo, rows, width)
    arrived = lax.all_to_all(shares, ("dp", "lo"), 0, 0, tiled=True)
    return jnp.sum(arrived.astype(F32), axis=0).astype(BF16)


def copies_sum(chunk, n_hi):
    arrived = lax.all_to_all(jnp.broadcast_to(chunk, (n_hi,) + chunk.shape), "hi", 0, 0, tiled=True)
    return jnp.sum(arrived.astype(F32), axis=0).astype(BF16)


def spread(chunk, axes, count, n_lo):
    rows, width = chunk.shape
    arrived = lax.all_to_all(jnp.broadcast_to(chunk, (count,) + chunk.shape), axes, 0, 0, tiled=True)
    blocks = arrived.reshape(count // n_lo, n_lo, rows, width).transpose(0, 2, 1, 3)
    return blocks.reshape(count // n_lo * rows, n_lo * width)


def per_device(
    hidden_in, norm_gain, route_ids, route_gates, w_gate, w_up, w_down, context, w_out, grad_out
):
    n_dp, n_hi, n_lo = (lax.axis_size(name) for name in ("dp", "hi", "lo"))
    me = lax.axis_index("dp")
    rows, width = hidden_in.shape
    expert = lax.axis_index("hi") * n_lo + lax.axis_index("lo")
    gate_own = jnp.sum(jnp.where(route_ids == expert, route_gates, 0.0), axis=1, keepdims=True)
    order = lambda blocks: jnp.roll(blocks, me, axis=0).reshape((n_dp * rows,) + blocks.shape[2:])
    hidden = order(blocks_of(hidden_in, n_dp)).astype(F32)
    grads = order(blocks_of(grad_out, n_dp)).astype(F32)
    gates = order(blocks_of(gate_own, n_dp))
    contexts = order(blocks_of(context, n_dp))

    scale_inv = lax.rsqrt(jnp.mean(hidden * hidden, axis=1, keepdims=True) + EPSILON)
    normed = (hidden * scale_inv * norm_gain).astype(BF16)
    rows_grad = (gates * grads).astype(BF16)
    dot = lambda a, b, dims: lax.dot_general(a, b, (dims, ((), ())), preferred_element_type=F32)
    wg, wu, wd = w_gate[0], w_up[0], w_down[0]
    pre_gate = dot(normed, wg, ((1,), (0,)))
    pre_up = dot(normed, wu, ((1,), (0,)))
    sig = jax.nn.sigmoid(pre_gate)
    act = (pre_gate * sig * pre_up).astype(BF16)
    out_part = (gates * dot(act, wd, ((1,), (0,)))).astype(BF16)
    out_plane = plane_sum(out_part, n_dp, n_lo)
    back_act = dot(rows_grad, wd, ((1,), (1,)))
    grad_gate = (back_act * pre_up * sig * (1.0 + pre_gate * (1.0 - sig))).astype(BF16)
    grad_up = (back_act * pre_gate * sig).astype(BF16)
    in_part = dot(grad_gate, wg, ((1,), (1,))) + dot(grad_up, wu, ((1,), (1,)))
    out_sum = copies_sum(out_plane, n_hi)
    in_plane = plane_sum(in_part.astype(BF16), n_dp, n_lo)
    moe_sum = spread(out_sum, "lo", n_lo, n_lo).astype(F32)
    in_sum = copies_sum(in_plane, n_hi)
    normed_grad = spread(in_sum, ("dp", "lo"), n_dp * n_lo, n_lo).astype(F32)

    output = (hidden_in.astype(F32) + moe_sum).astype(BF16)
    unit_rows = hidden * scale_inv
    scaled = normed_grad * norm_gain
    centre = jnp.mean(scaled * unit_rows, axis=1, keepdims=True)
    d_hidden = (grads + scale_inv * (scaled - unit_rows * centre)).astype(BF16)
    mine = lax.dynamic_slice_in_dim(d_hidden, me * rows, rows, 0)
    d_context = dot(mine, w_out, ((1,), (1,))).astype(BF16)
    part = width // n_dp
    columns = lax.dynamic_slice_in_dim(d_hidden, me * part, part, 1)
    d_w_out = dot(contexts, columns, ((0,), (0,))).astype(BF16)
    return (output, mine, d_context, d_w_out)


def low_count(n_dp, n_e):
    low = 1
    while n_e % (2 * low) == 0 and 2 * low * n_dp <= 2 * (n_e // (2 * low)):
        low = 2 * low
    return low


def solution(mesh):
    n_dp, n_e = mesh.shape["dp"], mesh.shape["expert"]
    low = low_count(n_dp, n_e)
    mesh = jax.sharding.Mesh(mesh.devices.reshape(n_dp, n_e // low, low), ("dp", "hi", "lo"))
    expert = ("hi", "lo")
    return jax.shard_map(
        per_device,
        mesh=mesh,
        in_specs=(
            P("dp", None),
            P(),
            P("dp", None),
            P("dp", None),
            P(expert, None, "dp"),
            P(expert, None, "dp"),
            P(expert, "dp", None),
            P("dp", expert),
            P(expert, None),
            P("dp", None),
        ),
        out_specs=(P("dp", None), P("dp", None), P("dp", expert), P(expert, "dp")),
        check_vma=False,
    )
```

```python
import functools

import jax
import jax.numpy as jnp
from jax import lax
from jax.experimental import pallas as pl
from jax.experimental.pallas import tpu as pltpu
from jax.sharding import PartitionSpec as P

EPSILON = 1e-06
F32 = jnp.float32
BF16 = jnp.bfloat16
STEP = 256
VMEM_LIMIT = 40 * 1024 * 1024


def dot(a, b, dims):
    return lax.dot_general(a, b, (dims, ((), ())), preferred_element_type=F32)


def place(step, count):
    return pl.multiple_of(step * count, count)


def rows_of(refs, columns):
    return jnp.concatenate([ref[:, columns].astype(F32) for ref in refs], axis=0)


def own_columns(ids, i, j, width):
    return ((ids[1] ^ j) * 2 + (ids[2] ^ i)) * width


def store_blocks(out_ref, j, columns, value, count):
    rows = value.shape[0] // count
    for k in range(count):
        out_ref[j, k, :, columns] = value[k * rows : (k + 1) * rows].astype(BF16)


def forward_kernel(n_dp, ids, *refs):
    hid, gates = refs[:n_dp], refs[n_dp : 2 * n_dp]
    gain, w_gate, w_up, w_down, pre_gate, pre_up, send, keep, normed, act = refs[2 * n_dp :]
    total = hid[0].shape[0] * n_dp
    width = hid[0].shape[1]
    chunk = send.shape[3]

    def squares(step, held):
        value = rows_of(hid, pl.ds(place(step, 512), 512))
        return held + jnp.sum(value * value, axis=1, keepdims=True)

    sums = lax.fori_loop(0, width // 512, squares, jnp.zeros((total, 1), F32))
    scale = lax.rsqrt(sums / width + EPSILON)

    def norm(step, carry):
        columns = pl.ds(place(step, 512), 512)
        normed[:, columns] = (rows_of(hid, columns) * scale * gain[:, columns]).astype(BF16)
        return carry

    lax.fori_loop(0, width // 512, norm, 0)

    def hidden_units(step, carry):
        columns = pl.ds(place(step, STEP), STEP)
        gate_part = dot(normed[...], w_gate[:, columns], ((1,), (0,)))
        up_part = dot(normed[...], w_up[:, columns], ((1,), (0,)))
        pre_gate[:, columns] = gate_part
        pre_up[:, columns] = up_part
        act[:, columns] = (gate_part * jax.nn.sigmoid(gate_part) * up_part).astype(BF16)
        return carry

    lax.fori_loop(0, w_gate.shape[1] // STEP, hidden_units, 0)
    weight = jnp.concatenate([gate[:, :1] for gate in gates], axis=0)
    for i, target in ((1, send), (0, keep)):
        for j in range(2):
            first = own_columns(ids, i, j, chunk)

            def outward(step, carry):
                columns = pl.ds(pl.multiple_of(first + step * STEP, STEP), STEP)
                part = weight * dot(act[...], w_down[:, columns], ((1,), (0,)))
                store_blocks(target, j, pl.ds(place(step, STEP), STEP), part, n_dp)
                return carry

            lax.fori_loop(0, chunk // STEP, outward, 0)


def inward_part(ids, i, n_dp, grad_gate, grad_up, w_gate, w_up, target):
    chunk = target.shape[3]
    for j in range(2):
        first = own_columns(ids, i, j, chunk)

        def inward(step, carry):
            columns = pl.ds(pl.multiple_of(first + step * STEP, STEP), STEP)
            part = dot(grad_gate[...], w_gate[columns, :], ((1,), (1,)))
            part = part + dot(grad_up[...], w_up[columns, :], ((1,), (1,)))
            store_blocks(target, j, pl.ds(place(step, STEP), STEP), part, n_dp)
            return carry

        lax.fori_loop(0, chunk // STEP, inward, 0)


def backward_kernel(n_dp, ids, *refs):
    grads, gates = refs[:n_dp], refs[n_dp : 2 * n_dp]
    pre_gate, pre_up, w_gate, w_up, w_down, grad_gate, grad_up, send, weighted = refs[2 * n_dp :]
    weight = jnp.concatenate([gate[:, :1] for gate in gates], axis=0)

    def weigh(step, carry):
        columns = pl.ds(place(step, 512), 512)
        weighted[:, columns] = (weight * rows_of(grads, columns)).astype(BF16)
        return carry

    lax.fori_loop(0, weighted.shape[1] // 512, weigh, 0)

    def hidden_units(step, carry):
        columns = pl.ds(place(step, STEP), STEP)
        back = dot(weighted[...], w_down[columns, :], ((1,), (1,)))
        gate_part, up_part = pre_gate[:, columns], pre_up[:, columns]
        sig = jax.nn.sigmoid(gate_part)
        grad_gate[:, columns] = (back * up_part * sig * (1.0 + gate_part * (1.0 - sig))).astype(BF16)
        grad_up[:, columns] = (back * gate_part * sig).astype(BF16)
        return carry

    lax.fori_loop(0, w_down.shape[0] // STEP, hidden_units, 0)
    inward_part(ids, 1, n_dp, grad_gate, grad_up, w_gate, w_up, send)


def keep_kernel(n_dp, ids, grad_gate, grad_up, w_gate, w_up, keep):
    inward_part(ids, 0, n_dp, grad_gate, grad_up, w_gate, w_up, keep)


def finish_kernel(n_dp, ids, *refs):
    hid, grads, contexts = refs[:n_dp], refs[n_dp : 2 * n_dp], refs[2 * n_dp : 3 * n_dp]
    gain, w_out, back_own, back_other, moe_own, moe_other = refs[3 * n_dp : 3 * n_dp + 6]
    output, d_hidden, d_context, d_w_out, summed, d_all = refs[3 * n_dp + 6 :]
    rows, width = hid[0].shape
    chunk = back_own.shape[3]
    for i, (back, moe) in enumerate(((back_own, moe_own), (back_other, moe_other))):
        for j in range(2):
            columns = pl.ds(pl.multiple_of(own_columns(ids, i, j, chunk), chunk), chunk)
            for k in range(n_dp):
                summed[k * rows : (k + 1) * rows, columns] = back[k, j].astype(F32) * gain[:, columns]
            output[:, columns] = (hid[0][:, columns].astype(F32) + moe[j].astype(F32)).astype(BF16)

    def sums(step, held):
        columns = pl.ds(place(step, 512), 512)
        value = rows_of(hid, columns)
        return (
            held[0] + jnp.sum(value * value, axis=1, keepdims=True),
            held[1] + jnp.sum(value * summed[:, columns], axis=1, keepdims=True),
        )

    zeros = jnp.zeros((rows * n_dp, 1), F32)
    squares, products = lax.fori_loop(0, width // 512, sums, (zeros, zeros))
    scale = lax.rsqrt(squares / width + EPSILON)
    centre = scale * products / width

    def total(step, carry):
        columns = pl.ds(place(step, 512), 512)
        unit_rows = rows_of(hid, columns) * scale
        value = rows_of(grads, columns) + scale * (summed[:, columns] - unit_rows * centre)
        d_all[:, columns] = value.astype(BF16)
        d_hidden[:, columns] = value[:rows].astype(BF16)
        return carry

    lax.fori_loop(0, width // 512, total, 0)
    d_context[...] = dot(d_hidden[...], w_out[...], ((1,), (1,))).astype(BF16)
    part = width // n_dp
    turned = jnp.concatenate([ref[...].astype(F32) for ref in contexts], axis=0).T.astype(BF16)
    step_width = min(part, 512)

    def product(step, carry):
        columns = pl.ds(pl.multiple_of(ids[0] * part + step * step_width, step_width), step_width)
        d_w_out[:, pl.ds(place(step, step_width), step_width)] = dot(
            turned, d_all[:, columns], ((1,), (0,))
        ).astype(BF16)
        return carry

    lax.fori_loop(0, part // step_width, product, 0)


def run(kernel, n_dp, ids, operands, outs, scratch, flops, name):
    held = [pltpu.with_memory_space_constraint(value, pltpu.VMEM) for value in operands]
    return pl.pallas_call(
        functools.partial(kernel, n_dp),
        out_shape=[pltpu.VMEM(shape, kind) for shape, kind in outs],
        in_specs=[pl.BlockSpec(memory_space=pltpu.SMEM)]
        + [pl.BlockSpec(memory_space=pltpu.VMEM)] * len(held),
        out_specs=[pl.BlockSpec(memory_space=pltpu.VMEM)] * len(outs),
        scratch_shapes=[pltpu.VMEM(shape, kind) for shape, kind in scratch],
        compiler_params=pltpu.CompilerParams(vmem_limit_bytes=VMEM_LIMIT),
        cost_estimate=pl.CostEstimate(flops=flops, bytes_accessed=flops // 96, transcendentals=0),
        name=name,
    )(ids, *held)


def per_device(
    hidden_in, norm_gain, route_ids, route_gates, w_gate, w_up, w_down, context, w_out, grad_out
):
    n_dp, n_hi = lax.axis_size("dp"), lax.axis_size("hi")
    me, hi, y, c = (lax.axis_index(name) for name in ("dp", "hi", "y", "c"))
    rows, width = hidden_in.shape
    all_rows, units, chunk = n_dp * rows, w_gate.shape[2], width // 4
    ids = jnp.stack([me, y, c]).astype(jnp.int32)

    def swap(value, axes, turn):
        sizes = [lax.axis_size(name) for name in axes]
        count = 1
        for size in sizes:
            count *= size
        return lax.ppermute(value, axes, [(i, i ^ turn) for i in range(count)])

    def all_blocks(value):
        return [value] + [swap(value, ("dp",), k) for k in range(1, n_dp)]

    hid = all_blocks(hidden_in)
    expert = (hi * 2 + y) * 2 + c
    gate_own = jnp.sum(jnp.where(route_ids == expert, route_gates, 0.0), axis=1, keepdims=True)
    small = all_blocks(
        jnp.concatenate([context.astype(F32), jnp.broadcast_to(gate_own, (rows, 128))], axis=1)
    )
    contexts = [value[:, : context.shape[1]] for value in small]
    gates = [value[:, context.shape[1] :] for value in small]
    grads = all_blocks(grad_out)
    gain = norm_gain.reshape(1, width)
    wg, wu, wd = w_gate[0], w_up[0], w_down[0]
    product = 2 * all_rows * width * units
    shares = ((2, n_dp, rows, chunk), BF16)

    def plane_share(send, keep):
        half = keep + swap(send, ("c",), 1)
        total = half[0, 0].astype(F32)
        pieces = [swap(half[t % 2, t // 2], ("dp", "y"), t) for t in range(1, 2 * n_dp)]
        for piece in pieces:
            total = total + piece.astype(F32)
        return total.astype(BF16)

    def column_sum(value):
        pieces = [swap(value, ("hi",), t) for t in range(1, n_hi)]
        total = value.astype(F32)
        for piece in pieces:
            total = total + piece.astype(F32)
        return total.astype(BF16)

    pre_gate, pre_up, out_send, out_keep = run(
        forward_kernel, n_dp, ids, hid + gates + [gain, wg, wu, wd],
        [((all_rows, units), F32), ((all_rows, units), F32), shares, shares],
        [((all_rows, width), BF16), ((all_rows, units), BF16)], 3 * product, "forward",
    )
    out_share = plane_share(out_send, out_keep)
    grad_gate, grad_up, in_send = run(
        backward_kernel, n_dp, ids, grads + gates + [pre_gate, pre_up, wg, wu, wd],
        [((all_rows, units), BF16), ((all_rows, units), BF16), shares],
        [((all_rows, width), BF16)], 2 * product, "backward",
    )
    (in_keep,) = run(
        keep_kernel, n_dp, ids, [grad_gate, grad_up, wg, wu], [shares], [], product, "backward_keep"
    )
    out_total = column_sum(out_share)
    in_share = plane_share(in_send, in_keep)
    moe_own = jnp.stack([out_total, swap(out_total, ("y",), 1)])
    in_total = column_sum(in_share)
    moe_other = swap(moe_own, ("c",), 1)
    pieces = [in_total] + [swap(in_total, ("dp", "y"), t) for t in range(1, 2 * n_dp)]
    back_own = jnp.stack(pieces).reshape(n_dp, 2, rows, chunk)
    back_other = swap(back_own, ("c",), 1)
    heads = context.shape[1]
    return run(
        finish_kernel, n_dp, ids,
        hid + grads + contexts + [gain, w_out, back_own, back_other, moe_own, moe_other],
        [((rows, width), BF16), ((rows, width), BF16), ((rows, heads), BF16), ((heads, width // n_dp), BF16)],
        [((all_rows, width), F32), ((all_rows, width), BF16)], product // 4, "finish",
    )


def solution(mesh):
    n_dp, n_e = mesh.shape["dp"], mesh.shape["expert"]
    names = ("dp", "hi", "y", "c")
    mesh = jax.sharding.Mesh(mesh.devices.reshape(n_dp, n_e // 4, 2, 2), names)
    expert = names[1:]
    return jax.shard_map(
        per_device,
        mesh=mesh,
        in_specs=(
            P("dp", None),
            P(),
            P("dp", None),
            P("dp", None),
            P(expert, None, "dp"),
            P(expert, None, "dp"),
            P(expert, "dp", None),
            P("dp", expert),
            P(expert, None),
            P("dp", None),
        ),
        out_specs=(P("dp", None), P("dp", None), P("dp", expert), P(expert, "dp")),
        check_vma=False,
    )
```

```python
import functools

import jax
import jax.numpy as jnp
from jax import lax
from jax.experimental import pallas as pl
from jax.experimental.pallas import tpu as pltpu
from jax.sharding import PartitionSpec as P

EPSILON = 1e-06
F32 = jnp.float32
BF16 = jnp.bfloat16
STEP = 256
LANES = 128
LOAD_PIECES = 4
FEW_ROWS = 64
VMEM_LIMIT = 12 * 1024 * 1024


def dot(a, b, dims):
    return lax.dot_general(a, b, (dims, ((), ())), preferred_element_type=F32)


def place(step, count):
    return pl.multiple_of(step * count, count)


def rows_of(refs, columns):
    return jnp.concatenate([ref[:, columns].astype(F32) for ref in refs], axis=0)


def own_columns(ids, i, j, width):
    return ((ids[1] ^ j) * 2 + (ids[2] ^ i)) * width


def store_blocks(out_ref, j, columns, value, count):
    rows = value.shape[0] // count
    for k in range(count):
        out_ref[j, k, :, columns] = value[k * rows : (k + 1) * rows].astype(BF16)


def load_kernel(n_dp, ids, w_gate, w_up, hid, grads, gain, named, weights, context, *refs):
    sources = (w_gate, w_up, hid, grads, gain)
    targets, small, named_held, weights_held, context_held, sems = (
        refs[:5], refs[5], refs[6], refs[7], refs[8], refs[9]
    )
    small_copies = [
        pltpu.make_async_copy(source, target, sems.at[n])
        for n, (source, target) in enumerate(
            ((named, named_held), (weights, weights_held), (context, context_held))
        )
    ]
    for copy in small_copies:
        copy.start()
    copies = []
    for source, target in zip(sources, targets):
        pieces = LOAD_PIECES if source.shape[0] % (LOAD_PIECES * 16) == 0 else 1
        part = source.shape[0] // pieces
        for p in range(pieces):
            block = pl.ds(p * part, part)
            where = (source.at[block], target.at[block]) if pieces > 1 else (source, target)
            copies.append(pltpu.make_async_copy(*where, sems.at[len(copies) + 3]))
    for copy in copies:
        copy.start()
    for copy in small_copies:
        copy.wait()
    rows = context_held.shape[0]
    row = jnp.sum(jnp.where(named_held[...] == ids[3], weights_held[...], 0.0), axis=0, keepdims=True)
    square = (rows, rows)
    diagonal = lax.broadcasted_iota(jnp.int32, square, 0) == lax.broadcasted_iota(jnp.int32, square, 1)
    gate = jnp.sum(jnp.where(diagonal, row, 0.0), axis=1, keepdims=True)
    heads = context_held.shape[1]
    small[:, :heads] = context_held[...].astype(F32)
    small[:, heads:] = jnp.broadcast_to(gate, (rows, LANES))
    for copy in copies:
        copy.wait()


def loop(count, body, unroll):
    if unroll:
        for step in range(count):
            body(step)
    else:
        def carried(step, carry):
            body(step)
            return carry

        lax.fori_loop(0, count, carried, 0)


def gates_of(smalls):
    return jnp.concatenate([small[:, small.shape[1] - LANES : small.shape[1] - LANES + 1] for small in smalls], axis=0)


def hidden_kernel(n_dp, ids, *refs):
    hid = refs[:n_dp]
    gain, w_gate, w_up, down_source, pre_gate, pre_up, act, w_down, normed, sem = refs[n_dp:]
    down_copy = pltpu.make_async_copy(down_source, w_down, sem)
    down_copy.start()
    total = hid[0].shape[0] * n_dp
    width = hid[0].shape[1]
    few = total <= FEW_ROWS
    sums = jnp.zeros((total, 1), F32)
    for step in range(width // 512):
        value = rows_of(hid, pl.ds(step * 512, 512))
        sums = sums + jnp.sum(value * value, axis=1, keepdims=True)
    scale = lax.rsqrt(sums / width + EPSILON)

    def norm(step):
        columns = pl.ds(place(step, 512), 512)
        normed[:, columns] = (rows_of(hid, columns) * scale * gain[:, columns]).astype(BF16)

    loop(width // 512, norm, few)

    def hidden_units(step):
        columns = pl.ds(place(step, STEP), STEP)
        gate_part = dot(normed[...], w_gate[:, columns], ((1,), (0,)))
        up_part = dot(normed[...], w_up[:, columns], ((1,), (0,)))
        pre_gate[:, columns] = gate_part
        pre_up[:, columns] = up_part
        act[:, columns] = (gate_part * jax.nn.sigmoid(gate_part) * up_part).astype(BF16)

    loop(w_gate.shape[1] // STEP, hidden_units, few)
    down_copy.wait()


def outward_kernel(n_dp, ids, *refs):
    smalls = refs[:n_dp]
    act, w_down, send, keep = refs[n_dp:]
    weight = gates_of(smalls)
    chunk = send.shape[3]
    few = act.shape[0] <= FEW_ROWS
    for i, target in ((1, send), (0, keep)):
        for j in range(2):
            first = own_columns(ids, i, j, chunk)

            def outward(step):
                columns = pl.ds(pl.multiple_of(first + step * STEP, STEP), STEP)
                part = weight * dot(act[...], w_down[:, columns], ((1,), (0,)))
                store_blocks(target, j, pl.ds(place(step, STEP), STEP), part, n_dp)

            loop(chunk // STEP, outward, few)


def inward_part(ids, i, n_dp, grad_gate, grad_up, w_gate, w_up, target):
    chunk = target.shape[3]
    few = grad_gate.shape[0] <= FEW_ROWS
    for j in range(2):
        first = own_columns(ids, i, j, chunk)

        def inward(step):
            columns = pl.ds(pl.multiple_of(first + step * STEP, STEP), STEP)
            part = dot(grad_gate[...], w_gate[columns, :], ((1,), (1,)))
            part = part + dot(grad_up[...], w_up[columns, :], ((1,), (1,)))
            store_blocks(target, j, pl.ds(place(step, STEP), STEP), part, n_dp)

        loop(chunk // STEP, inward, few)


def backward_kernel(n_dp, ids, *refs):
    grads, smalls = refs[:n_dp], refs[n_dp : 2 * n_dp]
    pre_gate, pre_up, w_gate, w_up, w_down, grad_gate, grad_up, send, weighted = refs[2 * n_dp :]
    weight = gates_of(smalls)
    few = weighted.shape[0] <= FEW_ROWS

    def weigh(step):
        columns = pl.ds(place(step, 512), 512)
        weighted[:, columns] = (weight * rows_of(grads, columns)).astype(BF16)

    loop(weighted.shape[1] // 512, weigh, few)

    def hidden_units(step):
        columns = pl.ds(place(step, STEP), STEP)
        back = dot(weighted[...], w_down[columns, :], ((1,), (1,)))
        gate_part, up_part = pre_gate[:, columns], pre_up[:, columns]
        sig = jax.nn.sigmoid(gate_part)
        grad_gate[:, columns] = (back * up_part * sig * (1.0 + gate_part * (1.0 - sig))).astype(BF16)
        grad_up[:, columns] = (back * gate_part * sig).astype(BF16)

    loop(w_down.shape[0] // STEP, hidden_units, few)
    inward_part(ids, 1, n_dp, grad_gate, grad_up, w_gate, w_up, send)


def keep_kernel(n_dp, ids, grad_gate, grad_up, w_gate, w_up, keep):
    inward_part(ids, 0, n_dp, grad_gate, grad_up, w_gate, w_up, keep)


def finish_kernel(n_dp, ids, *refs):
    hid, grads, smalls = refs[:n_dp], refs[n_dp : 2 * n_dp], refs[2 * n_dp : 3 * n_dp]
    gain, w_out, back_own, back_other, moe_own, moe_other = refs[3 * n_dp : 3 * n_dp + 6]
    output, d_hidden, d_context, d_w_out, summed, d_all = refs[3 * n_dp + 6 :]
    rows, width = hid[0].shape
    chunk = back_own.shape[3]
    for i, (back, moe) in enumerate(((back_own, moe_own), (back_other, moe_other))):
        for j in range(2):
            columns = pl.ds(pl.multiple_of(own_columns(ids, i, j, chunk), chunk), chunk)
            for k in range(n_dp):
                summed[k * rows : (k + 1) * rows, columns] = back[k, j].astype(F32) * gain[:, columns]
            output[:, columns] = (hid[0][:, columns].astype(F32) + moe[j].astype(F32)).astype(BF16)

    few = rows * n_dp <= FEW_ROWS
    squares = jnp.zeros((rows * n_dp, 1), F32)
    products = squares
    for step in range(width // 512):
        columns = pl.ds(step * 512, 512)
        value = rows_of(hid, columns)
        squares = squares + jnp.sum(value * value, axis=1, keepdims=True)
        products = products + jnp.sum(value * summed[:, columns], axis=1, keepdims=True)
    scale = lax.rsqrt(squares / width + EPSILON)
    centre = scale * products / width

    def total(step):
        columns = pl.ds(place(step, 512), 512)
        unit_rows = rows_of(hid, columns) * scale
        value = rows_of(grads, columns) + scale * (summed[:, columns] - unit_rows * centre)
        d_all[:, columns] = value.astype(BF16)
        d_hidden[:, columns] = value[:rows].astype(BF16)

    loop(width // 512, total, few)
    d_context[...] = dot(d_hidden[...], w_out[...], ((1,), (1,))).astype(BF16)
    part = width // n_dp
    heads = d_context.shape[1]
    turned = jnp.concatenate([small[:, :heads] for small in smalls], axis=0).T.astype(BF16)
    step_width = min(part, 512)

    def product(step):
        columns = pl.ds(pl.multiple_of(ids[0] * part + step * step_width, step_width), step_width)
        d_w_out[:, pl.ds(place(step, step_width), step_width)] = dot(
            turned, d_all[:, columns], ((1,), (0,))
        ).astype(BF16)

    loop(part // step_width, product, few)


def run(kernel, n_dp, ids, operands, outs, scratch, cost, name, far=(), out_space=pltpu.VMEM):
    spaces = [pltpu.HBM if n in far else pltpu.VMEM for n in range(len(operands))]
    held = [pltpu.with_memory_space_constraint(value, space) for value, space in zip(operands, spaces)]
    kinds = [
        pltpu.VMEM(shape, kind) if out_space is pltpu.VMEM else jax.ShapeDtypeStruct(shape, kind)
        for shape, kind in outs
    ]
    return pl.pallas_call(
        functools.partial(kernel, n_dp),
        out_shape=kinds,
        in_specs=[pl.BlockSpec(memory_space=pltpu.SMEM)]
        + [pl.BlockSpec(memory_space=space) for space in spaces],
        out_specs=[pl.BlockSpec(memory_space=pltpu.VMEM)] * len(outs),
        scratch_shapes=scratch,
        compiler_params=pltpu.CompilerParams(vmem_limit_bytes=VMEM_LIMIT),
        cost_estimate=pl.CostEstimate(flops=0, bytes_accessed=cost, transcendentals=0),
        name=name,
    )(ids, *held)


def per_device(
    hidden_in, norm_gain, route_ids, route_gates, w_gate, w_up, w_down, context, w_out, grad_out
):
    n_dp, n_hi = lax.axis_size("dp"), lax.axis_size("hi")
    me, hi, y, c = (lax.axis_index(name) for name in ("dp", "hi", "y", "c"))
    rows, width = hidden_in.shape
    top, heads = route_ids.shape[1], context.shape[1]
    all_rows, units, chunk = n_dp * rows, w_gate.shape[2], width // 4
    expert = (hi * 2 + y) * 2 + c
    ids = jnp.stack([me, y, c, expert]).astype(jnp.int32)

    def swap(value, axes, turn):
        sizes = [lax.axis_size(name) for name in axes]
        count = 1
        for size in sizes:
            count *= size
        return lax.ppermute(value, axes, [(i, i ^ turn) for i in range(count)])

    def all_blocks(value, own=None):
        own = value if own is None else own
        return [own] + [swap(value, ("dp",), k) for k in range(1, n_dp)]

    weights = 2 * width * units
    shares = ((2, n_dp, rows, chunk), BF16)
    wg, wu, hid_own, grads_own, gain, small_own = run(
        load_kernel, n_dp, ids,
        [w_gate[0], w_up[0], hidden_in, grad_out, norm_gain.reshape(1, width), route_ids.T, route_gates.T, context],
        [((width, units), BF16), ((width, units), BF16), ((rows, width), BF16), ((rows, width), BF16),
         ((1, width), F32), ((rows, heads + LANES), F32)],
        [pltpu.VMEM((top, rows), jnp.int32), pltpu.VMEM((top, rows), F32), pltpu.VMEM((rows, heads), BF16),
         pltpu.SemaphoreType.DMA((2 * LOAD_PIECES + 6,))],
        2 * weights, "load", far=range(8),
    )
    hid = all_blocks(hidden_in, hid_own)
    smalls = all_blocks(small_own)
    grads = all_blocks(grad_out, grads_own)

    def plane_halves(send, keep):
        return keep + swap(send, ("c",), 1)

    def plane_share(halves):
        totals = [half[0, 0].astype(F32) for half in halves]
        for t in range(1, 2 * n_dp):
            piece = swap(jnp.stack([half[t % 2, t // 2] for half in halves]), ("dp", "y"), t)
            totals = [total + piece[n].astype(F32) for n, total in enumerate(totals)]
        return [total.astype(BF16) for total in totals]

    def column_sum(value):
        pieces = [swap(value, ("hi",), t) for t in range(1, n_hi)]
        total = value.astype(F32)
        for piece in pieces:
            total = total + piece.astype(F32)
        return total.astype(BF16)

    pre_gate, pre_up, act, wd = run(
        hidden_kernel, n_dp, ids, hid + [gain, wg, wu, w_down[0]],
        [((all_rows, units), F32), ((all_rows, units), F32), ((all_rows, units), BF16), ((units, width), BF16)],
        [pltpu.VMEM((all_rows, width), BF16), pltpu.SemaphoreType.DMA], 2 * weights, "hidden", far=(n_dp + 3,),
    )
    out_send, out_keep = run(
        outward_kernel, n_dp, ids, smalls + [act, wd], [shares, shares], [], weights, "outward"
    )
    out_half = plane_halves(out_send, out_keep)
    grad_gate, grad_up, in_send = run(
        backward_kernel, n_dp, ids, grads + smalls + [pre_gate, pre_up, wg, wu, wd],
        [((all_rows, units), BF16), ((all_rows, units), BF16), shares],
        [pltpu.VMEM((all_rows, width), BF16)], 2 * weights, "backward",
    )
    (in_keep,) = run(
        keep_kernel, n_dp, ids, [grad_gate, grad_up, wg, wu], [shares], [], weights, "backward_keep"
    )
    in_half = plane_halves(in_send, in_keep)
    in_share, out_share = plane_share([in_half, out_half])
    in_total, out_total = column_sum(in_share), column_sum(out_share)
    pieces = [in_total] + [swap(in_total, ("dp", "y"), t) for t in range(1, 2 * n_dp)]
    back_own = jnp.stack(pieces).reshape(n_dp, 2, rows, chunk)
    back_other = swap(back_own, ("c",), 1)
    moe_own = jnp.stack([out_total, swap(out_total, ("y",), 1)])
    moe_other = swap(moe_own, ("c",), 1)
    return run(
        finish_kernel, n_dp, ids,
        hid + grads + smalls + [gain, w_out, back_own, back_other, moe_own, moe_other],
        [((rows, width), BF16), ((rows, width), BF16), ((rows, heads), BF16), ((heads, width // n_dp), BF16)],
        [pltpu.VMEM((all_rows, width), F32), pltpu.VMEM((all_rows, width), BF16)],
        weights, "finish", out_space=None,
    )


def solution(mesh):
    n_dp, n_e = mesh.shape["dp"], mesh.shape["expert"]
    names = ("dp", "hi", "y", "c")
    mesh = jax.sharding.Mesh(mesh.devices.reshape(n_dp, n_e // 4, 2, 2), names)
    expert = names[1:]
    return jax.shard_map(
        per_device,
        mesh=mesh,
        in_specs=(
            P("dp", None),
            P(),
            P("dp", None),
            P("dp", None),
            P(expert, None, "dp"),
            P(expert, None, "dp"),
            P(expert, "dp", None),
            P("dp", expert),
            P(expert, None),
            P("dp", None),
        ),
        out_specs=(P("dp", None), P("dp", None), P("dp", expert), P(expert, "dp")),
        check_vma=False,
    )
```

```python
import functools

import jax
import jax.numpy as jnp
from jax import lax
from jax.experimental import pallas as pl
from jax.experimental.pallas import tpu as pltpu
from jax.sharding import PartitionSpec as P

EPSILON = 1e-06
F32 = jnp.float32
BF16 = jnp.bfloat16
STEP = 256
LANES = 128
LOAD_PIECES = 8
FEW_ROWS = 64
VMEM_LIMIT = 12 * 1024 * 1024


def dot(a, b, dims):
    return lax.dot_general(a, b, (dims, ((), ())), preferred_element_type=F32)


def place(step, count):
    return pl.multiple_of(step * count, count)


def rows_of(refs, columns):
    return jnp.concatenate([ref[:, columns].astype(F32) for ref in refs], axis=0)


def own_columns(ids, i, j, width):
    return ((ids[1] ^ j) * 2 + (ids[2] ^ i)) * width


def store_blocks(out_ref, j, columns, value, count):
    rows = value.shape[0] // count
    for k in range(count):
        out_ref[k, j, :, columns] = value[k * rows : (k + 1) * rows].astype(BF16)


def load_kernel(n_dp, ids, w_gate, w_up, hid, grads, gain, named, weights, context, *refs):
    sources = (w_gate, w_up, hid, grads, gain)
    targets, small, named_held, weights_held, context_held, sems = (
        refs[:5], refs[5], refs[6], refs[7], refs[8], refs[9]
    )
    small_copies = [
        pltpu.make_async_copy(source, target, sems.at[n])
        for n, (source, target) in enumerate(
            ((named, named_held), (weights, weights_held), (context, context_held))
        )
    ]
    for copy in small_copies:
        copy.start()
    copies = []
    for source, target in zip(sources, targets):
        pieces = LOAD_PIECES if source.shape[0] % (LOAD_PIECES * 16) == 0 else 1
        part = source.shape[0] // pieces
        for p in range(pieces):
            block = pl.ds(p * part, part)
            where = (source.at[block], target.at[block]) if pieces > 1 else (source, target)
            copies.append(pltpu.make_async_copy(*where, sems.at[len(copies) + 3]))
    for copy in copies:
        copy.start()
    for copy in small_copies:
        copy.wait()
    rows = context_held.shape[0]
    row = jnp.sum(jnp.where(named_held[...] == ids[3], weights_held[...], 0.0), axis=0, keepdims=True)
    square = (rows, rows)
    diagonal = lax.broadcasted_iota(jnp.int32, square, 0) == lax.broadcasted_iota(jnp.int32, square, 1)
    gate = jnp.sum(jnp.where(diagonal, row, 0.0), axis=1, keepdims=True)
    heads = context_held.shape[1]
    small[:, :heads] = context_held[...].astype(F32)
    small[:, heads:] = jnp.broadcast_to(gate, (rows, LANES))
    for copy in copies:
        copy.wait()


def loop(count, body, unroll):
    if unroll:
        for step in range(count):
            body(step)
    else:
        def carried(step, carry):
            body(step)
            return carry

        lax.fori_loop(0, count, carried, 0)


def gates_of(smalls):
    return jnp.concatenate([small[:, small.shape[1] - LANES : small.shape[1] - LANES + 1] for small in smalls], axis=0)


def hidden_kernel(n_dp, ids, *refs):
    hid = refs[:n_dp]
    gain, w_gate, w_up, down_source, pre_gate, pre_up, act, w_down, normed, sem = refs[n_dp:]
    down_copy = pltpu.make_async_copy(down_source, w_down, sem)
    down_copy.start()
    total = hid[0].shape[0] * n_dp
    width = hid[0].shape[1]
    few = total <= FEW_ROWS
    sums = jnp.zeros((total, 1), F32)
    for step in range(width // 512):
        value = rows_of(hid, pl.ds(step * 512, 512))
        sums = sums + jnp.sum(value * value, axis=1, keepdims=True)
    scale = lax.rsqrt(sums / width + EPSILON)

    def norm(step):
        columns = pl.ds(place(step, 512), 512)
        normed[:, columns] = (rows_of(hid, columns) * scale * gain[:, columns]).astype(BF16)

    loop(width // 512, norm, few)

    def hidden_units(step):
        columns = pl.ds(place(step, STEP), STEP)
        gate_part = dot(normed[...], w_gate[:, columns], ((1,), (0,)))
        up_part = dot(normed[...], w_up[:, columns], ((1,), (0,)))
        pre_gate[:, columns] = gate_part
        pre_up[:, columns] = up_part
        act[:, columns] = (gate_part * jax.nn.sigmoid(gate_part) * up_part).astype(BF16)

    loop(w_gate.shape[1] // STEP, hidden_units, few)
    down_copy.wait()


def outward_kernel(n_dp, ids, *refs):
    smalls = refs[:n_dp]
    act, w_down, send, keep = refs[2 * n_dp :]
    weight = gates_of(smalls)
    chunk = send.shape[3]
    few = act.shape[0] <= FEW_ROWS
    for i, target in ((1, send), (0, keep)):
        for j in range(2):
            first = own_columns(ids, i, j, chunk)

            def outward(step):
                columns = pl.ds(pl.multiple_of(first + step * STEP, STEP), STEP)
                part = weight * dot(act[...], w_down[:, columns], ((1,), (0,)))
                store_blocks(target, j, pl.ds(place(step, STEP), STEP), part, n_dp)

            loop(chunk // STEP, outward, few)


def inward_part(ids, i, n_dp, grad_gate, grad_up, w_gate, w_up, target):
    chunk = target.shape[3]
    few = grad_gate.shape[0] <= FEW_ROWS
    for j in range(2):
        first = own_columns(ids, i, j, chunk)

        def inward(step):
            columns = pl.ds(pl.multiple_of(first + step * STEP, STEP), STEP)
            part = dot(grad_gate[...], w_gate[columns, :], ((1,), (1,)))
            part = part + dot(grad_up[...], w_up[columns, :], ((1,), (1,)))
            store_blocks(target, j, pl.ds(place(step, STEP), STEP), part, n_dp)

        loop(chunk // STEP, inward, few)


def backward_kernel(n_dp, ids, *refs):
    grads, smalls = refs[:n_dp], refs[n_dp : 2 * n_dp]
    pre_gate, pre_up, w_down, waiting, grad_gate, grad_up, passed, rows_grad = refs[2 * n_dp :]
    passed[...] = waiting[...]
    weight = gates_of(smalls)
    few = rows_grad.shape[0] <= FEW_ROWS

    def weigh(step):
        columns = pl.ds(place(step, 512), 512)
        rows_grad[:, columns] = (weight * rows_of(grads, columns)).astype(BF16)

    loop(rows_grad.shape[1] // 512, weigh, few)

    def hidden_units(step):
        columns = pl.ds(place(step, STEP), STEP)
        back = dot(rows_grad[...], w_down[columns, :], ((1,), (1,)))
        gate_part, up_part = pre_gate[:, columns], pre_up[:, columns]
        sig = jax.nn.sigmoid(gate_part)
        grad_gate[:, columns] = (back * up_part * sig * (1.0 + gate_part * (1.0 - sig))).astype(BF16)
        grad_up[:, columns] = (back * gate_part * sig).astype(BF16)

    loop(w_down.shape[0] // STEP, hidden_units, few)


def inward_kernel(i, n_dp, ids, grad_gate, grad_up, w_gate, w_up, waiting, target, passed):
    passed[...] = waiting[...]
    inward_part(ids, i, n_dp, grad_gate, grad_up, w_gate, w_up, target)


def finish_kernel(n_dp, ids, *refs):
    hid, grads, smalls = refs[:n_dp], refs[n_dp : 2 * n_dp], refs[2 * n_dp : 3 * n_dp]
    back, moe = refs[3 * n_dp : 7 * n_dp], refs[7 * n_dp : 7 * n_dp + 4]
    gain, w_out, output, d_hidden, d_context, d_w_out, summed, d_all = refs[7 * n_dp + 4 :]
    rows, width = hid[0].shape
    chunk = moe[0].shape[1]
    for i in range(2):
        for j in range(2):
            columns = pl.ds(pl.multiple_of(own_columns(ids, i, j, chunk), chunk), chunk)
            for k in range(n_dp):
                piece = back[(i * n_dp + k) * 2 + j]
                summed[k * rows : (k + 1) * rows, columns] = piece[...].astype(F32) * gain[:, columns]
            piece = moe[i * 2 + j]
            output[:, columns] = (hid[0][:, columns].astype(F32) + piece[...].astype(F32)).astype(BF16)

    few = rows * n_dp <= FEW_ROWS
    squares = jnp.zeros((rows * n_dp, 1), F32)
    products = squares
    for step in range(width // 512):
        columns = pl.ds(step * 512, 512)
        value = rows_of(hid, columns)
        squares = squares + jnp.sum(value * value, axis=1, keepdims=True)
        products = products + jnp.sum(value * summed[:, columns], axis=1, keepdims=True)
    scale = lax.rsqrt(squares / width + EPSILON)
    centre = scale * products / width

    def total(step):
        columns = pl.ds(place(step, 512), 512)
        unit_rows = rows_of(hid, columns) * scale
        value = rows_of(grads, columns) + scale * (summed[:, columns] - unit_rows * centre)
        d_all[:, columns] = value.astype(BF16)
        d_hidden[:, columns] = value[:rows].astype(BF16)

    loop(width // 512, total, few)
    d_context[...] = dot(d_hidden[...], w_out[...], ((1,), (1,))).astype(BF16)
    part = width // n_dp
    heads = d_context.shape[1]
    turned = jnp.concatenate([small[:, :heads] for small in smalls], axis=0).T.astype(BF16)
    step_width = min(part, 512)

    def product(step):
        columns = pl.ds(pl.multiple_of(ids[0] * part + step * step_width, step_width), step_width)
        d_w_out[:, pl.ds(place(step, step_width), step_width)] = dot(
            turned, d_all[:, columns], ((1,), (0,))
        ).astype(BF16)

    loop(part // step_width, product, few)


def run(kernel, n_dp, ids, operands, outs, scratch, cost, name, far=(), out_space=pltpu.VMEM):
    spaces = [pltpu.HBM if n in far else pltpu.VMEM for n in range(len(operands))]
    held = [pltpu.with_memory_space_constraint(value, space) for value, space in zip(operands, spaces)]
    kinds = [
        pltpu.VMEM(shape, kind) if out_space is pltpu.VMEM else jax.ShapeDtypeStruct(shape, kind)
        for shape, kind in outs
    ]
    return pl.pallas_call(
        functools.partial(kernel, n_dp),
        out_shape=kinds,
        in_specs=[pl.BlockSpec(memory_space=pltpu.SMEM)]
        + [pl.BlockSpec(memory_space=space) for space in spaces],
        out_specs=[pl.BlockSpec(memory_space=pltpu.VMEM)] * len(outs),
        scratch_shapes=scratch,
        compiler_params=pltpu.CompilerParams(vmem_limit_bytes=VMEM_LIMIT),
        cost_estimate=pl.CostEstimate(flops=0, bytes_accessed=cost, transcendentals=0),
        name=name,
    )(ids, *held)


def per_device(
    hidden_in, norm_gain, route_ids, route_gates, w_gate, w_up, w_down, context, w_out, grad_out
):
    n_dp, n_hi = lax.axis_size("dp"), lax.axis_size("hi")
    me, hi, y, c = (lax.axis_index(name) for name in ("dp", "hi", "y", "c"))
    rows, width = hidden_in.shape
    top, heads = route_ids.shape[1], context.shape[1]
    all_rows, units, chunk = n_dp * rows, w_gate.shape[2], width // 4
    expert = (hi * 2 + y) * 2 + c
    ids = jnp.stack([me, y, c, expert]).astype(jnp.int32)

    def swap(value, axes, turn):
        sizes = [lax.axis_size(name) for name in axes]
        count = 1
        for size in sizes:
            count *= size
        return lax.ppermute(value, axes, [(i, i ^ turn) for i in range(count)])

    def all_blocks(value, own=None):
        own = value if own is None else own
        return [own] + [swap(value, ("dp",), k) for k in range(1, n_dp)]

    weights = 2 * width * units
    shares = ((n_dp, 2, rows, chunk), BF16)
    wg, wu, hid_own, grads_own, gain, small_own = run(
        load_kernel, n_dp, ids,
        [w_gate[0], w_up[0], hidden_in, grad_out, norm_gain.reshape(1, width), route_ids.T, route_gates.T, context],
        [((width, units), BF16), ((width, units), BF16), ((rows, width), BF16), ((rows, width), BF16),
         ((1, width), F32), ((rows, heads + LANES), F32)],
        [pltpu.VMEM((top, rows), jnp.int32), pltpu.VMEM((top, rows), F32), pltpu.VMEM((rows, heads), BF16),
         pltpu.SemaphoreType.DMA((2 * LOAD_PIECES + 6,))],
        2 * weights, "load", far=range(8),
    )
    hid = all_blocks(hidden_in, hid_own)
    smalls = all_blocks(small_own)
    grads = all_blocks(grad_out, grads_own)

    def add(one, other):
        return (one.astype(F32) + other.astype(F32)).astype(BF16)

    def total_of(pieces):
        total = pieces[0].astype(F32)
        for piece in pieces[1:]:
            total = total + piece.astype(F32)
        return total.astype(BF16)

    pre_gate, pre_up, act, wd = run(
        hidden_kernel, n_dp, ids, hid + [gain, wg, wu, w_down[0]],
        [((all_rows, units), F32), ((all_rows, units), F32), ((all_rows, units), BF16), ((units, width), BF16)],
        [pltpu.VMEM((all_rows, width), BF16), pltpu.SemaphoreType.DMA], 2 * weights, "hidden", far=(n_dp + 3,),
    )
    out_send, out_keep = run(
        outward_kernel, n_dp, ids, smalls + grads + [act, wd], [shares, shares], [], weights, "outward"
    )
    out_other = swap(out_send, ("c",), 1)
    grad_gate, grad_up, out_keep = run(
        backward_kernel, n_dp, ids, grads + smalls + [pre_gate, pre_up, wd, out_keep],
        [((all_rows, units), BF16), ((all_rows, units), BF16), shares],
        [pltpu.VMEM((all_rows, width), BF16)], weights, "backward",
    )
    out_half = add(out_keep, out_other)
    out_blocks = [swap(out_half[k], ("dp",), k) for k in range(1, n_dp)]
    in_send, out_block = run(
        functools.partial(inward_kernel, 1), n_dp, ids, [grad_gate, grad_up, wg, wu, out_half[0]],
        [shares, (shares[0][1:], BF16)], [], weights, "inward_send",
    )
    in_other = swap(in_send, ("c",), 1)
    out_block = total_of([out_block] + out_blocks)
    out_other = swap(out_block[1], ("y",), 1)
    in_keep, out_share = run(
        functools.partial(inward_kernel, 0), n_dp, ids, [grad_gate, grad_up, wg, wu, out_block[0]],
        [shares, (shares[0][2:], BF16)], [], weights, "inward_keep",
    )
    out_total = add(out_share, out_other)
    in_half = add(in_keep, in_other)
    turns = [t for t in range(2 * n_dp - 1, 0, -1)]
    in_share = total_of([in_half[0, 0]] + [swap(in_half[t // 2, t % 2], ("dp", "y"), t) for t in turns])
    in_total = total_of([in_share] + [swap(in_share, ("hi",), t) for t in range(n_hi - 1, 0, -1)])
    turn = 1
    while turn < n_hi:
        out_total = add(out_total, swap(out_total, ("hi",), turn))
        turn = 2 * turn
    spread = {t: swap(in_total, ("dp", "y"), t) for t in turns}
    back = [in_total] + [spread[t] for t in range(1, 2 * n_dp)]
    moe = [out_total, swap(out_total, ("y",), 1)]
    back = back + [swap(piece, ("c",), 1) for piece in back]
    moe = moe + [swap(piece, ("c",), 1) for piece in moe]
    return run(
        finish_kernel, n_dp, ids, hid + grads + smalls + back + moe + [gain, w_out],
        [((rows, width), BF16), ((rows, width), BF16), ((rows, heads), BF16), ((heads, width // n_dp), BF16)],
        [pltpu.VMEM((all_rows, width), F32), pltpu.VMEM((all_rows, width), BF16)],
        weights, "finish", out_space=None,
    )


def solution(mesh):
    n_dp, n_e = mesh.shape["dp"], mesh.shape["expert"]
    names = ("dp", "hi", "y", "c")
    mesh = jax.sharding.Mesh(mesh.devices.reshape(n_dp, n_e // 4, 2, 2), names)
    expert = names[1:]
    return jax.shard_map(
        per_device,
        mesh=mesh,
        in_specs=(
            P("dp", None),
            P(),
            P("dp", None),
            P("dp", None),
            P(expert, None, "dp"),
            P(expert, None, "dp"),
            P(expert, "dp", None),
            P("dp", expert),
            P(expert, None),
            P("dp", None),
        ),
        out_specs=(P("dp", None), P("dp", None), P("dp", expert), P(expert, "dp")),
        check_vma=False,
    )
```

```python
import functools

import jax
import jax.numpy as jnp
from jax import lax
from jax.experimental import pallas as pl
from jax.experimental.pallas import tpu as pltpu
from jax.sharding import PartitionSpec as P

EPSILON = 1e-06
F32 = jnp.float32
BF16 = jnp.bfloat16
STEP = 256
LANES = 128
LOAD_PIECES = 8
FEW_ROWS = 64
VMEM_LIMIT = 12 * 1024 * 1024


def dot(a, b, dims):
    return lax.dot_general(a, b, (dims, ((), ())), preferred_element_type=F32)


def place(step, count):
    return pl.multiple_of(step * count, count)


def rows_of(refs, columns):
    return jnp.concatenate([ref[:, columns].astype(F32) for ref in refs], axis=0)


def store_blocks(place_of, columns, value, count):
    rows = value.shape[0] // count
    for k in range(count):
        ref, lead = place_of(k)
        ref[(*lead, slice(None), columns)] = value[k * rows : (k + 1) * rows].astype(BF16)


def load_kernel(n_dp, ids, w_gate, w_up, hid, grads, gain, named, weights, context, *refs):
    sources = (w_gate, w_up, hid, grads, gain)
    targets, small, named_held, weights_held, context_held, sems = (
        refs[:5], refs[5], refs[6], refs[7], refs[8], refs[9]
    )
    small_copies = [
        pltpu.make_async_copy(source, target, sems.at[n])
        for n, (source, target) in enumerate(
            ((named, named_held), (weights, weights_held), (context, context_held))
        )
    ]
    for copy in small_copies:
        copy.start()
    copies = []
    for source, target in zip(sources, targets):
        pieces = LOAD_PIECES if source.shape[0] % (LOAD_PIECES * 16) == 0 else 1
        part = source.shape[0] // pieces
        for p in range(pieces):
            block = pl.ds(p * part, part)
            where = (source.at[block], target.at[block]) if pieces > 1 else (source, target)
            copies.append(pltpu.make_async_copy(*where, sems.at[len(copies) + 3]))
    for copy in copies:
        copy.start()
    for copy in small_copies:
        copy.wait()
    rows = context_held.shape[0]
    row = jnp.sum(jnp.where(named_held[...] == ids[3], weights_held[...], 0.0), axis=0, keepdims=True)
    square = (rows, rows)
    diagonal = lax.broadcasted_iota(jnp.int32, square, 0) == lax.broadcasted_iota(jnp.int32, square, 1)
    gate = jnp.sum(jnp.where(diagonal, row, 0.0), axis=1, keepdims=True)
    heads = context_held.shape[1]
    small[:, :heads] = context_held[...].astype(F32)
    small[:, heads:] = jnp.broadcast_to(gate, (rows, LANES))
    for copy in copies:
        copy.wait()


def loop(count, body, unroll):
    if unroll:
        for step in range(count):
            body(step)
    else:
        def carried(step, carry):
            body(step)
            return carry

        lax.fori_loop(0, count, carried, 0)


def gates_of(smalls):
    return jnp.concatenate([small[:, small.shape[1] - LANES : small.shape[1] - LANES + 1] for small in smalls], axis=0)


def hidden_kernel(n_dp, ids, *refs):
    hid = refs[:n_dp]
    gain, w_gate, w_up, down_source, pre_gate, pre_up, act, w_down, normed, sem = refs[n_dp:]
    down_copy = pltpu.make_async_copy(down_source, w_down, sem)
    down_copy.start()
    total = hid[0].shape[0] * n_dp
    width = hid[0].shape[1]
    few = total <= FEW_ROWS
    sums = jnp.zeros((total, 1), F32)
    for step in range(width // 512):
        value = rows_of(hid, pl.ds(step * 512, 512))
        sums = sums + jnp.sum(value * value, axis=1, keepdims=True)
    scale = lax.rsqrt(sums / width + EPSILON)

    def norm(step):
        columns = pl.ds(place(step, 512), 512)
        normed[:, columns] = (rows_of(hid, columns) * scale * gain[:, columns]).astype(BF16)

    loop(width // 512, norm, few)

    def hidden_units(step):
        columns = pl.ds(place(step, STEP), STEP)
        gate_part = dot(normed[...], w_gate[:, columns], ((1,), (0,)))
        up_part = dot(normed[...], w_up[:, columns], ((1,), (0,)))
        pre_gate[:, columns] = gate_part
        pre_up[:, columns] = up_part
        act[:, columns] = (gate_part * jax.nn.sigmoid(gate_part) * up_part).astype(BF16)

    loop(w_gate.shape[1] // STEP, hidden_units, few)
    down_copy.wait()


def outward_kernel(n_dp, ids, *refs):
    smalls = refs[:n_dp]
    act, w_down, target = refs[2 * n_dp :]
    weight = gates_of(smalls)
    chunk = target.shape[3]
    few = act.shape[0] <= FEW_ROWS
    for j in range(2):
        first = (ids[1] ^ j) * chunk

        def outward(step):
            columns = pl.ds(pl.multiple_of(first + step * STEP, STEP), STEP)
            part = weight * dot(act[...], w_down[:, columns], ((1,), (0,)))
            store_blocks(lambda k: (target, (k, j)), pl.ds(place(step, STEP), STEP), part, n_dp)

        loop(chunk // STEP, outward, few)


def inward_last_kernel(n_dp, ids, grad_gate, grad_up, w_gate, w_up, waiting, earlier, target, passed):
    passed[...] = waiting[...]
    inward_kernel(0, n_dp, ids, grad_gate, grad_up, w_gate, w_up, target)


def inward_kernel(j, n_dp, ids, grad_gate, grad_up, w_gate, w_up, target):
    chunk = target.shape[2]
    few = grad_gate.shape[0] <= FEW_ROWS
    first = (ids[1] ^ j) * chunk

    def inward(step):
        columns = pl.ds(pl.multiple_of(first + step * STEP, STEP), STEP)
        part = dot(grad_gate[...], w_gate[columns, :], ((1,), (1,)))
        part = part + dot(grad_up[...], w_up[columns, :], ((1,), (1,)))
        store_blocks(lambda k: (target, (k,)), pl.ds(place(step, STEP), STEP), part, n_dp)

    loop(chunk // STEP, inward, few)


def backward_kernel(n_dp, ids, *refs):
    grads, smalls = refs[:n_dp], refs[n_dp : 2 * n_dp]
    pre_gate, pre_up, w_down, waiting, grad_gate, grad_up, passed, rows_grad = refs[2 * n_dp :]
    passed[...] = waiting[...]
    weight = gates_of(smalls)
    few = rows_grad.shape[0] <= FEW_ROWS

    def weigh(step):
        columns = pl.ds(place(step, 512), 512)
        rows_grad[:, columns] = (weight * rows_of(grads, columns)).astype(BF16)

    loop(rows_grad.shape[1] // 512, weigh, few)

    def hidden_units(step):
        columns = pl.ds(place(step, STEP), STEP)
        back = dot(rows_grad[...], w_down[columns, :], ((1,), (1,)))
        gate_part, up_part = pre_gate[:, columns], pre_up[:, columns]
        sig = jax.nn.sigmoid(gate_part)
        grad_gate[:, columns] = (back * up_part * sig * (1.0 + gate_part * (1.0 - sig))).astype(BF16)
        grad_up[:, columns] = (back * gate_part * sig).astype(BF16)

    loop(w_down.shape[0] // STEP, hidden_units, few)


def finish_kernel(n_dp, ids, *refs):
    hid, grads, smalls = refs[:n_dp], refs[n_dp : 2 * n_dp], refs[2 * n_dp : 3 * n_dp]
    back, moe = refs[3 * n_dp : 7 * n_dp], refs[7 * n_dp : 7 * n_dp + 4]
    gain, w_out, output, d_hidden, d_context, d_w_out, summed, d_all = refs[7 * n_dp + 4 :]
    rows, width = hid[0].shape
    chunk = moe[0].shape[1]
    first_core = ids[2] == 0
    for j in range(2):
        columns = pl.ds(pl.multiple_of((ids[1] ^ j) * chunk, chunk), chunk)
        for k in range(n_dp):
            here, there = back[k * 2 + j], back[(n_dp + k) * 2 + j]
            piece = jnp.where(first_core, here[...].astype(F32), there[...].astype(F32))
            summed[k * rows : (k + 1) * rows, columns] = piece * gain[:, columns]
        piece = jnp.where(first_core, moe[2 + j][...].astype(F32), moe[j][...].astype(F32))
        output[:, columns] = (hid[0][:, columns].astype(F32) + piece).astype(BF16)

    few = rows * n_dp <= FEW_ROWS
    squares = jnp.zeros((rows * n_dp, 1), F32)
    products = squares
    for step in range(width // 512):
        columns = pl.ds(step * 512, 512)
        value = rows_of(hid, columns)
        squares = squares + jnp.sum(value * value, axis=1, keepdims=True)
        products = products + jnp.sum(value * summed[:, columns], axis=1, keepdims=True)
    scale = lax.rsqrt(squares / width + EPSILON)
    centre = scale * products / width

    def total(step):
        columns = pl.ds(place(step, 512), 512)
        unit_rows = rows_of(hid, columns) * scale
        value = rows_of(grads, columns) + scale * (summed[:, columns] - unit_rows * centre)
        d_all[:, columns] = value.astype(BF16)
        d_hidden[:, columns] = value[:rows].astype(BF16)

    loop(width // 512, total, few)
    d_context[...] = dot(d_hidden[...], w_out[...], ((1,), (1,))).astype(BF16)
    part = width // n_dp
    heads = d_context.shape[1]
    turned = jnp.concatenate([small[:, :heads] for small in smalls], axis=0).T.astype(BF16)
    step_width = min(part, 512)

    def product(step):
        columns = pl.ds(pl.multiple_of(ids[0] * part + step * step_width, step_width), step_width)
        d_w_out[:, pl.ds(place(step, step_width), step_width)] = dot(
            turned, d_all[:, columns], ((1,), (0,))
        ).astype(BF16)

    loop(part // step_width, product, few)


def run(kernel, n_dp, ids, operands, outs, scratch, cost, name, far=(), out_space=pltpu.VMEM):
    spaces = [pltpu.HBM if n in far else pltpu.VMEM for n in range(len(operands))]
    held = [pltpu.with_memory_space_constraint(value, space) for value, space in zip(operands, spaces)]
    kinds = [
        pltpu.VMEM(shape, kind) if out_space is pltpu.VMEM else jax.ShapeDtypeStruct(shape, kind)
        for shape, kind in outs
    ]
    return pl.pallas_call(
        functools.partial(kernel, n_dp),
        out_shape=kinds,
        in_specs=[pl.BlockSpec(memory_space=pltpu.SMEM)]
        + [pl.BlockSpec(memory_space=space) for space in spaces],
        out_specs=[pl.BlockSpec(memory_space=pltpu.VMEM)] * len(outs),
        scratch_shapes=scratch,
        compiler_params=pltpu.CompilerParams(vmem_limit_bytes=VMEM_LIMIT),
        cost_estimate=pl.CostEstimate(flops=0, bytes_accessed=cost, transcendentals=0),
        name=name,
    )(ids, *held)


def per_device(
    hidden_in, norm_gain, route_ids, route_gates, w_gate, w_up, w_down, context, w_out, grad_out
):
    n_dp, n_hi = lax.axis_size("dp"), lax.axis_size("hi")
    me, hi, y, c = (lax.axis_index(name) for name in ("dp", "hi", "y", "c"))
    rows, width = hidden_in.shape
    top, heads = route_ids.shape[1], context.shape[1]
    all_rows, units, chunk = n_dp * rows, w_gate.shape[2], width // 2
    expert = (hi * 2 + y) * 2 + c
    ids = jnp.stack([me, y, c, expert]).astype(jnp.int32)

    def swap(value, axes, turn, core=None):
        count = 1
        for name in axes:
            count *= lax.axis_size(name)
        if core is None:
            return lax.ppermute(value, axes, [(i, i ^ turn) for i in range(count)])
        pairs = [(2 * i + core, 2 * (i ^ turn) + core) for i in range(count)]
        return lax.ppermute(value, axes + ("c",), pairs)

    def hand_over(value, core):
        return lax.ppermute(value, ("c",), [(core, 1 - core)])

    def all_blocks(value, own=None):
        own = value if own is None else own
        return [own] + [swap(value, ("dp",), k) for k in range(1, n_dp)]

    weights = 2 * width * units
    shares = ((n_dp, rows, chunk), BF16)
    wg, wu, hid_own, grads_own, gain, small_own = run(
        load_kernel, n_dp, ids,
        [w_gate[0], w_up[0], hidden_in, grad_out, norm_gain.reshape(1, width), route_ids.T, route_gates.T, context],
        [((width, units), BF16), ((width, units), BF16), ((rows, width), BF16), ((rows, width), BF16),
         ((1, width), F32), ((rows, heads + LANES), F32)],
        [pltpu.VMEM((top, rows), jnp.int32), pltpu.VMEM((top, rows), F32), pltpu.VMEM((rows, heads), BF16),
         pltpu.SemaphoreType.DMA((2 * LOAD_PIECES + 6,))],
        2 * weights, "load", far=range(8),
    )
    hid = all_blocks(hidden_in, hid_own)
    smalls = all_blocks(small_own)
    grads = all_blocks(grad_out, grads_own)

    def add(one, other):
        return (one.astype(F32) + other.astype(F32)).astype(BF16)

    def total_of(pieces):
        total = pieces[0].astype(F32)
        for piece in pieces[1:]:
            total = total + piece.astype(F32)
        return total.astype(BF16)

    pre_gate, pre_up, act, wd = run(
        hidden_kernel, n_dp, ids, hid + [gain, wg, wu, w_down[0]],
        [((all_rows, units), F32), ((all_rows, units), F32), ((all_rows, units), BF16), ((units, width), BF16)],
        [pltpu.VMEM((all_rows, width), BF16), pltpu.SemaphoreType.DMA], 2 * weights, "hidden", far=(n_dp + 3,),
    )
    (out_part,) = run(
        outward_kernel, n_dp, ids, smalls + grads + [act, wd], [((n_dp, 2, rows, chunk), BF16)], [],
        weights, "outward",
    )
    out_other = hand_over(out_part, 0)
    grad_gate, grad_up, out_part = run(
        backward_kernel, n_dp, ids, grads + smalls + [pre_gate, pre_up, wd, out_part],
        [((all_rows, units), BF16), ((all_rows, units), BF16), ((n_dp, 2, rows, chunk), BF16)],
        [pltpu.VMEM((all_rows, width), BF16)], weights, "backward",
    )
    (in_part,) = run(
        functools.partial(inward_kernel, 1), n_dp, ids, [grad_gate, grad_up, wg, wu], [shares], [],
        weights, "inward_first",
    )
    in_other = hand_over(in_part, 1)
    out_sum = add(out_part, out_other)
    last_part, in_part = run(
        inward_last_kernel, n_dp, ids, [grad_gate, grad_up, wg, wu, in_part, out_sum[0]], [shares, shares], [],
        weights, "inward_last",
    )
    in_sums = [add(last_part, hand_over(last_part, 1)), add(in_part, in_other)]
    turns = [t for t in range(2 * n_dp - 1, 0, -1)]
    in_share = total_of(
        [in_sums[0][0]] + [swap(in_sums[t % 2][t // 2], ("dp", "y"), t, 0) for t in turns]
    )
    in_total = total_of([in_share] + [swap(in_share, ("hi",), t, 0) for t in range(1, n_hi)])
    out_block = total_of([out_sum[0]] + [swap(out_sum[k], ("dp",), k, 1) for k in range(1, n_dp)])
    out_total = add(out_block[0], swap(out_block[1], ("y",), 1, 1))
    turn = 1
    while turn < n_hi:
        out_total = add(out_total, swap(out_total, ("hi",), turn, 1))
        turn = 2 * turn
    spread = {t: swap(in_total, ("dp", "y"), t, 0) for t in turns}
    back = [in_total] + [spread[t] for t in range(1, 2 * n_dp)]
    moe = [out_total, swap(out_total, ("y",), 1, 1)]
    back = back + [hand_over(piece, 0) for piece in back]
    moe = moe + [hand_over(piece, 1) for piece in moe]
    return run(
        finish_kernel, n_dp, ids, hid + grads + smalls + back + moe + [gain, w_out],
        [((rows, width), BF16), ((rows, width), BF16), ((rows, heads), BF16), ((heads, width // n_dp), BF16)],
        [pltpu.VMEM((all_rows, width), F32), pltpu.VMEM((all_rows, width), BF16)],
        weights, "finish", out_space=None,
    )


def solution(mesh):
    n_dp, n_e = mesh.shape["dp"], mesh.shape["expert"]
    names = ("dp", "hi", "y", "c")
    mesh = jax.sharding.Mesh(mesh.devices.reshape(n_dp, n_e // 4, 2, 2), names)
    expert = names[1:]
    return jax.shard_map(
        per_device,
        mesh=mesh,
        in_specs=(
            P("dp", None),
            P(),
            P("dp", None),
            P("dp", None),
            P(expert, None, "dp"),
            P(expert, None, "dp"),
            P(expert, "dp", None),
            P("dp", expert),
            P(expert, None),
            P("dp", None),
        ),
        out_specs=(P("dp", None), P("dp", None), P("dp", expert), P(expert, "dp")),
        check_vma=False,
    )
```

```python
import functools

import jax
import jax.numpy as jnp
from jax import lax
from jax.experimental import pallas as pl
from jax.experimental.pallas import tpu as pltpu
from jax.sharding import PartitionSpec as P

EPSILON = 1e-06
F32 = jnp.float32
BF16 = jnp.bfloat16
STEP = 256
LANES = 128
LOAD_PIECES = 8
FEW_ROWS = 64
VMEM_LIMIT = 12 * 1024 * 1024


def dot(a, b, dims):
    return lax.dot_general(a, b, (dims, ((), ())), preferred_element_type=F32)


def place(step, count):
    return pl.multiple_of(step * count, count)


def rows_of(refs, columns):
    return jnp.concatenate([ref[:, columns].astype(F32) for ref in refs], axis=0)


def own_columns(ids, i, j, width):
    return ((ids[1] ^ j) * 2 + (ids[2] ^ i)) * width


def store_blocks(out_ref, j, columns, value, count):
    rows = value.shape[0] // count
    for k in range(count):
        out_ref[k, j, :, columns] = value[k * rows : (k + 1) * rows].astype(BF16)


def gates_kernel(n_dp, ids, named, weights, context, w_gate, w_up, w_down, small, *held):
    targets, sems = held[:3], held[3]
    copies = [
        pltpu.make_async_copy(source, target, sems.at[n])
        for n, (source, target) in enumerate(zip((named, weights, context), targets))
    ]
    for copy in copies:
        copy.start()
    for copy in copies:
        copy.wait()
    named_held, weights_held, context_held = targets
    rows, heads = context_held.shape
    row = jnp.sum(jnp.where(named_held[...] == ids[3], weights_held[...], 0.0), axis=0, keepdims=True)
    square = (rows, rows)
    diagonal = lax.broadcasted_iota(jnp.int32, square, 0) == lax.broadcasted_iota(jnp.int32, square, 1)
    gate = jnp.sum(jnp.where(diagonal, row, 0.0), axis=1, keepdims=True)
    small[:, :heads] = context_held[...].astype(F32)
    small[:, heads:] = jnp.broadcast_to(gate, (rows, LANES))


def loop(count, body, unroll):
    if unroll:
        for step in range(count):
            body(step)
    else:
        def carried(step, carry):
            body(step)
            return carry

        lax.fori_loop(0, count, carried, 0)


def gates_of(smalls):
    return jnp.concatenate([small[:, small.shape[1] - LANES : small.shape[1] - LANES + 1] for small in smalls], axis=0)


def hidden_kernel(n_dp, ids, *refs):
    hid = refs[:n_dp]
    gain, w_gate, w_up, pre_gate, pre_up, act, normed = refs[n_dp:]
    total = hid[0].shape[0] * n_dp
    width = hid[0].shape[1]
    few = total <= FEW_ROWS
    sums = jnp.zeros((total, 1), F32)
    for step in range(width // 512):
        value = rows_of(hid, pl.ds(step * 512, 512))
        sums = sums + jnp.sum(value * value, axis=1, keepdims=True)
    scale = lax.rsqrt(sums / width + EPSILON)

    def norm(step):
        columns = pl.ds(place(step, 512), 512)
        normed[:, columns] = (rows_of(hid, columns) * scale * gain[:, columns]).astype(BF16)

    loop(width // 512, norm, few)

    def hidden_units(step):
        columns = pl.ds(place(step, STEP), STEP)
        gate_part = dot(normed[...], w_gate[:, columns], ((1,), (0,)))
        up_part = dot(normed[...], w_up[:, columns], ((1,), (0,)))
        pre_gate[:, columns] = gate_part
        pre_up[:, columns] = up_part
        act[:, columns] = (gate_part * jax.nn.sigmoid(gate_part) * up_part).astype(BF16)

    loop(w_gate.shape[1] // STEP, hidden_units, few)


def outward_kernel(i, n_dp, ids, *refs):
    smalls = refs[:n_dp]
    act, w_down, earlier, target = refs[2 * n_dp :]
    weight = gates_of(smalls)
    chunk = target.shape[3]
    few = act.shape[0] <= FEW_ROWS
    for j in range(2):
        first = own_columns(ids, i, j, chunk)

        def outward(step):
            columns = pl.ds(pl.multiple_of(first + step * STEP, STEP), STEP)
            part = weight * dot(act[...], w_down[:, columns], ((1,), (0,)))
            store_blocks(target, j, pl.ds(place(step, STEP), STEP), part, n_dp)

        loop(chunk // STEP, outward, few)


def inward_part(ids, i, n_dp, grad_gate, grad_up, w_gate, w_up, target):
    chunk = target.shape[3]
    few = grad_gate.shape[0] <= FEW_ROWS
    for j in range(2):
        first = own_columns(ids, i, j, chunk)

        def inward(step):
            columns = pl.ds(pl.multiple_of(first + step * STEP, STEP), STEP)
            part = dot(grad_gate[...], w_gate[columns, :], ((1,), (1,)))
            part = part + dot(grad_up[...], w_up[columns, :], ((1,), (1,)))
            store_blocks(target, j, pl.ds(place(step, STEP), STEP), part, n_dp)

        loop(chunk // STEP, inward, few)


def backward_kernel(n_dp, ids, *refs):
    grads, smalls = refs[:n_dp], refs[n_dp : 2 * n_dp]
    pre_gate, pre_up, w_down, waiting, grad_gate, grad_up, passed, rows_grad = refs[2 * n_dp :]
    passed[...] = waiting[...]
    weight = gates_of(smalls)
    few = rows_grad.shape[0] <= FEW_ROWS

    def weigh(step):
        columns = pl.ds(place(step, 512), 512)
        rows_grad[:, columns] = (weight * rows_of(grads, columns)).astype(BF16)

    loop(rows_grad.shape[1] // 512, weigh, few)

    def hidden_units(step):
        columns = pl.ds(place(step, STEP), STEP)
        back = dot(rows_grad[...], w_down[columns, :], ((1,), (1,)))
        gate_part, up_part = pre_gate[:, columns], pre_up[:, columns]
        sig = jax.nn.sigmoid(gate_part)
        grad_gate[:, columns] = (back * up_part * sig * (1.0 + gate_part * (1.0 - sig))).astype(BF16)
        grad_up[:, columns] = (back * gate_part * sig).astype(BF16)

    loop(w_down.shape[0] // STEP, hidden_units, few)


def inward_kernel(i, n_dp, ids, grad_gate, grad_up, w_gate, w_up, waiting, target, passed):
    passed[...] = waiting[...]
    inward_part(ids, i, n_dp, grad_gate, grad_up, w_gate, w_up, target)


def finish_kernel(n_dp, ids, *refs):
    hid, grads, smalls = refs[:n_dp], refs[n_dp : 2 * n_dp], refs[2 * n_dp : 3 * n_dp]
    back, moe = refs[3 * n_dp : 7 * n_dp], refs[7 * n_dp : 7 * n_dp + 4]
    gain, w_out, output, d_hidden, d_context, d_w_out, summed, d_all = refs[7 * n_dp + 4 :]
    rows, width = hid[0].shape
    chunk = moe[0].shape[1]
    for i in range(2):
        for j in range(2):
            columns = pl.ds(pl.multiple_of(own_columns(ids, i, j, chunk), chunk), chunk)
            for k in range(n_dp):
                piece = back[(i * n_dp + k) * 2 + j]
                summed[k * rows : (k + 1) * rows, columns] = piece[...].astype(F32) * gain[:, columns]
            piece = moe[i * 2 + j]
            output[:, columns] = (hid[0][:, columns].astype(F32) + piece[...].astype(F32)).astype(BF16)

    few = rows * n_dp <= FEW_ROWS
    squares = jnp.zeros((rows * n_dp, 1), F32)
    products = squares
    for step in range(width // 512):
        columns = pl.ds(step * 512, 512)
        value = rows_of(hid, columns)
        squares = squares + jnp.sum(value * value, axis=1, keepdims=True)
        products = products + jnp.sum(value * summed[:, columns], axis=1, keepdims=True)
    scale = lax.rsqrt(squares / width + EPSILON)
    centre = scale * products / width

    def total(step):
        columns = pl.ds(place(step, 512), 512)
        unit_rows = rows_of(hid, columns) * scale
        value = rows_of(grads, columns) + scale * (summed[:, columns] - unit_rows * centre)
        d_all[:, columns] = value.astype(BF16)
        d_hidden[:, columns] = value[:rows].astype(BF16)

    loop(width // 512, total, few)
    d_context[...] = dot(d_hidden[...], w_out[...], ((1,), (1,))).astype(BF16)
    part = width // n_dp
    heads = d_context.shape[1]
    turned = jnp.concatenate([small[:, :heads] for small in smalls], axis=0).T.astype(BF16)
    step_width = min(part, 512)

    def product(step):
        columns = pl.ds(pl.multiple_of(ids[0] * part + step * step_width, step_width), step_width)
        d_w_out[:, pl.ds(place(step, step_width), step_width)] = dot(
            turned, d_all[:, columns], ((1,), (0,))
        ).astype(BF16)

    loop(part // step_width, product, few)


def run(kernel, n_dp, ids, operands, outs, scratch, cost, name, far=(), out_space=pltpu.VMEM):
    spaces = [pltpu.HBM if n in far else pltpu.VMEM for n in range(len(operands))]
    held = [pltpu.with_memory_space_constraint(value, space) for value, space in zip(operands, spaces)]
    kinds = [
        pltpu.VMEM(shape, kind) if out_space is pltpu.VMEM else jax.ShapeDtypeStruct(shape, kind)
        for shape, kind in outs
    ]
    return pl.pallas_call(
        functools.partial(kernel, n_dp),
        out_shape=kinds,
        in_specs=[pl.BlockSpec(memory_space=pltpu.SMEM)]
        + [pl.BlockSpec(memory_space=space) for space in spaces],
        out_specs=[pl.BlockSpec(memory_space=pltpu.VMEM)] * len(outs),
        scratch_shapes=scratch,
        compiler_params=pltpu.CompilerParams(vmem_limit_bytes=VMEM_LIMIT),
        cost_estimate=pl.CostEstimate(flops=0, bytes_accessed=cost, transcendentals=0),
        name=name,
    )(ids, *held)


def per_device(
    hidden_in, norm_gain, route_ids, route_gates, w_gate, w_up, w_down, context, w_out, grad_out
):
    n_dp, n_hi = lax.axis_size("dp"), lax.axis_size("hi")
    me, hi, y, c = (lax.axis_index(name) for name in ("dp", "hi", "y", "c"))
    rows, width = hidden_in.shape
    top, heads = route_ids.shape[1], context.shape[1]
    all_rows, units, chunk = n_dp * rows, w_gate.shape[2], width // 4
    expert = (hi * 2 + y) * 2 + c
    ids = jnp.stack([me, y, c, expert]).astype(jnp.int32)

    def swap(value, axes, turn):
        sizes = [lax.axis_size(name) for name in axes]
        count = 1
        for size in sizes:
            count *= size
        return lax.ppermute(value, axes, [(i, i ^ turn) for i in range(count)])

    def all_blocks(value):
        return [value] + [swap(value, ("dp",), k) for k in range(1, n_dp)]

    weights = 2 * width * units
    shares = ((n_dp, 2, rows, chunk), BF16)
    wg, wu, wd, gain = w_gate[0], w_up[0], w_down[0], norm_gain.reshape(1, width)
    (small_own,) = run(
        gates_kernel, n_dp, ids, [route_ids.T, route_gates.T, context, wg, wu, wd],
        [((rows, heads + LANES), F32)],
        [pltpu.VMEM((top, rows), jnp.int32), pltpu.VMEM((top, rows), F32), pltpu.VMEM((rows, heads), BF16),
         pltpu.SemaphoreType.DMA((3,))],
        4 * weights, "gates", far=range(6),
    )
    hid = all_blocks(hidden_in)
    smalls = all_blocks(small_own)
    grads = all_blocks(grad_out)

    def add(one, other):
        return (one.astype(F32) + other.astype(F32)).astype(BF16)

    def total_of(pieces):
        total = pieces[0].astype(F32)
        for piece in pieces[1:]:
            total = total + piece.astype(F32)
        return total.astype(BF16)

    pre_gate, pre_up, act = run(
        hidden_kernel, n_dp, ids, hid + [gain, wg, wu],
        [((all_rows, units), F32), ((all_rows, units), F32), ((all_rows, units), BF16)],
        [pltpu.VMEM((all_rows, width), BF16)], 2 * weights, "hidden",
    )
    (out_send,) = run(
        functools.partial(outward_kernel, 1), n_dp, ids, smalls + grads + [act, wd, act], [shares], [],
        weights // 2, "outward_send",
    )
    out_other = swap(out_send, ("c",), 1)
    (out_keep,) = run(
        functools.partial(outward_kernel, 0), n_dp, ids, smalls + grads + [act, wd, out_send], [shares], [],
        weights // 2, "outward_keep",
    )
    out_half = add(out_keep, out_other)
    out_blocks = [swap(out_half[k], ("dp",), k) for k in range(1, n_dp)]
    block = (shares[0][1:], BF16)
    grad_gate, grad_up, out_block = run(
        backward_kernel, n_dp, ids, grads + smalls + [pre_gate, pre_up, wd, out_half[0]],
        [((all_rows, units), BF16), ((all_rows, units), BF16), block],
        [pltpu.VMEM((all_rows, width), BF16)], weights, "backward",
    )
    in_send, out_block = run(
        functools.partial(inward_kernel, 1), n_dp, ids, [grad_gate, grad_up, wg, wu, out_block],
        [shares, block], [], weights, "inward_send",
    )
    in_other = swap(in_send, ("c",), 1)
    out_block = total_of([out_block] + out_blocks)
    out_other = swap(out_block[1], ("y",), 1)
    in_keep, out_share = run(
        functools.partial(inward_kernel, 0), n_dp, ids, [grad_gate, grad_up, wg, wu, out_block[0]],
        [shares, (shares[0][2:], BF16)], [], weights, "inward_keep",
    )
    out_total = add(out_share, out_other)
    in_half = add(in_keep, in_other)
    turns = [t for t in range(2 * n_dp - 1, 0, -1)]
    in_share = total_of([in_half[0, 0]] + [swap(in_half[t // 2, t % 2], ("dp", "y"), t) for t in turns])
    in_total = total_of([in_share] + [swap(in_share, ("hi",), t) for t in range(n_hi - 1, 0, -1)])
    turn = 1
    while turn < n_hi:
        out_total = add(out_total, swap(out_total, ("hi",), turn))
        turn = 2 * turn
    spread = {t: swap(in_total, ("dp", "y"), t) for t in turns}
    back = [in_total] + [spread[t] for t in range(1, 2 * n_dp)]
    moe = [out_total, swap(out_total, ("y",), 1)]
    back = back + [swap(piece, ("c",), 1) for piece in back]
    moe = moe + [swap(piece, ("c",), 1) for piece in moe]
    return run(
        finish_kernel, n_dp, ids, hid + grads + smalls + back + moe + [gain, w_out],
        [((rows, width), BF16), ((rows, width), BF16), ((rows, heads), BF16), ((heads, width // n_dp), BF16)],
        [pltpu.VMEM((all_rows, width), F32), pltpu.VMEM((all_rows, width), BF16)],
        weights, "finish", out_space=None,
    )


def solution(mesh):
    n_dp, n_e = mesh.shape["dp"], mesh.shape["expert"]
    names = ("dp", "hi", "y", "c")
    mesh = jax.sharding.Mesh(mesh.devices.reshape(n_dp, n_e // 4, 2, 2), names)
    expert = names[1:]
    return jax.shard_map(
        per_device,
        mesh=mesh,
        in_specs=(
            P("dp", None),
            P(),
            P("dp", None),
            P("dp", None),
            P(expert, None, "dp"),
            P(expert, None, "dp"),
            P(expert, "dp", None),
            P("dp", expert),
            P(expert, None),
            P("dp", None),
        ),
        out_specs=(P("dp", None), P("dp", None), P("dp", expert), P(expert, "dp")),
        check_vma=False,
    )
```

```python
import functools

import jax
import jax.numpy as jnp
from jax import lax
from jax.experimental import pallas as pl
from jax.experimental.pallas import tpu as pltpu
from jax.sharding import PartitionSpec as P

EPSILON = 1e-06
F32 = jnp.float32
BF16 = jnp.bfloat16
STEP = 256
LANES = 128
LOAD_PIECES = 8
FEW_ROWS = 64
VMEM_LIMIT = 12 * 1024 * 1024


def dot(a, b, dims):
    return lax.dot_general(a, b, (dims, ((), ())), preferred_element_type=F32)


def place(step, count):
    return pl.multiple_of(step * count, count)


def rows_of(refs, columns):
    return jnp.concatenate([ref[:, columns].astype(F32) for ref in refs], axis=0)


def own_columns(i, j, width):
    return ((lax.axis_index("y") ^ j) * 2 + (lax.axis_index("c") ^ i)) * width


def store_blocks(out_ref, j, columns, value, count):
    rows = value.shape[0] // count
    for k in range(count):
        out_ref[k, j, :, columns] = value[k * rows : (k + 1) * rows].astype(BF16)


def gates_kernel(n_dp, named, weights, context, w_gate, w_up, w_down, small, *held):
    targets, sems = held[:3], held[3]
    copies = [
        pltpu.make_async_copy(source, target, sems.at[n])
        for n, (source, target) in enumerate(zip((named, weights, context), targets))
    ]
    for copy in copies:
        copy.start()
    for copy in copies:
        copy.wait()
    named_held, weights_held, context_held = targets
    rows, heads = context_held.shape
    expert = (lax.axis_index("hi") * 2 + lax.axis_index("y")) * 2 + lax.axis_index("c")
    row = jnp.sum(jnp.where(named_held[...] == expert, weights_held[...], 0.0), axis=0, keepdims=True)
    square = (rows, rows)
    diagonal = lax.broadcasted_iota(jnp.int32, square, 0) == lax.broadcasted_iota(jnp.int32, square, 1)
    gate = jnp.sum(jnp.where(diagonal, row, 0.0), axis=1, keepdims=True)
    small[:, :heads] = context_held[...].astype(F32)
    small[:, heads:] = jnp.broadcast_to(gate, (rows, LANES))


def loop(count, body, unroll):
    if unroll:
        for step in range(count):
            body(step)
    else:
        def carried(step, carry):
            body(step)
            return carry

        lax.fori_loop(0, count, carried, 0)


def gates_of(smalls):
    return jnp.concatenate([small[:, small.shape[1] - LANES : small.shape[1] - LANES + 1] for small in smalls], axis=0)


def hidden_kernel(n_dp, *refs):
    hid = refs[:n_dp]
    gain, w_gate, w_up, pre_gate, pre_up, act, normed = refs[n_dp:]
    total = hid[0].shape[0] * n_dp
    width = hid[0].shape[1]
    few = total <= FEW_ROWS
    sums = jnp.zeros((total, 1), F32)
    for step in range(width // 512):
        value = rows_of(hid, pl.ds(step * 512, 512))
        sums = sums + jnp.sum(value * value, axis=1, keepdims=True)
    scale = lax.rsqrt(sums / width + EPSILON)

    def norm(step):
        columns = pl.ds(place(step, 512), 512)
        normed[:, columns] = (rows_of(hid, columns) * scale * gain[:, columns]).astype(BF16)

    loop(width // 512, norm, few)

    def hidden_units(step):
        columns = pl.ds(place(step, STEP), STEP)
        gate_part = dot(normed[...], w_gate[:, columns], ((1,), (0,)))
        up_part = dot(normed[...], w_up[:, columns], ((1,), (0,)))
        pre_gate[:, columns] = gate_part
        pre_up[:, columns] = up_part
        act[:, columns] = (gate_part * jax.nn.sigmoid(gate_part) * up_part).astype(BF16)

    loop(w_gate.shape[1] // STEP, hidden_units, few)


def outward_kernel(i, n_dp, *refs):
    smalls = refs[:n_dp]
    act, w_down, *_, target = refs[n_dp:]
    weight = gates_of(smalls)
    chunk = target.shape[3]
    few = act.shape[0] <= FEW_ROWS
    for j in range(2):
        first = own_columns(i, j, chunk)

        def outward(step):
            columns = pl.ds(pl.multiple_of(first + step * STEP, STEP), STEP)
            part = weight * dot(act[...], w_down[:, columns], ((1,), (0,)))
            store_blocks(target, j, pl.ds(place(step, STEP), STEP), part, n_dp)

        loop(chunk // STEP, outward, few)


def inward_part(i, n_dp, grad_gate, grad_up, w_gate, w_up, target):
    chunk = target.shape[3]
    few = grad_gate.shape[0] <= FEW_ROWS
    for j in range(2):
        first = own_columns(i, j, chunk)

        def inward(step):
            columns = pl.ds(pl.multiple_of(first + step * STEP, STEP), STEP)
            part = dot(grad_gate[...], w_gate[columns, :], ((1,), (1,)))
            part = part + dot(grad_up[...], w_up[columns, :], ((1,), (1,)))
            store_blocks(target, j, pl.ds(place(step, STEP), STEP), part, n_dp)

        loop(chunk // STEP, inward, few)


def backward_kernel(n_dp, *refs):
    grads, smalls = refs[:n_dp], refs[n_dp : 2 * n_dp]
    pre_gate, pre_up, w_down, waiting, grad_gate, grad_up, passed, rows_grad = refs[2 * n_dp :]
    passed[...] = waiting[...]
    weight = gates_of(smalls)
    few = rows_grad.shape[0] <= FEW_ROWS

    def weigh(step):
        columns = pl.ds(place(step, 512), 512)
        rows_grad[:, columns] = (weight * rows_of(grads, columns)).astype(BF16)

    loop(rows_grad.shape[1] // 512, weigh, few)

    def hidden_units(step):
        columns = pl.ds(place(step, STEP), STEP)
        back = dot(rows_grad[...], w_down[columns, :], ((1,), (1,)))
        gate_part, up_part = pre_gate[:, columns], pre_up[:, columns]
        sig = jax.nn.sigmoid(gate_part)
        grad_gate[:, columns] = (back * up_part * sig * (1.0 + gate_part * (1.0 - sig))).astype(BF16)
        grad_up[:, columns] = (back * gate_part * sig).astype(BF16)

    loop(w_down.shape[0] // STEP, hidden_units, few)


def inward_kernel(i, n_dp, grad_gate, grad_up, w_gate, w_up, waiting, target, passed):
    passed[...] = waiting[...]
    inward_part(i, n_dp, grad_gate, grad_up, w_gate, w_up, target)


def finish_kernel(n_dp, *refs):
    hid, grads, smalls = refs[:n_dp], refs[n_dp : 2 * n_dp], refs[2 * n_dp : 3 * n_dp]
    back, moe = refs[3 * n_dp : 7 * n_dp], refs[7 * n_dp : 7 * n_dp + 4]
    gain, w_out = refs[7 * n_dp + 4 : 7 * n_dp + 6]
    targets, held = refs[7 * n_dp + 6 : 7 * n_dp + 10], refs[7 * n_dp + 10 : 7 * n_dp + 14]
    summed, d_all, sems = refs[7 * n_dp + 14 :]
    output, d_hidden, d_context, d_w_out = held
    copies = [pltpu.make_async_copy(held[n], targets[n], sems.at[n]) for n in range(4)]
    rows, width = hid[0].shape
    chunk = moe[0].shape[1]
    for i in range(2):
        for j in range(2):
            columns = pl.ds(pl.multiple_of(own_columns(i, j, chunk), chunk), chunk)
            for k in range(n_dp):
                piece = back[(i * n_dp + k) * 2 + j]
                summed[k * rows : (k + 1) * rows, columns] = piece[...].astype(F32) * gain[:, columns]
            piece = moe[i * 2 + j]
            output[:, columns] = (hid[0][:, columns].astype(F32) + piece[...].astype(F32)).astype(BF16)
    copies[0].start()

    few = rows * n_dp <= FEW_ROWS
    squares = jnp.zeros((rows * n_dp, 1), F32)
    products = squares
    for step in range(width // 512):
        columns = pl.ds(step * 512, 512)
        value = rows_of(hid, columns)
        squares = squares + jnp.sum(value * value, axis=1, keepdims=True)
        products = products + jnp.sum(value * summed[:, columns], axis=1, keepdims=True)
    scale = lax.rsqrt(squares / width + EPSILON)
    centre = scale * products / width

    def total(step):
        columns = pl.ds(place(step, 512), 512)
        unit_rows = rows_of(hid, columns) * scale
        value = rows_of(grads, columns) + scale * (summed[:, columns] - unit_rows * centre)
        d_all[:, columns] = value.astype(BF16)
        d_hidden[:, columns] = value[:rows].astype(BF16)

    loop(width // 512, total, few)
    copies[1].start()
    d_context[...] = dot(d_hidden[...], w_out[...], ((1,), (1,))).astype(BF16)
    part = width // n_dp
    copies[2].start()
    heads = d_context.shape[1]
    turned = jnp.concatenate([small[:, :heads] for small in smalls], axis=0).T.astype(BF16)
    step_width = min(part, 512)

    def product(step):
        columns = pl.ds(pl.multiple_of(lax.axis_index("dp") * part + step * step_width, step_width), step_width)
        d_w_out[:, pl.ds(place(step, step_width), step_width)] = dot(
            turned, d_all[:, columns], ((1,), (0,))
        ).astype(BF16)

    loop(part // step_width, product, few)
    copies[3].start()
    for copy in copies:
        copy.wait()


def run(kernel, n_dp, operands, outs, scratch, cost, name, far=(), out_space=pltpu.VMEM):
    spaces = [pltpu.HBM if n in far else pltpu.VMEM for n in range(len(operands))]
    held = [pltpu.with_memory_space_constraint(value, space) for value, space in zip(operands, spaces)]
    kinds = [out_space(shape, kind) for shape, kind in outs]
    return pl.pallas_call(
        functools.partial(kernel, n_dp),
        out_shape=kinds,
        in_specs=[pl.BlockSpec(memory_space=space) for space in spaces],
        out_specs=[pl.BlockSpec(memory_space=out_space)] * len(outs),
        scratch_shapes=scratch,
        compiler_params=pltpu.CompilerParams(vmem_limit_bytes=VMEM_LIMIT),
        cost_estimate=pl.CostEstimate(flops=0, bytes_accessed=cost, transcendentals=0),
        name=name,
    )(*held)


def per_device(
    hidden_in, norm_gain, route_ids, route_gates, w_gate, w_up, w_down, context, w_out, grad_out
):
    n_dp, n_hi = lax.axis_size("dp"), lax.axis_size("hi")
    rows, width = hidden_in.shape
    top, heads = route_ids.shape[1], context.shape[1]
    all_rows, units, chunk = n_dp * rows, w_gate.shape[2], width // 4

    def swap(value, axes, turn):
        sizes = [lax.axis_size(name) for name in axes]
        count = 1
        for size in sizes:
            count *= size
        return lax.ppermute(value, axes, [(i, i ^ turn) for i in range(count)])

    def all_blocks(value):
        return [value] + [swap(value, ("dp",), k) for k in range(1, n_dp)]

    weights = 2 * width * units
    shares = ((n_dp, 2, rows, chunk), BF16)
    wg, wu, wd, gain = w_gate[0], w_up[0], w_down[0], norm_gain.reshape(1, width)
    (small_own,) = run(
        gates_kernel, n_dp, [route_ids.T, route_gates.T, context, wg, wu, wd],
        [((rows, heads + LANES), F32)],
        [pltpu.VMEM((top, rows), jnp.int32), pltpu.VMEM((top, rows), F32), pltpu.VMEM((rows, heads), BF16),
         pltpu.SemaphoreType.DMA((3,))],
        4 * weights, "gates", far=range(6),
    )
    hid = all_blocks(hidden_in)
    smalls = all_blocks(small_own)
    grads = all_blocks(grad_out)

    def add(one, other):
        return (one.astype(F32) + other.astype(F32)).astype(BF16)

    def total_of(pieces):
        total = pieces[0].astype(F32)
        for piece in pieces[1:]:
            total = total + piece.astype(F32)
        return total.astype(BF16)

    pre_gate, pre_up, act = run(
        hidden_kernel, n_dp, hid + [gain, wg, wu],
        [((all_rows, units), F32), ((all_rows, units), F32), ((all_rows, units), BF16)],
        [pltpu.VMEM((all_rows, width), BF16)], 2 * weights, "hidden",
    )
    (out_send,) = run(
        functools.partial(outward_kernel, 1), n_dp, smalls + [act, wd], [shares], [],
        weights // 2, "outward_send",
    )
    out_other = swap(out_send, ("c",), 1)
    (out_keep,) = run(
        functools.partial(outward_kernel, 0), n_dp, smalls + [act, wd, out_send] + grads, [shares], [],
        weights // 2, "outward_keep",
    )
    out_half = add(out_keep, out_other)
    out_blocks = [swap(out_half[k], ("dp",), k) for k in range(1, n_dp)]
    block = (shares[0][1:], BF16)
    grad_gate, grad_up, out_block = run(
        backward_kernel, n_dp, grads + smalls + [pre_gate, pre_up, wd, out_half[0]],
        [((all_rows, units), BF16), ((all_rows, units), BF16), block],
        [pltpu.VMEM((all_rows, width), BF16)], weights, "backward",
    )
    in_send, out_block = run(
        functools.partial(inward_kernel, 1), n_dp, [grad_gate, grad_up, wg, wu, out_block],
        [shares, block], [], weights, "inward_send",
    )
    in_other = swap(in_send, ("c",), 1)
    out_block = total_of([out_block] + out_blocks)
    out_other = swap(out_block[1], ("y",), 1)
    in_keep, out_share = run(
        functools.partial(inward_kernel, 0), n_dp, [grad_gate, grad_up, wg, wu, out_block[0]],
        [shares, (shares[0][2:], BF16)], [], weights, "inward_keep",
    )
    out_total = add(out_share, out_other)
    in_half = add(in_keep, in_other)
    turns = [t for t in range(2 * n_dp - 1, 0, -1)]
    in_share = total_of([in_half[0, 0]] + [swap(in_half[t // 2, t % 2], ("dp", "y"), t) for t in turns])
    in_total = total_of([in_share] + [swap(in_share, ("hi",), t) for t in range(1, n_hi)])
    turn = 1
    while turn < n_hi:
        out_total = add(out_total, swap(out_total, ("hi",), turn))
        turn = 2 * turn
    order = [t for t in turns if t < 2] + [t for t in turns if t >= 2]
    spread = {t: swap(in_total, ("dp", "y"), t) for t in order}
    back = [in_total] + [spread[t] for t in range(1, 2 * n_dp)]
    moe = [out_total, swap(out_total, ("y",), 1)]
    back = back + [swap(piece, ("c",), 1) for piece in back]
    moe = moe + [swap(piece, ("c",), 1) for piece in moe]
    outs = [((rows, width), BF16), ((rows, width), BF16), ((rows, heads), BF16), ((heads, width // n_dp), BF16)]
    return run(
        finish_kernel, n_dp, hid + grads + smalls + back + moe + [gain, w_out], outs,
        [pltpu.VMEM(*out) for out in outs]
        + [pltpu.VMEM((all_rows, width), F32), pltpu.VMEM((all_rows, width), BF16), pltpu.SemaphoreType.DMA((4,))],
        weights, "finish", out_space=pltpu.HBM,
    )


def solution(mesh):
    n_dp, n_e = mesh.shape["dp"], mesh.shape["expert"]
    names = ("dp", "hi", "y", "c")
    mesh = jax.sharding.Mesh(mesh.devices.reshape(n_dp, n_e // 4, 2, 2), names)
    expert = names[1:]
    return jax.shard_map(
        per_device,
        mesh=mesh,
        in_specs=(
            P("dp", None),
            P(),
            P("dp", None),
            P("dp", None),
            P(expert, None, "dp"),
            P(expert, None, "dp"),
            P(expert, "dp", None),
            P("dp", expert),
            P(expert, None),
            P("dp", None),
        ),
        out_specs=(P("dp", None), P("dp", None), P("dp", expert), P(expert, "dp")),
        check_vma=False,
    )
```

```python
import functools

import jax
import jax.numpy as jnp
from jax import lax
from jax.experimental import pallas as pl
from jax.experimental.pallas import tpu as pltpu
from jax.sharding import PartitionSpec as P

EPSILON = 1e-06
F32 = jnp.float32
BF16 = jnp.bfloat16
STEP = 256
LANES = 128
LOAD_PIECES = 8
FEW_ROWS = 64
VMEM_LIMIT = 12 * 1024 * 1024


def dot(a, b, dims):
    return lax.dot_general(a, b, (dims, ((), ())), preferred_element_type=F32)


def place(step, count):
    return pl.multiple_of(step * count, count)


def rows_of(refs, columns):
    return jnp.concatenate([ref[:, columns].astype(F32) for ref in refs], axis=0)


def own_columns(i, j, width):
    return ((lax.axis_index("y") ^ j) * 2 + (lax.axis_index("c") ^ i)) * width


def store_blocks(out_ref, j, columns, value, count):
    rows = value.shape[0] // count
    for k in range(count):
        out_ref[k, j, :, columns] = value[k * rows : (k + 1) * rows].astype(BF16)


def gates_kernel(n_dp, named, weights, context, w_gate, w_up, w_down, small, *held):
    targets, sems = held[:3], held[3]
    copies = [
        pltpu.make_async_copy(source, target, sems.at[n])
        for n, (source, target) in enumerate(zip((named, weights, context), targets))
    ]
    for copy in copies:
        copy.start()
    for copy in copies:
        copy.wait()
    named_held, weights_held, context_held = targets
    rows, heads = context_held.shape
    expert = (lax.axis_index("hi") * 2 + lax.axis_index("y")) * 2 + lax.axis_index("c")
    row = jnp.sum(jnp.where(named_held[...] == expert, weights_held[...], 0.0), axis=0, keepdims=True)
    square = (rows, rows)
    diagonal = lax.broadcasted_iota(jnp.int32, square, 0) == lax.broadcasted_iota(jnp.int32, square, 1)
    gate = jnp.sum(jnp.where(diagonal, row, 0.0), axis=1, keepdims=True)
    small[:, :heads] = context_held[...].astype(F32)
    small[:, heads:] = jnp.broadcast_to(gate, (rows, LANES))


def loop(count, body, unroll):
    if unroll:
        for step in range(count):
            body(step)
    else:
        def carried(step, carry):
            body(step)
            return carry

        lax.fori_loop(0, count, carried, 0)


def gates_of(smalls):
    return jnp.concatenate([small[:, small.shape[1] - LANES : small.shape[1] - LANES + 1] for small in smalls], axis=0)


def hidden_kernel(n_dp, *refs):
    hid = refs[:n_dp]
    gain, w_gate, w_up, pre_gate, pre_up, act, normed = refs[n_dp:]
    total = hid[0].shape[0] * n_dp
    width = hid[0].shape[1]
    few = total <= FEW_ROWS
    sums = jnp.zeros((total, 1), F32)
    for step in range(width // 512):
        value = rows_of(hid, pl.ds(step * 512, 512))
        sums = sums + jnp.sum(value * value, axis=1, keepdims=True)
    scale = lax.rsqrt(sums / width + EPSILON)

    def norm(step):
        columns = pl.ds(place(step, 512), 512)
        normed[:, columns] = (rows_of(hid, columns) * scale * gain[:, columns]).astype(BF16)

    loop(width // 512, norm, few)

    def hidden_units(step):
        columns = pl.ds(place(step, STEP), STEP)
        gate_part = dot(normed[...], w_gate[:, columns], ((1,), (0,)))
        up_part = dot(normed[...], w_up[:, columns], ((1,), (0,)))
        pre_gate[:, columns] = gate_part
        pre_up[:, columns] = up_part
        act[:, columns] = (gate_part * jax.nn.sigmoid(gate_part) * up_part).astype(BF16)

    loop(w_gate.shape[1] // STEP, hidden_units, few)


def outward_kernel(i, n_dp, *refs):
    smalls = refs[:n_dp]
    act, w_down, *_, target = refs[n_dp:]
    weight = gates_of(smalls)
    chunk = target.shape[3]
    few = act.shape[0] <= FEW_ROWS
    for j in range(2):
        first = own_columns(i, j, chunk)

        def outward(step):
            columns = pl.ds(pl.multiple_of(first + step * STEP, STEP), STEP)
            part = weight * dot(act[...], w_down[:, columns], ((1,), (0,)))
            store_blocks(target, j, pl.ds(place(step, STEP), STEP), part, n_dp)

        loop(chunk // STEP, outward, few)


def inward_part(i, n_dp, grad_gate, grad_up, w_gate, w_up, target):
    chunk = target.shape[3]
    few = grad_gate.shape[0] <= FEW_ROWS
    for j in range(2):
        first = own_columns(i, j, chunk)

        def inward(step):
            columns = pl.ds(pl.multiple_of(first + step * STEP, STEP), STEP)
            part = dot(grad_gate[...], w_gate[columns, :], ((1,), (1,)))
            part = part + dot(grad_up[...], w_up[columns, :], ((1,), (1,)))
            store_blocks(target, j, pl.ds(place(step, STEP), STEP), part, n_dp)

        loop(chunk // STEP, inward, few)


def backward_kernel(n_dp, *refs):
    grads, smalls = refs[:n_dp], refs[n_dp : 2 * n_dp]
    pre_gate, pre_up, w_down, waiting, grad_gate, grad_up, passed, rows_grad = refs[2 * n_dp :]
    passed[...] = waiting[...]
    weight = gates_of(smalls)
    few = rows_grad.shape[0] <= FEW_ROWS

    def weigh(step):
        columns = pl.ds(place(step, 512), 512)
        rows_grad[:, columns] = (weight * rows_of(grads, columns)).astype(BF16)

    loop(rows_grad.shape[1] // 512, weigh, few)

    def hidden_units(step):
        columns = pl.ds(place(step, STEP), STEP)
        back = dot(rows_grad[...], w_down[columns, :], ((1,), (1,)))
        gate_part, up_part = pre_gate[:, columns], pre_up[:, columns]
        sig = jax.nn.sigmoid(gate_part)
        grad_gate[:, columns] = (back * up_part * sig * (1.0 + gate_part * (1.0 - sig))).astype(BF16)
        grad_up[:, columns] = (back * gate_part * sig).astype(BF16)

    loop(w_down.shape[0] // STEP, hidden_units, few)


def inward_kernel(i, n_dp, grad_gate, grad_up, w_gate, w_up, waiting, target, passed):
    passed[...] = waiting[...]
    inward_part(i, n_dp, grad_gate, grad_up, w_gate, w_up, target)


def join_kernel(n_dp, in_keep, in_other, out_block, *refs):
    for t in range(2 * n_dp):
        k, j = t // 2, t % 2
        refs[t][...] = (in_keep[k, j].astype(F32) + in_other[k, j].astype(F32)).astype(BF16)
    for j, target in enumerate(refs[-2:]):
        target[...] = out_block[j]


def finish_kernel(n_dp, *refs):
    hid, grads, smalls = refs[:n_dp], refs[n_dp : 2 * n_dp], refs[2 * n_dp : 3 * n_dp]
    back, moe = refs[3 * n_dp : 7 * n_dp], refs[7 * n_dp : 7 * n_dp + 4]
    gain, w_out = refs[7 * n_dp + 4 : 7 * n_dp + 6]
    targets, held = refs[7 * n_dp + 6 : 7 * n_dp + 10], refs[7 * n_dp + 10 : 7 * n_dp + 14]
    summed, d_all, sems = refs[7 * n_dp + 14 :]
    output, d_hidden, d_context, d_w_out = held
    copies = [pltpu.make_async_copy(held[n], targets[n], sems.at[n]) for n in range(4)]
    rows, width = hid[0].shape
    chunk = moe[0].shape[1]
    for i in range(2):
        for j in range(2):
            columns = pl.ds(pl.multiple_of(own_columns(i, j, chunk), chunk), chunk)
            for k in range(n_dp):
                piece = back[(i * n_dp + k) * 2 + j]
                summed[k * rows : (k + 1) * rows, columns] = piece[...].astype(F32) * gain[:, columns]
            piece = moe[i * 2 + j]
            output[:, columns] = (hid[0][:, columns].astype(F32) + piece[...].astype(F32)).astype(BF16)
    copies[0].start()

    few = rows * n_dp <= FEW_ROWS
    squares = jnp.zeros((rows * n_dp, 1), F32)
    products = squares
    for step in range(width // 512):
        columns = pl.ds(step * 512, 512)
        value = rows_of(hid, columns)
        squares = squares + jnp.sum(value * value, axis=1, keepdims=True)
        products = products + jnp.sum(value * summed[:, columns], axis=1, keepdims=True)
    scale = lax.rsqrt(squares / width + EPSILON)
    centre = scale * products / width

    def total(step):
        columns = pl.ds(place(step, 512), 512)
        unit_rows = rows_of(hid, columns) * scale
        value = rows_of(grads, columns) + scale * (summed[:, columns] - unit_rows * centre)
        d_all[:, columns] = value.astype(BF16)
        d_hidden[:, columns] = value[:rows].astype(BF16)

    loop(width // 512, total, few)
    copies[1].start()
    d_context[...] = dot(d_hidden[...], w_out[...], ((1,), (1,))).astype(BF16)
    part = width // n_dp
    copies[2].start()
    heads = d_context.shape[1]
    turned = jnp.concatenate([small[:, :heads] for small in smalls], axis=0).T.astype(BF16)
    step_width = min(part, 512)

    def product(step):
        columns = pl.ds(pl.multiple_of(lax.axis_index("dp") * part + step * step_width, step_width), step_width)
        d_w_out[:, pl.ds(place(step, step_width), step_width)] = dot(
            turned, d_all[:, columns], ((1,), (0,))
        ).astype(BF16)

    loop(part // step_width, product, few)
    copies[3].start()
    for copy in copies:
        copy.wait()


def run(kernel, n_dp, operands, outs, scratch, cost, name, far=(), out_space=pltpu.VMEM):
    spaces = [pltpu.HBM if n in far else pltpu.VMEM for n in range(len(operands))]
    held = [pltpu.with_memory_space_constraint(value, space) for value, space in zip(operands, spaces)]
    kinds = [out_space(shape, kind) for shape, kind in outs]
    return pl.pallas_call(
        functools.partial(kernel, n_dp),
        out_shape=kinds,
        in_specs=[pl.BlockSpec(memory_space=space) for space in spaces],
        out_specs=[pl.BlockSpec(memory_space=out_space)] * len(outs),
        scratch_shapes=scratch,
        compiler_params=pltpu.CompilerParams(vmem_limit_bytes=VMEM_LIMIT),
        cost_estimate=pl.CostEstimate(flops=0, bytes_accessed=cost, transcendentals=0),
        name=name,
    )(*held)


def per_device(
    hidden_in, norm_gain, route_ids, route_gates, w_gate, w_up, w_down, context, w_out, grad_out
):
    n_dp, n_hi = lax.axis_size("dp"), lax.axis_size("hi")
    rows, width = hidden_in.shape
    top, heads = route_ids.shape[1], context.shape[1]
    all_rows, units, chunk = n_dp * rows, w_gate.shape[2], width // 4

    def swap(value, axes, turn):
        sizes = [lax.axis_size(name) for name in axes]
        count = 1
        for size in sizes:
            count *= size
        return lax.ppermute(value, axes, [(i, i ^ turn) for i in range(count)])

    def all_blocks(value):
        return [value] + [swap(value, ("dp",), k) for k in range(1, n_dp)]

    weights = 2 * width * units
    shares = ((n_dp, 2, rows, chunk), BF16)
    wg, wu, wd, gain = w_gate[0], w_up[0], w_down[0], norm_gain.reshape(1, width)
    (small_own,) = run(
        gates_kernel, n_dp, [route_ids.T, route_gates.T, context, wg, wu, wd],
        [((rows, heads + LANES), F32)],
        [pltpu.VMEM((top, rows), jnp.int32), pltpu.VMEM((top, rows), F32), pltpu.VMEM((rows, heads), BF16),
         pltpu.SemaphoreType.DMA((3,))],
        4 * weights, "gates", far=range(6),
    )
    hid = all_blocks(hidden_in)
    smalls = all_blocks(small_own)
    grads = all_blocks(grad_out)

    def add(one, other):
        return (one.astype(F32) + other.astype(F32)).astype(BF16)

    def total_of(pieces):
        total = pieces[0].astype(F32)
        for piece in pieces[1:]:
            total = total + piece.astype(F32)
        return total.astype(BF16)

    pre_gate, pre_up, act = run(
        hidden_kernel, n_dp, hid + [gain, wg, wu],
        [((all_rows, units), F32), ((all_rows, units), F32), ((all_rows, units), BF16)],
        [pltpu.VMEM((all_rows, width), BF16)], 2 * weights, "hidden",
    )
    (out_send,) = run(
        functools.partial(outward_kernel, 1), n_dp, smalls + [act, wd], [shares], [],
        weights // 2, "outward_send",
    )
    out_other = swap(out_send, ("c",), 1)
    (out_keep,) = run(
        functools.partial(outward_kernel, 0), n_dp, smalls + [act, wd, out_send] + grads, [shares], [],
        weights // 2, "outward_keep",
    )
    out_half = add(out_keep, out_other)
    out_blocks = [swap(out_half[k], ("dp",), k) for k in range(1, n_dp)]
    block = (shares[0][1:], BF16)
    grad_gate, grad_up, out_block = run(
        backward_kernel, n_dp, grads + smalls + [pre_gate, pre_up, wd, out_half[0]],
        [((all_rows, units), BF16), ((all_rows, units), BF16), block],
        [pltpu.VMEM((all_rows, width), BF16)], weights, "backward",
    )
    in_send, out_block = run(
        functools.partial(inward_kernel, 1), n_dp, [grad_gate, grad_up, wg, wu, out_block],
        [shares, block], [], weights, "inward_send",
    )
    in_other = swap(in_send, ("c",), 1)
    out_block = total_of([out_block] + out_blocks)
    in_keep, out_block = run(
        functools.partial(inward_kernel, 0), n_dp, [grad_gate, grad_up, wg, wu, out_block], [shares, block], [],
        weights, "inward_keep",
    )
    *in_pieces, out_share, out_piece = run(
        join_kernel, n_dp, [in_keep, in_other, out_block], [((rows, chunk), BF16)] * (2 * n_dp + 2), [],
        rows * width, "join",
    )
    turns = [t for t in range(2 * n_dp - 1, 0, -1)]
    in_share = total_of([in_pieces[0]] + [swap(in_pieces[t], ("dp", "y"), t) for t in turns])
    out_total = add(out_share, swap(out_piece, ("y",), 1))
    in_total = total_of([in_share] + [swap(in_share, ("hi",), t) for t in range(1, n_hi)])
    turn = 1
    while turn < n_hi:
        out_total = add(out_total, swap(out_total, ("hi",), turn))
        turn = 2 * turn
    order = [t for t in turns if t < 2] + [t for t in turns if t >= 2]
    spread = {t: swap(in_total, ("dp", "y"), t) for t in order}
    back = [in_total] + [spread[t] for t in range(1, 2 * n_dp)]
    moe = [out_total, swap(out_total, ("y",), 1)]
    back = back + [swap(piece, ("c",), 1) for piece in back]
    moe = moe + [swap(piece, ("c",), 1) for piece in moe]
    outs = [((rows, width), BF16), ((rows, width), BF16), ((rows, heads), BF16), ((heads, width // n_dp), BF16)]
    return run(
        finish_kernel, n_dp, hid + grads + smalls + back + moe + [gain, w_out], outs,
        [pltpu.VMEM(*out) for out in outs]
        + [pltpu.VMEM((all_rows, width), F32), pltpu.VMEM((all_rows, width), BF16), pltpu.SemaphoreType.DMA((4,))],
        weights, "finish", out_space=pltpu.HBM,
    )


def solution(mesh):
    n_dp, n_e = mesh.shape["dp"], mesh.shape["expert"]
    names = ("dp", "hi", "y", "c")
    mesh = jax.sharding.Mesh(mesh.devices.reshape(n_dp, n_e // 4, 2, 2), names)
    expert = names[1:]
    return jax.shard_map(
        per_device,
        mesh=mesh,
        in_specs=(
            P("dp", None),
            P(),
            P("dp", None),
            P("dp", None),
            P(expert, None, "dp"),
            P(expert, None, "dp"),
            P(expert, "dp", None),
            P("dp", expert),
            P(expert, None),
            P("dp", None),
        ),
        out_specs=(P("dp", None), P("dp", None), P("dp", expert), P(expert, "dp")),
        check_vma=False,
    )
```

```python
import functools

import jax
import jax.numpy as jnp
from jax import lax
from jax.experimental import pallas as pl
from jax.experimental.pallas import tpu as pltpu
from jax.sharding import PartitionSpec as P

EPSILON = 1e-06
F32 = jnp.float32
BF16 = jnp.bfloat16
STEP = 256
LANES = 128
LOAD_PIECES = 8
FEW_ROWS = 64
VMEM_LIMIT = 12 * 1024 * 1024


def dot(a, b, dims):
    return lax.dot_general(a, b, (dims, ((), ())), preferred_element_type=F32)


def place(step, count):
    return pl.multiple_of(step * count, count)


def rows_of(refs, columns):
    return jnp.concatenate([ref[:, columns].astype(F32) for ref in refs], axis=0)


def own_columns(i, j, width):
    return ((lax.axis_index("y") ^ j) * 2 + (lax.axis_index("c") ^ i)) * width


def store_blocks(out_ref, j, columns, value, count):
    rows = value.shape[0] // count
    for k in range(count):
        out_ref[k, j, :, columns] = value[k * rows : (k + 1) * rows].astype(BF16)


def gates_kernel(n_dp, named, weights, context, w_gate, w_up, w_down, small, *held):
    targets, sems = held[:3], held[3]
    copies = [
        pltpu.make_async_copy(source, target, sems.at[n])
        for n, (source, target) in enumerate(zip((named, weights, context), targets))
    ]
    for copy in copies:
        copy.start()
    for copy in copies:
        copy.wait()
    named_held, weights_held, context_held = targets
    rows, heads = context_held.shape
    expert = (lax.axis_index("hi") * 2 + lax.axis_index("y")) * 2 + lax.axis_index("c")
    row = jnp.sum(jnp.where(named_held[...] == expert, weights_held[...], 0.0), axis=0, keepdims=True)
    square = (rows, rows)
    diagonal = lax.broadcasted_iota(jnp.int32, square, 0) == lax.broadcasted_iota(jnp.int32, square, 1)
    gate = jnp.sum(jnp.where(diagonal, row, 0.0), axis=1, keepdims=True)
    small[:, :heads] = context_held[...].astype(F32)
    small[:, heads:] = jnp.broadcast_to(gate, (rows, LANES))


def unit_step(units):
    return STEP if units % STEP == 0 else units


def loop(count, body, unroll):
    if unroll:
        for step in range(count):
            body(step)
    else:
        def carried(step, carry):
            body(step)
            return carry

        lax.fori_loop(0, count, carried, 0)


def gates_of(smalls):
    return jnp.concatenate([small[:, small.shape[1] - LANES : small.shape[1] - LANES + 1] for small in smalls], axis=0)


def hidden_kernel(n_dp, *refs):
    hid = refs[:n_dp]
    gain, w_gate, w_up, pre_gate, pre_up, act, normed = refs[n_dp:]
    total = hid[0].shape[0] * n_dp
    width = hid[0].shape[1]
    few = total <= FEW_ROWS
    sums = jnp.zeros((total, 1), F32)
    for step in range(width // 512):
        value = rows_of(hid, pl.ds(step * 512, 512))
        sums = sums + jnp.sum(value * value, axis=1, keepdims=True)
    scale = lax.rsqrt(sums / width + EPSILON)

    def norm(step):
        columns = pl.ds(place(step, 512), 512)
        normed[:, columns] = (rows_of(hid, columns) * scale * gain[:, columns]).astype(BF16)

    loop(width // 512, norm, few)

    size = unit_step(w_gate.shape[1])

    def hidden_units(step):
        columns = pl.ds(place(step, size), size)
        gate_part = dot(normed[...], w_gate[:, columns], ((1,), (0,)))
        up_part = dot(normed[...], w_up[:, columns], ((1,), (0,)))
        pre_gate[:, columns] = gate_part
        pre_up[:, columns] = up_part
        act[:, columns] = (gate_part * jax.nn.sigmoid(gate_part) * up_part).astype(BF16)

    loop(w_gate.shape[1] // size, hidden_units, few)


def outward_kernel(i, n_dp, *refs):
    smalls = refs[:n_dp]
    act, w_down, *_, target = refs[n_dp:]
    weight = gates_of(smalls)
    chunk = target.shape[3]
    few = act.shape[0] <= FEW_ROWS
    for j in range(2):
        first = own_columns(i, j, chunk)

        def outward(step):
            columns = pl.ds(pl.multiple_of(first + step * STEP, STEP), STEP)
            part = weight * dot(act[...], w_down[:, columns], ((1,), (0,)))
            store_blocks(target, j, pl.ds(place(step, STEP), STEP), part, n_dp)

        loop(chunk // STEP, outward, few)


def inward_part(i, n_dp, grad_refs, w_gate, w_up, target):
    chunk = target.shape[3]
    few = grad_refs[0].shape[0] <= FEW_ROWS
    for j in range(2):
        first = own_columns(i, j, chunk)

        def inward(step):
            columns = pl.ds(pl.multiple_of(first + step * STEP, STEP), STEP)
            part = 0.0
            for parity, weights in ((0, w_gate), (1, w_up)):
                start = 0
                for ref in grad_refs[parity::2]:
                    part = part + dot(ref[...], weights[columns, start : start + ref.shape[1]], ((1,), (1,)))
                    start += ref.shape[1]
            store_blocks(target, j, pl.ds(place(step, STEP), STEP), part, n_dp)

        loop(chunk // STEP, inward, few)


def gradients(first, weighted, pre_gate, pre_up, w_down, grad_gate, grad_up, few):
    size = unit_step(w_down.shape[0])

    def hidden_units(step):
        columns = pl.ds(place(step, size), size)
        units = pl.ds(first + step * size, size)
        back = dot(weighted[...], w_down[units, :], ((1,), (1,)))
        gate_part, up_part = pre_gate[:, units], pre_up[:, units]
        sig = jax.nn.sigmoid(gate_part)
        grad_gate[:, columns] = (back * up_part * sig * (1.0 + gate_part * (1.0 - sig))).astype(BF16)
        grad_up[:, columns] = (back * gate_part * sig).astype(BF16)

    loop(grad_gate.shape[1] // size, hidden_units, few or grad_gate.shape[1] == size)


def backward_first_kernel(n_dp, *refs):
    grads, smalls = refs[:n_dp], refs[n_dp : 2 * n_dp]
    pre_gate, pre_up, w_down, waiting, grad_gate, grad_up, weighted, passed = refs[2 * n_dp :]
    passed[...] = waiting[...]
    weight = gates_of(smalls)
    few = weighted.shape[0] <= FEW_ROWS

    def weigh(step):
        columns = pl.ds(place(step, 512), 512)
        weighted[:, columns] = (weight * rows_of(grads, columns)).astype(BF16)

    loop(weighted.shape[1] // 512, weigh, few)
    gradients(0, weighted, pre_gate, pre_up, w_down, grad_gate, grad_up, few)


def backward_rest_kernel(n_dp, weighted, pre_gate, pre_up, w_down, waiting, grad_gate, grad_up, passed):
    passed[...] = waiting[...]
    first = pre_gate.shape[1] - grad_gate.shape[1]
    gradients(first, weighted, pre_gate, pre_up, w_down, grad_gate, grad_up, True)


def inward_kernel(i, n_dp, *refs):
    w_gate, w_up, waiting, target, passed = refs[-5:]
    passed[...] = waiting[...]
    inward_part(i, n_dp, refs[:-5], w_gate, w_up, target)


def join_kernel(n_dp, in_keep, in_other, out_block, *refs):
    for t in range(2 * n_dp):
        k, j = t // 2, t % 2
        refs[t][...] = (in_keep[k, j].astype(F32) + in_other[k, j].astype(F32)).astype(BF16)
    refs[-1][...] = out_block[...]


def finish_kernel(n_dp, *refs):
    hid, grads, smalls = refs[:n_dp], refs[n_dp : 2 * n_dp], refs[2 * n_dp : 3 * n_dp]
    back, moe = refs[3 * n_dp : 7 * n_dp], refs[7 * n_dp : 7 * n_dp + 2]
    gain, w_out = refs[7 * n_dp + 2 : 7 * n_dp + 4]
    targets, held = refs[7 * n_dp + 4 : 7 * n_dp + 8], refs[7 * n_dp + 8 : 7 * n_dp + 12]
    summed, d_all, sems = refs[7 * n_dp + 12 :]
    output, d_hidden, d_context, d_w_out = held
    copies = [pltpu.make_async_copy(held[n], targets[n], sems.at[n]) for n in range(4)]
    rows, width = hid[0].shape
    chunk = moe[0].shape[2]
    for i in range(2):
        for j in range(2):
            columns = pl.ds(pl.multiple_of(own_columns(i, j, chunk), chunk), chunk)
            for k in range(n_dp):
                piece = back[(i * n_dp + k) * 2 + j]
                summed[k * rows : (k + 1) * rows, columns] = piece[...].astype(F32) * gain[:, columns]
            output[:, columns] = (hid[0][:, columns].astype(F32) + moe[i][j].astype(F32)).astype(BF16)
    copies[0].start()

    few = rows * n_dp <= FEW_ROWS
    squares = jnp.zeros((rows * n_dp, 1), F32)
    products = squares
    for step in range(width // 512):
        columns = pl.ds(step * 512, 512)
        value = rows_of(hid, columns)
        squares = squares + jnp.sum(value * value, axis=1, keepdims=True)
        products = products + jnp.sum(value * summed[:, columns], axis=1, keepdims=True)
    scale = lax.rsqrt(squares / width + EPSILON)
    centre = scale * products / width

    def total(step):
        columns = pl.ds(place(step, 512), 512)
        unit_rows = rows_of(hid, columns) * scale
        value = rows_of(grads, columns) + scale * (summed[:, columns] - unit_rows * centre)
        d_all[:, columns] = value.astype(BF16)
        d_hidden[:, columns] = value[:rows].astype(BF16)

    loop(width // 512, total, few)
    copies[1].start()
    d_context[...] = dot(d_hidden[...], w_out[...], ((1,), (1,))).astype(BF16)
    part = width // n_dp
    copies[2].start()
    heads = d_context.shape[1]
    turned = jnp.concatenate([small[:, :heads] for small in smalls], axis=0).T.astype(BF16)
    step_width = min(part, 512)

    def product(step):
        columns = pl.ds(pl.multiple_of(lax.axis_index("dp") * part + step * step_width, step_width), step_width)
        d_w_out[:, pl.ds(place(step, step_width), step_width)] = dot(
            turned, d_all[:, columns], ((1,), (0,))
        ).astype(BF16)

    loop(part // step_width, product, few)
    copies[3].start()
    for copy in copies:
        copy.wait()


def run(kernel, n_dp, operands, outs, scratch, cost, name, far=(), out_space=pltpu.VMEM):
    spaces = [pltpu.HBM if n in far else pltpu.VMEM for n in range(len(operands))]
    held = [pltpu.with_memory_space_constraint(value, space) for value, space in zip(operands, spaces)]
    kinds = [out_space(shape, kind) for shape, kind in outs]
    return pl.pallas_call(
        functools.partial(kernel, n_dp),
        out_shape=kinds,
        in_specs=[pl.BlockSpec(memory_space=space) for space in spaces],
        out_specs=[pl.BlockSpec(memory_space=out_space)] * len(outs),
        scratch_shapes=scratch,
        compiler_params=pltpu.CompilerParams(vmem_limit_bytes=VMEM_LIMIT),
        cost_estimate=pl.CostEstimate(flops=0, bytes_accessed=cost, transcendentals=0),
        name=name,
    )(*held)


def per_device(
    hidden_in, norm_gain, route_ids, route_gates, w_gate, w_up, w_down, context, w_out, grad_out
):
    n_dp, n_hi = lax.axis_size("dp"), lax.axis_size("hi")
    rows, width = hidden_in.shape
    top, heads = route_ids.shape[1], context.shape[1]
    all_rows, units, chunk = n_dp * rows, w_gate.shape[2], width // 4

    def swap(value, axes, turn):
        sizes = [lax.axis_size(name) for name in axes]
        count = 1
        for size in sizes:
            count *= size
        return lax.ppermute(value, axes, [(i, i ^ turn) for i in range(count)])

    def all_blocks(value):
        return [value] + [swap(value, ("dp",), k) for k in range(1, n_dp)]

    weights = 2 * width * units
    shares = ((n_dp, 2, rows, chunk), BF16)
    wg, wu, wd, gain = w_gate[0], w_up[0], w_down[0], norm_gain.reshape(1, width)
    (small_own,) = run(
        gates_kernel, n_dp, [route_ids.T, route_gates.T, context, wg, wu, wd],
        [((rows, heads + LANES), F32)],
        [pltpu.VMEM((top, rows), jnp.int32), pltpu.VMEM((top, rows), F32), pltpu.VMEM((rows, heads), BF16),
         pltpu.SemaphoreType.DMA((3,))],
        4 * weights, "gates", far=range(6),
    )
    hid = all_blocks(hidden_in)
    smalls = all_blocks(small_own)
    grads = all_blocks(grad_out)

    def add(one, other):
        return (one.astype(F32) + other.astype(F32)).astype(BF16)

    def total_of(pieces):
        total = pieces[0].astype(F32)
        for piece in pieces[1:]:
            total = total + piece.astype(F32)
        return total.astype(BF16)

    pre_gate, pre_up, act = run(
        hidden_kernel, n_dp, hid + [gain, wg, wu],
        [((all_rows, units), F32), ((all_rows, units), F32), ((all_rows, units), BF16)],
        [pltpu.VMEM((all_rows, width), BF16)], 2 * weights, "hidden",
    )
    (out_send,) = run(
        functools.partial(outward_kernel, 1), n_dp, smalls + [act, wd], [shares], [],
        weights // 2, "outward_send",
    )
    out_other = swap(out_send, ("c",), 1)
    (out_keep,) = run(
        functools.partial(outward_kernel, 0), n_dp, smalls + [act, wd, out_send] + grads, [shares], [],
        weights // 2, "outward_keep",
    )
    size = unit_step(units)
    first_units, rest_units = ((all_rows, size), BF16), ((all_rows, units - size), BF16)
    gate_first, up_first, weighted, out_keep = run(
        backward_first_kernel, n_dp, grads + smalls + [pre_gate, pre_up, wd, out_keep],
        [first_units, first_units, ((all_rows, width), BF16), shares], [], weights // 3, "backward_first",
    )
    back_grads = [gate_first, up_first]
    out_half = add(out_keep, out_other)
    out_blocks = [swap(out_half[k], ("dp",), k) for k in range(1, n_dp)]
    block, out_block = (shares[0][1:], BF16), out_half[0]
    if size < units:
        gate_rest, up_rest, out_block = run(
            backward_rest_kernel, n_dp, [weighted, pre_gate, pre_up, wd, out_block],
            [rest_units, rest_units, block], [], weights * 2 // 3, "backward_rest",
        )
        back_grads = back_grads + [gate_rest, up_rest]
    in_send, out_block = run(
        functools.partial(inward_kernel, 1), n_dp, back_grads + [wg, wu, out_block],
        [shares, block], [], weights, "inward_send",
    )
    in_other = swap(in_send, ("c",), 1)
    out_block = total_of([out_block] + out_blocks)
    in_keep, out_block = run(
        functools.partial(inward_kernel, 0), n_dp, back_grads + [wg, wu, out_block], [shares, block], [],
        weights, "inward_keep",
    )
    *in_pieces, out_block = run(
        join_kernel, n_dp, [in_keep, in_other, out_block], [((rows, chunk), BF16)] * (2 * n_dp) + [block], [],
        rows * width, "join",
    )
    turns = [t for t in range(2 * n_dp - 1, 0, -1)]
    in_share = total_of([in_pieces[0]] + [swap(in_pieces[t], ("dp", "y"), t) for t in turns])
    out_total = add(out_block, swap(out_block, ("y",), 1)[::-1])
    in_total = total_of([in_share] + [swap(in_share, ("hi",), t) for t in range(1, n_hi)])
    turn = 1
    while turn < n_hi:
        out_total = add(out_total, swap(out_total, ("hi",), turn))
        turn = 2 * turn
    order = [t for t in turns if t < 2] + [t for t in turns if t >= 2]
    spread = {t: swap(in_total, ("dp", "y"), t) for t in order}
    back = [in_total] + [spread[t] for t in range(1, 2 * n_dp)]
    back = back + [swap(piece, ("c",), 1) for piece in back]
    moe = [out_total, swap(out_total, ("c",), 1)]
    outs = [((rows, width), BF16), ((rows, width), BF16), ((rows, heads), BF16), ((heads, width // n_dp), BF16)]
    return run(
        finish_kernel, n_dp, hid + grads + smalls + back + moe + [gain, w_out], outs,
        [pltpu.VMEM(*out) for out in outs]
        + [pltpu.VMEM((all_rows, width), F32), pltpu.VMEM((all_rows, width), BF16), pltpu.SemaphoreType.DMA((4,))],
        weights, "finish", out_space=pltpu.HBM,
    )


def solution(mesh):
    n_dp, n_e = mesh.shape["dp"], mesh.shape["expert"]
    names = ("dp", "hi", "y", "c")
    mesh = jax.sharding.Mesh(mesh.devices.reshape(n_dp, n_e // 4, 2, 2), names)
    expert = names[1:]
    return jax.shard_map(
        per_device,
        mesh=mesh,
        in_specs=(
            P("dp", None),
            P(),
            P("dp", None),
            P("dp", None),
            P(expert, None, "dp"),
            P(expert, None, "dp"),
            P(expert, "dp", None),
            P("dp", expert),
            P(expert, None),
            P("dp", None),
        ),
        out_specs=(P("dp", None), P("dp", None), P("dp", expert), P(expert, "dp")),
        check_vma=False,
    )
```

```python
import functools

import jax
import jax.numpy as jnp
from jax import lax
from jax.experimental import pallas as pl
from jax.experimental.pallas import tpu as pltpu
from jax.sharding import PartitionSpec as P

EPSILON = 1e-06
F32 = jnp.float32
BF16 = jnp.bfloat16
STEP = 256
LANES = 128
LOAD_PIECES = 8
FEW_ROWS = 64
VMEM_LIMIT = 12 * 1024 * 1024
VMEM_LIMIT_MANY = 24 * 1024 * 1024


def dot(a, b, dims):
    return lax.dot_general(a, b, (dims, ((), ())), preferred_element_type=F32)


def place(step, count):
    return pl.multiple_of(step * count, count)


def parity(number):
    shift = 1
    while shift < 32:
        number = number ^ (number >> shift)
        shift = 2 * shift
    return number & 1


def own_half():
    chip = lax.axis_index("dp") ^ lax.axis_index("y") ^ lax.axis_index("hi")
    return lax.axis_index("c") ^ parity(chip)


def own_columns(i, j, width):
    return ((lax.axis_index("y") ^ j) * 2 + (own_half() ^ i)) * width


def both_halves(refs, width, body):
    core, half = lax.axis_index("c"), width // 2
    size = 512 if len(refs[0]) <= 3 else 128
    for h in range(2):
        for step in range(half // size):
            columns = pl.ds(pl.multiple_of((core ^ h) * half + step * size, size), size)

            def rows_at(group):
                first = group[0][:, columns].astype(F32)
                others = [ref[:, step * size : (step + 1) * size].astype(F32) for ref in group[1 + h :: 2]]
                return jnp.concatenate([first] + others, axis=0)

            body(columns, *[rows_at(group) for group in refs])


def store_blocks(out_ref, j, columns, value, count):
    rows = value.shape[0] // count
    for k in range(count):
        out_ref[k, j, :, columns] = value[k * rows : (k + 1) * rows].astype(BF16)


def gates_kernel(n_dp, named, weights, context, w_gate, w_up, w_down, small, *held):
    targets, sems = held[:3], held[3]
    copies = [
        pltpu.make_async_copy(source, target, sems.at[n])
        for n, (source, target) in enumerate(zip((named, weights, context), targets))
    ]
    for copy in copies:
        copy.start()
    for copy in copies:
        copy.wait()
    named_held, weights_held, context_held = targets
    rows, heads = context_held.shape
    expert = (lax.axis_index("hi") * 2 + lax.axis_index("y")) * 2 + lax.axis_index("c")
    row = jnp.sum(jnp.where(named_held[...] == expert, weights_held[...], 0.0), axis=0, keepdims=True)
    square = (rows, rows)
    diagonal = lax.broadcasted_iota(jnp.int32, square, 0) == lax.broadcasted_iota(jnp.int32, square, 1)
    gate = jnp.sum(jnp.where(diagonal, row, 0.0), axis=1, keepdims=True)
    small[:, :heads] = context_held[...].astype(F32)
    small[:, heads:] = jnp.broadcast_to(gate, (rows, LANES))


def unit_step(units):
    return STEP if units % STEP == 0 else units


def loop(count, body, unroll):
    if unroll:
        for step in range(count):
            body(step)
    else:
        def carried(step, carry):
            body(step)
            return carry

        lax.fori_loop(0, count, carried, 0)


def gates_of(smalls):
    return jnp.concatenate([small[:, small.shape[1] - LANES : small.shape[1] - LANES + 1] for small in smalls], axis=0)


def hidden_kernel(n_dp, *refs):
    hid = refs[: 2 * n_dp - 1]
    gain, w_gate, w_up, pre_gate, pre_up, act, normed = refs[2 * n_dp - 1 :]
    total, width = hid[0].shape[0] * n_dp, hid[0].shape[1]
    few = total <= FEW_ROWS
    sums = [jnp.zeros((total, 1), F32)]

    def square(columns, value):
        sums[0] = sums[0] + jnp.sum(value * value, axis=1, keepdims=True)

    both_halves([hid], width, square)
    scale = lax.rsqrt(sums[0] / width + EPSILON)

    def norm(columns, value):
        normed[:, columns] = (value * scale * gain[:, columns]).astype(BF16)

    both_halves([hid], width, norm)
    size = unit_step(w_gate.shape[1])

    def hidden_units(step):
        columns = pl.ds(place(step, size), size)
        gate_part = dot(normed[...], w_gate[:, columns], ((1,), (0,)))
        up_part = dot(normed[...], w_up[:, columns], ((1,), (0,)))
        pre_gate[:, columns] = gate_part
        pre_up[:, columns] = up_part
        act[:, columns] = (gate_part * jax.nn.sigmoid(gate_part) * up_part).astype(BF16)

    loop(w_gate.shape[1] // size, hidden_units, few)


def outward_kernel(i, n_dp, *refs):
    smalls = refs[:n_dp]
    act, w_down, *_, target = refs[n_dp:]
    weight = gates_of(smalls)
    chunk = target.shape[3]
    few = act.shape[0] <= FEW_ROWS
    for j in range(2):
        first = own_columns(i, j, chunk)

        def outward(step):
            columns = pl.ds(pl.multiple_of(first + step * STEP, STEP), STEP)
            part = weight * dot(act[...], w_down[:, columns], ((1,), (0,)))
            store_blocks(target, j, pl.ds(place(step, STEP), STEP), part, n_dp)

        loop(chunk // STEP, outward, few)


def inward_part(i, n_dp, grad_refs, w_gate, w_up, target):
    chunk = target.shape[3]
    few = grad_refs[0].shape[0] <= FEW_ROWS
    for j in range(2):
        first = own_columns(i, j, chunk)

        def inward(step):
            columns = pl.ds(pl.multiple_of(first + step * STEP, STEP), STEP)
            part = 0.0
            for parity, weights in ((0, w_gate), (1, w_up)):
                start = 0
                for ref in grad_refs[parity::2]:
                    part = part + dot(ref[...], weights[columns, start : start + ref.shape[1]], ((1,), (1,)))
                    start += ref.shape[1]
            store_blocks(target, j, pl.ds(place(step, STEP), STEP), part, n_dp)

        loop(chunk // STEP, inward, few)


def gradients(first, weighted, pre_gate, pre_up, w_down, grad_gate, grad_up, few):
    size = unit_step(w_down.shape[0])

    def hidden_units(step):
        columns = pl.ds(place(step, size), size)
        units = pl.ds(first + step * size, size)
        back = dot(weighted[...], w_down[units, :], ((1,), (1,)))
        gate_part, up_part = pre_gate[:, units], pre_up[:, units]
        sig = jax.nn.sigmoid(gate_part)
        grad_gate[:, columns] = (back * up_part * sig * (1.0 + gate_part * (1.0 - sig))).astype(BF16)
        grad_up[:, columns] = (back * gate_part * sig).astype(BF16)

    loop(grad_gate.shape[1] // size, hidden_units, few or grad_gate.shape[1] == size)


def backward_first_kernel(n_dp, *refs):
    grads, smalls = refs[: 2 * n_dp - 1], refs[2 * n_dp - 1 : 3 * n_dp - 1]
    pre_gate, pre_up, w_down, waiting, grad_gate, grad_up, weighted, passed = refs[3 * n_dp - 1 :]
    passed[...] = waiting[...]
    weight = gates_of(smalls)
    few = weighted.shape[0] <= FEW_ROWS

    def weigh(columns, value):
        weighted[:, columns] = (weight * value).astype(BF16)

    both_halves([grads], weighted.shape[1], weigh)
    gradients(0, weighted, pre_gate, pre_up, w_down, grad_gate, grad_up, few)


def backward_rest_kernel(n_dp, weighted, pre_gate, pre_up, w_down, waiting, grad_gate, grad_up, passed):
    passed[...] = waiting[...]
    first = pre_gate.shape[1] - grad_gate.shape[1]
    gradients(first, weighted, pre_gate, pre_up, w_down, grad_gate, grad_up, True)


def inward_kernel(i, n_dp, *refs):
    w_gate, w_up, waiting, target, passed = refs[-5:]
    passed[...] = waiting[...]
    inward_part(i, n_dp, refs[:-5], w_gate, w_up, target)


def join_kernel(n_dp, in_keep, in_other, out_block, *refs):
    for t in range(2 * n_dp):
        k, j = t // 2, t % 2
        refs[t][...] = (in_keep[k, j].astype(F32) + in_other[k, j].astype(F32)).astype(BF16)
    refs[-1][...] = out_block[...]


def finish_kernel(n_dp, *refs):
    count = 2 * n_dp - 1
    hid, grads, smalls = refs[:count], refs[count : 2 * count], refs[2 * count : 2 * count + n_dp]
    refs = refs[2 * count + n_dp :]
    back, moe = refs[: 4 * n_dp], refs[4 * n_dp : 4 * n_dp + 2]
    refs = refs[4 * n_dp + 2 :]
    gain, w_out, targets, held = refs[0], refs[1], refs[2:6], refs[6:10]
    summed, d_all, sems = refs[10:]
    output, d_hidden, d_context, d_w_out = held
    copies = [pltpu.make_async_copy(held[n], targets[n], sems.at[n]) for n in range(4)]
    rows, width = hid[0].shape
    chunk = moe[0].shape[2]
    for i in range(2):
        for j in range(2):
            columns = pl.ds(pl.multiple_of(own_columns(i, j, chunk), chunk), chunk)
            for k in range(n_dp):
                piece = back[(i * n_dp + k) * 2 + j]
                summed[k * rows : (k + 1) * rows, columns] = piece[...].astype(F32) * gain[:, columns]
            output[:, columns] = (hid[0][:, columns].astype(F32) + moe[i][j].astype(F32)).astype(BF16)
    copies[0].start()

    few = rows * n_dp <= FEW_ROWS
    sums = [jnp.zeros((rows * n_dp, 1), F32)] * 2

    def products(columns, value):
        sums[0] = sums[0] + jnp.sum(value * value, axis=1, keepdims=True)
        sums[1] = sums[1] + jnp.sum(value * summed[:, columns], axis=1, keepdims=True)

    both_halves([hid], width, products)
    scale = lax.rsqrt(sums[0] / width + EPSILON)
    centre = scale * sums[1] / width

    def total(columns, value, grad):
        result = grad + scale * (summed[:, columns] - value * scale * centre)
        d_all[:, columns] = result.astype(BF16)
        d_hidden[:, columns] = result[:rows].astype(BF16)

    both_halves([hid, grads], width, total)
    copies[1].start()
    d_context[...] = dot(d_hidden[...], w_out[...], ((1,), (1,))).astype(BF16)
    part = width // n_dp
    copies[2].start()
    heads = d_context.shape[1]
    turned = jnp.concatenate([small[:, :heads] for small in smalls], axis=0).T.astype(BF16)
    step_width = min(part, 512)

    def product(step):
        columns = pl.ds(pl.multiple_of(lax.axis_index("dp") * part + step * step_width, step_width), step_width)
        d_w_out[:, pl.ds(place(step, step_width), step_width)] = dot(
            turned, d_all[:, columns], ((1,), (0,))
        ).astype(BF16)

    loop(part // step_width, product, few)
    copies[3].start()
    for copy in copies:
        copy.wait()


def run(kernel, n_dp, operands, outs, scratch, cost, name, far=(), out_space=pltpu.VMEM):
    spaces = [pltpu.HBM if n in far else pltpu.VMEM for n in range(len(operands))]
    held = [pltpu.with_memory_space_constraint(value, space) for value, space in zip(operands, spaces)]
    kinds = [out_space(shape, kind) for shape, kind in outs]
    return pl.pallas_call(
        functools.partial(kernel, n_dp),
        out_shape=kinds,
        in_specs=[pl.BlockSpec(memory_space=space) for space in spaces],
        out_specs=[pl.BlockSpec(memory_space=out_space)] * len(outs),
        scratch_shapes=scratch,
        compiler_params=pltpu.CompilerParams(vmem_limit_bytes=VMEM_LIMIT if n_dp <= 2 else VMEM_LIMIT_MANY),
        cost_estimate=pl.CostEstimate(flops=0, bytes_accessed=cost, transcendentals=0),
        name=name,
    )(*held)


def per_device(
    hidden_in, norm_gain, route_ids, route_gates, w_gate, w_up, w_down, context, w_out, grad_out
):
    n_dp, n_hi = lax.axis_size("dp"), lax.axis_size("hi")
    rows, width = hidden_in.shape
    top, heads = route_ids.shape[1], context.shape[1]
    all_rows, units, chunk = n_dp * rows, w_gate.shape[2], width // 4

    def swap(value, axes, turn, cross=True):
        count = 2
        for name in axes:
            count *= lax.axis_size(name)
        turn = 2 * turn + (parity(turn) if cross else 0)
        return lax.ppermute(value, axes + ("c",), [(i, i ^ turn) for i in range(count)])

    def other_core(value):
        return lax.ppermute(value, ("c",), [(0, 1), (1, 0)])

    def all_blocks(value):
        half = lax.dynamic_slice_in_dim(value, lax.axis_index("c") * (width // 2), width // 2, 1)
        here = [swap(half, ("dp",), k, False) for k in range(1, n_dp)]
        return [value] + [piece for one in here for piece in (one, other_core(one))]

    weights = 2 * width * units
    shares = ((n_dp, 2, rows, chunk), BF16)
    wg, wu, wd, gain = w_gate[0], w_up[0], w_down[0], norm_gain.reshape(1, width)
    (small_own,) = run(
        gates_kernel, n_dp, [route_ids.T, route_gates.T, context, wg, wu, wd],
        [((rows, heads + LANES), F32)],
        [pltpu.VMEM((top, rows), jnp.int32), pltpu.VMEM((top, rows), F32), pltpu.VMEM((rows, heads), BF16),
         pltpu.SemaphoreType.DMA((3,))],
        4 * weights, "gates", far=range(6),
    )
    hid = all_blocks(hidden_in)
    smalls = [small_own] + [swap(small_own, ("dp",), k, False) for k in range(1, n_dp)]
    grads = all_blocks(grad_out)

    def add(one, other):
        return (one.astype(F32) + other.astype(F32)).astype(BF16)

    def total_of(pieces):
        total = pieces[0].astype(F32)
        for piece in pieces[1:]:
            total = total + piece.astype(F32)
        return total.astype(BF16)

    pre_gate, pre_up, act = run(
        hidden_kernel, n_dp, hid + [gain, wg, wu],
        [((all_rows, units), F32), ((all_rows, units), F32), ((all_rows, units), BF16)],
        [pltpu.VMEM((all_rows, width), BF16)], 2 * weights, "hidden",
    )
    (out_send,) = run(
        functools.partial(outward_kernel, 1), n_dp, smalls + [act, wd], [shares], [],
        weights // 2, "outward_send",
    )
    out_other = other_core(out_send)
    (out_keep,) = run(
        functools.partial(outward_kernel, 0), n_dp, smalls + [act, wd, out_send] + grads, [shares], [],
        weights // 2, "outward_keep",
    )
    size = unit_step(units)
    first_units, rest_units = ((all_rows, size), BF16), ((all_rows, units - size), BF16)
    gate_first, up_first, weighted, out_keep = run(
        backward_first_kernel, n_dp, grads + smalls + [pre_gate, pre_up, wd, out_keep],
        [first_units, first_units, ((all_rows, width), BF16), shares], [], weights // 3, "backward_first",
    )
    back_grads = [gate_first, up_first]
    out_half = add(out_keep, out_other)
    out_blocks = [swap(out_half[k], ("dp",), k) for k in range(1, n_dp)]
    block, out_block = (shares[0][1:], BF16), out_half[0]
    if size < units:
        gate_rest, up_rest, out_block = run(
            backward_rest_kernel, n_dp, [weighted, pre_gate, pre_up, wd, out_block],
            [rest_units, rest_units, block], [], weights * 2 // 3, "backward_rest",
        )
        back_grads = back_grads + [gate_rest, up_rest]
    in_send, out_block = run(
        functools.partial(inward_kernel, 1), n_dp, back_grads + [wg, wu, out_block],
        [shares, block], [], weights, "inward_send",
    )
    in_other = other_core(in_send)
    out_block = total_of([out_block] + out_blocks)
    in_keep, out_block = run(
        functools.partial(inward_kernel, 0), n_dp, back_grads + [wg, wu, out_block], [shares, block], [],
        weights, "inward_keep",
    )
    *in_pieces, out_block = run(
        join_kernel, n_dp, [in_keep, in_other, out_block], [((rows, chunk), BF16)] * (2 * n_dp) + [block], [],
        rows * width, "join",
    )
    turns = [t for t in range(2 * n_dp - 1, 0, -1)]
    in_share = total_of([in_pieces[0]] + [swap(in_pieces[t], ("dp", "y"), t) for t in turns])
    out_total = add(out_block, swap(out_block, ("y",), 1)[::-1])
    in_total = total_of([in_share] + [swap(in_share, ("hi",), t) for t in range(1, n_hi)])
    turn = 1
    while turn < n_hi:
        out_total = add(out_total, swap(out_total, ("hi",), turn))
        turn = 2 * turn
    order = [t for t in turns if t < 2] + [t for t in turns if t >= 2]
    spread = {t: swap(in_total, ("dp", "y"), t) for t in order}
    back = [in_total] + [spread[t] for t in range(1, 2 * n_dp)]
    back = back + [other_core(piece) for piece in back]
    moe = [out_total, other_core(out_total)]
    outs = [((rows, width), BF16), ((rows, width), BF16), ((rows, heads), BF16), ((heads, width // n_dp), BF16)]
    return run(
        finish_kernel, n_dp, hid + grads + smalls + back + moe + [gain, w_out], outs,
        [pltpu.VMEM(*out) for out in outs]
        + [pltpu.VMEM((all_rows, width), F32), pltpu.VMEM((all_rows, width), BF16), pltpu.SemaphoreType.DMA((4,))],
        weights, "finish", out_space=pltpu.HBM,
    )


def solution(mesh):
    n_dp, n_e = mesh.shape["dp"], mesh.shape["expert"]
    names = ("dp", "hi", "y", "c")
    mesh = jax.sharding.Mesh(mesh.devices.reshape(n_dp, n_e // 4, 2, 2), names)
    expert = names[1:]
    return jax.shard_map(
        per_device,
        mesh=mesh,
        in_specs=(
            P("dp", None),
            P(),
            P("dp", None),
            P("dp", None),
            P(expert, None, "dp"),
            P(expert, None, "dp"),
            P(expert, "dp", None),
            P("dp", expert),
            P(expert, None),
            P("dp", None),
        ),
        out_specs=(P("dp", None), P("dp", None), P("dp", expert), P(expert, "dp")),
        check_vma=False,
    )
```

```python
import functools

import jax
import jax.numpy as jnp
from jax import lax
from jax.experimental import pallas as pl
from jax.experimental.pallas import tpu as pltpu
from jax.sharding import PartitionSpec as P

EPSILON = 1e-06
F32 = jnp.float32
BF16 = jnp.bfloat16
STEP = 256
LANES = 128
TERMS = 3
LOAD_PIECES = 8
FEW_ROWS = 64
VMEM_LIMIT = 12 * 1024 * 1024
VMEM_LIMIT_MANY = 24 * 1024 * 1024


def dot(a, b, dims):
    return lax.dot_general(a, b, (dims, ((), ())), preferred_element_type=F32)


def place(step, count):
    return pl.multiple_of(step * count, count)


def parity(number):
    shift = 1
    while shift < 32:
        number = number ^ (number >> shift)
        shift = 2 * shift
    return number & 1


def own_half():
    chip = lax.axis_index("dp") ^ lax.axis_index("y") ^ lax.axis_index("hi")
    return lax.axis_index("c") ^ parity(chip)


def own_columns(i, j, width):
    return ((lax.axis_index("y") ^ j) * 2 + (own_half() ^ i)) * width


def folded(value):
    return sum(value[:, start : start + LANES] for start in range(0, value.shape[1], LANES))


def both_halves(refs, width, body):
    core, half = lax.axis_index("c"), width // 2
    size = 512 if len(refs[0]) <= 3 else 128
    for h in range(2):
        for step in range(half // size):
            columns = pl.ds(pl.multiple_of((core ^ h) * half + step * size, size), size)

            def rows_at(group):
                first = group[0][:, columns].astype(F32)
                others = [ref[:, step * size : (step + 1) * size].astype(F32) for ref in group[1 + h :: 2]]
                return jnp.concatenate([first] + others, axis=0)

            body(columns, *[rows_at(group) for group in refs])


def store_blocks(out_ref, j, columns, value, count):
    rows = value.shape[0] // count
    for k in range(count):
        out_ref[k, j, :, columns] = value[k * rows : (k + 1) * rows].astype(BF16)


def cut_kernel(n_dp, source, target, sem):
    width = target.shape[1]
    columns = pl.ds(pl.multiple_of(lax.axis_index("c") * width, width), width)
    copy = pltpu.make_async_copy(source.at[:, columns], target, sem)
    copy.start()
    copy.wait()


def gates_kernel(n_dp, named, weights, context, grads, w_gate, w_up, w_down, packed, named_held, weights_held, sems):
    width, heads = grads.shape[1] // 2, context.shape[1]
    columns = pl.ds(pl.multiple_of(lax.axis_index("c") * width, width), width)
    pairs = [
        (named, named_held), (weights, weights_held), (context, packed.at[:, pl.ds(width, heads)]),
        (grads.at[:, columns], packed.at[:, pl.ds(0, width)]),
    ]
    copies = [pltpu.make_async_copy(*pair, sems.at[n]) for n, pair in enumerate(pairs)]
    for copy in copies:
        copy.start()
    copies[0].wait()
    copies[1].wait()
    rows = context.shape[0]
    expert = (lax.axis_index("hi") * 2 + lax.axis_index("y")) * 2 + lax.axis_index("c")
    row = jnp.sum(jnp.where(named_held[...] == expert, weights_held[...], 0.0), axis=0, keepdims=True)
    square = (rows, rows)
    diagonal = lax.broadcasted_iota(jnp.int32, square, 0) == lax.broadcasted_iota(jnp.int32, square, 1)
    gate = jnp.sum(jnp.where(diagonal, row, 0.0), axis=1, keepdims=True)
    lane = lax.broadcasted_iota(jnp.int32, (rows, LANES), 1)
    rest, block = jnp.broadcast_to(gate, (rows, LANES)), jnp.zeros((rows, LANES), F32)
    for term in range(TERMS):
        rounded = rest.astype(BF16).astype(F32)
        block = jnp.where(lane == term, rounded, block)
        rest = rest - rounded
    packed[:, width + heads :] = block.astype(BF16)
    copies[2].wait()
    copies[3].wait()


def unit_step(units):
    return STEP if units % STEP == 0 else units


def loop(count, body, unroll):
    if unroll:
        for step in range(count):
            body(step)
    else:
        def carried(step, carry):
            body(step)
            return carry

        lax.fori_loop(0, count, carried, 0)


def gates_of(packs):
    first = packs[0].shape[1] - LANES
    blocks = [pack[:, first : first + LANES].astype(F32) for pack in packs]
    gates = jnp.concatenate(blocks, axis=0)
    return gates[:, 0:1] + gates[:, 1:2] + gates[:, 2:3]


def hidden_kernel(n_dp, *refs):
    hid = refs[: 2 * n_dp - 1]
    gain, w_gate, w_up, pre_gate, pre_up, act, normed = refs[2 * n_dp - 1 :]
    total, width = hid[0].shape[0] * n_dp, hid[0].shape[1]
    few = total <= FEW_ROWS
    sums = [0.0]

    def square(columns, value):
        sums[0] = sums[0] + folded(value * value)

    both_halves([hid], width, square)
    scale = lax.rsqrt(jnp.sum(sums[0], axis=1, keepdims=True) / width + EPSILON)

    def norm(columns, value):
        normed[:, columns] = (value * scale * gain[:, columns]).astype(BF16)

    both_halves([hid], width, norm)
    size = unit_step(w_gate.shape[1])

    def hidden_units(step):
        columns = pl.ds(place(step, size), size)
        gate_part = dot(normed[...], w_gate[:, columns], ((1,), (0,)))
        up_part = dot(normed[...], w_up[:, columns], ((1,), (0,)))
        pre_gate[:, columns] = gate_part
        pre_up[:, columns] = up_part
        act[:, columns] = (gate_part * jax.nn.sigmoid(gate_part) * up_part).astype(BF16)

    loop(w_gate.shape[1] // size, hidden_units, few)


def outward_kernel(i, n_dp, *refs):
    smalls = refs[:n_dp]
    act, w_down, *_, target = refs[n_dp:]
    weight = gates_of(smalls)
    chunk = target.shape[3]
    few = act.shape[0] <= FEW_ROWS
    for j in range(2):
        first = own_columns(i, j, chunk)

        def outward(step):
            columns = pl.ds(pl.multiple_of(first + step * STEP, STEP), STEP)
            part = weight * dot(act[...], w_down[:, columns], ((1,), (0,)))
            store_blocks(target, j, pl.ds(place(step, STEP), STEP), part, n_dp)

        loop(chunk // STEP, outward, few)


def inward_part(i, n_dp, grad_refs, w_gate, w_up, target):
    chunk = target.shape[3]
    few = grad_refs[0].shape[0] <= FEW_ROWS
    for j in range(2):
        first = own_columns(i, j, chunk)

        def inward(step):
            columns = pl.ds(pl.multiple_of(first + step * STEP, STEP), STEP)
            part = 0.0
            for parity, weights in ((0, w_gate), (1, w_up)):
                start = 0
                for ref in grad_refs[parity::2]:
                    part = part + dot(ref[...], weights[columns, start : start + ref.shape[1]], ((1,), (1,)))
                    start += ref.shape[1]
            store_blocks(target, j, pl.ds(place(step, STEP), STEP), part, n_dp)

        loop(chunk // STEP, inward, few)


def gradients(first, weighted, pre_gate, pre_up, w_down, grad_gate, grad_up, few):
    size = unit_step(w_down.shape[0])

    def hidden_units(step):
        columns = pl.ds(place(step, size), size)
        units = pl.ds(first + step * size, size)
        back = dot(weighted[...], w_down[units, :], ((1,), (1,)))
        gate_part, up_part = pre_gate[:, units], pre_up[:, units]
        sig = jax.nn.sigmoid(gate_part)
        grad_gate[:, columns] = (back * up_part * sig * (1.0 + gate_part * (1.0 - sig))).astype(BF16)
        grad_up[:, columns] = (back * gate_part * sig).astype(BF16)

    loop(grad_gate.shape[1] // size, hidden_units, few or grad_gate.shape[1] == size)


def backward_first_kernel(n_dp, *refs):
    grads, smalls = refs[: 2 * n_dp - 1], refs[2 * n_dp - 1 : 3 * n_dp - 1]
    pre_gate, pre_up, w_down, waiting, grad_gate, grad_up, weighted, passed = refs[3 * n_dp - 1 :]
    passed[...] = waiting[...]
    weight = gates_of(smalls)
    few = weighted.shape[0] <= FEW_ROWS

    def weigh(columns, value):
        weighted[:, columns] = (weight * value).astype(BF16)

    both_halves([grads], weighted.shape[1], weigh)
    gradients(0, weighted, pre_gate, pre_up, w_down, grad_gate, grad_up, few)


def backward_rest_kernel(n_dp, weighted, pre_gate, pre_up, w_down, waiting, grad_gate, grad_up, passed):
    passed[...] = waiting[...]
    first = pre_gate.shape[1] - grad_gate.shape[1]
    gradients(first, weighted, pre_gate, pre_up, w_down, grad_gate, grad_up, True)


def inward_kernel(i, n_dp, *refs):
    w_gate, w_up, waiting, target, passed = refs[-5:]
    passed[...] = waiting[...]
    inward_part(i, n_dp, refs[:-5], w_gate, w_up, target)


def join_kernel(n_dp, in_keep, in_other, out_block, *refs):
    for t in range(2 * n_dp):
        k, j = t // 2, t % 2
        refs[t][...] = (in_keep[k, j].astype(F32) + in_other[k, j].astype(F32)).astype(BF16)
    refs[-1][...] = out_block[...]


def finish_kernel(n_dp, *refs):
    count = 2 * n_dp - 1
    hid, grads, smalls = refs[:count], refs[count : 2 * count], refs[2 * count : 2 * count + n_dp]
    refs = refs[2 * count + n_dp :]
    back, moe = refs[: 4 * n_dp], refs[4 * n_dp : 4 * n_dp + 2]
    refs = refs[4 * n_dp + 2 :]
    gain, w_out, targets, held = refs[0], refs[1], refs[2:6], refs[6:10]
    summed, d_all, sems = refs[10:]
    output, d_hidden, d_context, d_w_out = held
    copies = [pltpu.make_async_copy(held[n], targets[n], sems.at[n]) for n in range(4)]
    rows, width = hid[0].shape
    chunk = moe[0].shape[2]
    for i in range(2):
        for j in range(2):
            columns = pl.ds(pl.multiple_of(own_columns(i, j, chunk), chunk), chunk)
            for k in range(n_dp):
                piece = back[(i * n_dp + k) * 2 + j]
                summed[k * rows : (k + 1) * rows, columns] = piece[...].astype(F32) * gain[:, columns]
            output[:, columns] = (hid[0][:, columns].astype(F32) + moe[i][j].astype(F32)).astype(BF16)
    copies[0].start()

    few = rows * n_dp <= FEW_ROWS
    sums = [0.0, 0.0]

    def products(columns, value):
        sums[0] = sums[0] + folded(value * value)
        sums[1] = sums[1] + folded(value * summed[:, columns])

    both_halves([hid], width, products)
    scale = lax.rsqrt(jnp.sum(sums[0], axis=1, keepdims=True) / width + EPSILON)
    centre = scale * jnp.sum(sums[1], axis=1, keepdims=True) / width

    def total(columns, value, grad):
        result = grad + scale * (summed[:, columns] - value * scale * centre)
        d_all[:, columns] = result.astype(BF16)
        d_hidden[:, columns] = result[:rows].astype(BF16)

    both_halves([hid, grads], width, total)
    copies[1].start()
    d_context[...] = dot(d_hidden[...], w_out[...], ((1,), (1,))).astype(BF16)
    part = width // n_dp
    copies[2].start()
    heads = d_context.shape[1]
    lanes = slice(width // 2, width // 2 + heads)
    turned = jnp.concatenate([small[:, lanes].astype(F32) for small in smalls], axis=0).T.astype(BF16)
    step_width = min(part, 512)

    def product(step):
        columns = pl.ds(pl.multiple_of(lax.axis_index("dp") * part + step * step_width, step_width), step_width)
        d_w_out[:, pl.ds(place(step, step_width), step_width)] = dot(
            turned, d_all[:, columns], ((1,), (0,))
        ).astype(BF16)

    loop(part // step_width, product, few)
    copies[3].start()
    for copy in copies:
        copy.wait()


def run(kernel, n_dp, operands, outs, scratch, cost, name, far=(), out_space=pltpu.VMEM):
    spaces = [pltpu.HBM if n in far else pltpu.VMEM for n in range(len(operands))]
    held = [pltpu.with_memory_space_constraint(value, space) for value, space in zip(operands, spaces)]
    kinds = [out_space(shape, kind) for shape, kind in outs]
    return pl.pallas_call(
        functools.partial(kernel, n_dp),
        out_shape=kinds,
        in_specs=[pl.BlockSpec(memory_space=space) for space in spaces],
        out_specs=[pl.BlockSpec(memory_space=out_space)] * len(outs),
        scratch_shapes=scratch,
        compiler_params=pltpu.CompilerParams(vmem_limit_bytes=VMEM_LIMIT if n_dp <= 2 else VMEM_LIMIT_MANY),
        cost_estimate=pl.CostEstimate(flops=0, bytes_accessed=cost, transcendentals=0),
        name=name,
    )(*held)


def per_device(
    hidden_in, norm_gain, route_ids, route_gates, w_gate, w_up, w_down, context, w_out, grad_out
):
    n_dp, n_hi = lax.axis_size("dp"), lax.axis_size("hi")
    rows, width = hidden_in.shape
    top, heads = route_ids.shape[1], context.shape[1]
    all_rows, units, chunk = n_dp * rows, w_gate.shape[2], width // 4

    def swap(value, axes, turn, cross=True):
        count = 2
        for name in axes:
            count *= lax.axis_size(name)
        turn = 2 * turn + (parity(turn) if cross else 0)
        return lax.ppermute(value, axes + ("c",), [(i, i ^ turn) for i in range(count)])

    def other_core(value):
        return lax.ppermute(value, ("c",), [(0, 1), (1, 0)])

    weights = 2 * width * units
    shares = ((n_dp, 2, rows, chunk), BF16)
    wg, wu, wd, gain = w_gate[0], w_up[0], w_down[0], norm_gain.reshape(1, width)
    half = width // 2
    (hid_half,) = run(
        cut_kernel, n_dp, [hidden_in], [((rows, half), BF16)], [pltpu.SemaphoreType.DMA], rows * width, "cut", far=(0,)
    )
    (packed,) = run(
        gates_kernel, n_dp, [route_ids.T, route_gates.T, context, grad_out, wg, wu, wd],
        [((rows, half + heads + LANES), BF16)],
        [pltpu.VMEM((top, rows), jnp.int32), pltpu.VMEM((top, rows), F32), pltpu.SemaphoreType.DMA((4,))],
        4 * weights, "gates", far=range(7),
    )

    def others(value):
        here = [swap(value, ("dp",), k, False) for k in range(1, n_dp)]
        return here, [piece for one in here for piece in (one, other_core(one))]

    hid = [hidden_in] + others(hid_half)[1]
    packs, blocks = others(packed)
    smalls, grads = [packed] + packs, [grad_out] + blocks

    def add(one, other):
        return (one.astype(F32) + other.astype(F32)).astype(BF16)

    def total_of(pieces):
        total = pieces[0].astype(F32)
        for piece in pieces[1:]:
            total = total + piece.astype(F32)
        return total.astype(BF16)

    pre_gate, pre_up, act = run(
        hidden_kernel, n_dp, hid + [gain, wg, wu],
        [((all_rows, units), F32), ((all_rows, units), F32), ((all_rows, units), BF16)],
        [pltpu.VMEM((all_rows, width), BF16)], 2 * weights, "hidden",
    )
    (out_send,) = run(
        functools.partial(outward_kernel, 1), n_dp, smalls + [act, wd], [shares], [],
        weights // 2, "outward_send",
    )
    out_other = other_core(out_send)
    (out_keep,) = run(
        functools.partial(outward_kernel, 0), n_dp, smalls + [act, wd, out_send], [shares], [],
        weights // 2, "outward_keep",
    )
    size = unit_step(units)
    first_units, rest_units = ((all_rows, size), BF16), ((all_rows, units - size), BF16)
    gate_first, up_first, weighted, out_keep = run(
        backward_first_kernel, n_dp, grads + smalls + [pre_gate, pre_up, wd, out_keep],
        [first_units, first_units, ((all_rows, width), BF16), shares], [], weights // 3, "backward_first",
    )
    back_grads = [gate_first, up_first]
    out_half = add(out_keep, out_other)
    out_blocks = [swap(out_half[k], ("dp",), k) for k in range(1, n_dp)]
    block, out_block = (shares[0][1:], BF16), out_half[0]
    if size < units:
        gate_rest, up_rest, out_block = run(
            backward_rest_kernel, n_dp, [weighted, pre_gate, pre_up, wd, out_block],
            [rest_units, rest_units, block], [], weights * 2 // 3, "backward_rest",
        )
        back_grads = back_grads + [gate_rest, up_rest]
    in_send, out_block = run(
        functools.partial(inward_kernel, 1), n_dp, back_grads + [wg, wu, out_block],
        [shares, block], [], weights, "inward_send",
    )
    in_other = other_core(in_send)
    out_block = total_of([out_block] + out_blocks)
    in_keep, out_block = run(
        functools.partial(inward_kernel, 0), n_dp, back_grads + [wg, wu, out_block], [shares, block], [],
        weights, "inward_keep",
    )
    *in_pieces, out_block = run(
        join_kernel, n_dp, [in_keep, in_other, out_block], [((rows, chunk), BF16)] * (2 * n_dp) + [block], [],
        rows * width, "join",
    )
    turns = [t for t in range(2 * n_dp - 1, 0, -1)]
    in_share = total_of([in_pieces[0]] + [swap(in_pieces[t], ("dp", "y"), t) for t in turns])
    out_total = add(out_block, swap(out_block, ("y",), 1)[::-1])
    in_total = total_of([in_share] + [swap(in_share, ("hi",), t) for t in range(1, n_hi)])
    turn = 1
    while turn < n_hi:
        out_total = add(out_total, swap(out_total, ("hi",), turn))
        turn = 2 * turn
    order = [t for t in turns if t < 2] + [t for t in turns if t >= 2]
    spread = {t: swap(in_total, ("dp", "y"), t) for t in order}
    back = [in_total] + [spread[t] for t in range(1, 2 * n_dp)]
    back = back + [other_core(piece) for piece in back]
    moe = [out_total, other_core(out_total)]
    outs = [((rows, width), BF16), ((rows, width), BF16), ((rows, heads), BF16), ((heads, width // n_dp), BF16)]
    return run(
        finish_kernel, n_dp, hid + grads + smalls + back + moe + [gain, w_out], outs,
        [pltpu.VMEM(*out) for out in outs]
        + [pltpu.VMEM((all_rows, width), F32), pltpu.VMEM((all_rows, width), BF16), pltpu.SemaphoreType.DMA((4,))],
        weights, "finish", out_space=pltpu.HBM,
    )


def solution(mesh):
    n_dp, n_e = mesh.shape["dp"], mesh.shape["expert"]
    names = ("dp", "hi", "y", "c")
    mesh = jax.sharding.Mesh(mesh.devices.reshape(n_dp, n_e // 4, 2, 2), names)
    expert = names[1:]
    return jax.shard_map(
        per_device,
        mesh=mesh,
        in_specs=(
            P("dp", None),
            P(),
            P("dp", None),
            P("dp", None),
            P(expert, None, "dp"),
            P(expert, None, "dp"),
            P(expert, "dp", None),
            P("dp", expert),
            P(expert, None),
            P("dp", None),
        ),
        out_specs=(P("dp", None), P("dp", None), P("dp", expert), P(expert, "dp")),
        check_vma=False,
    )
```

```python
import functools

import jax
import jax.numpy as jnp
from jax import lax
from jax.experimental import pallas as pl
from jax.experimental.pallas import tpu as pltpu
from jax.sharding import PartitionSpec as P

EPSILON = 1e-06
F32 = jnp.float32
BF16 = jnp.bfloat16
STEP = 256
LANES = 128
TERMS = 3
PIECES = 2
LOAD_PIECES = 8
FEW_ROWS = 64
VMEM_LIMIT = 12 * 1024 * 1024
VMEM_LIMIT_MANY = 24 * 1024 * 1024


def dot(a, b, dims):
    return lax.dot_general(a, b, (dims, ((), ())), preferred_element_type=F32)


def place(step, count):
    return pl.multiple_of(step * count, count)


def parity(number):
    shift = 1
    while shift < 32:
        number = number ^ (number >> shift)
        shift = 2 * shift
    return number & 1


def own_half():
    chip = lax.axis_index("dp") ^ lax.axis_index("y") ^ lax.axis_index("hi")
    return lax.axis_index("c") ^ parity(chip)


def own_columns(i, j, width):
    return ((lax.axis_index("y") ^ j) * 2 + (own_half() ^ i)) * width


def folded(value):
    return sum(value[:, start : start + LANES] for start in range(0, value.shape[1], LANES))


def both_halves(refs, width, body):
    core, half = lax.axis_index("c"), width // 2
    size = 512 if len(refs[0]) <= 3 else 128
    for h in range(2):
        for step in range(half // size):
            columns = pl.ds(pl.multiple_of((core ^ h) * half + step * size, size), size)

            def rows_at(group):
                first = group[0][:, columns].astype(F32)
                others = [ref[:, step * size : (step + 1) * size].astype(F32) for ref in group[1 + h :: 2]]
                return jnp.concatenate([first] + others, axis=0)

            body(columns, *[rows_at(group) for group in refs])


def store_blocks(out_ref, j, columns, value, count):
    rows = value.shape[0] // count
    for k in range(count):
        out_ref[k, j, :, columns] = value[k * rows : (k + 1) * rows].astype(BF16)


def cut_kernel(n_dp, source, target, sem):
    width = target.shape[1]
    columns = pl.ds(pl.multiple_of(lax.axis_index("c") * width, width), width)
    copy = pltpu.make_async_copy(source.at[:, columns], target, sem)
    copy.start()
    copy.wait()


def gates_kernel(n_dp, named, weights, context, grads, w_gate, w_up, w_down, packed, named_held, weights_held, sems):
    width, heads = grads.shape[1] // 2, context.shape[1]
    columns = pl.ds(pl.multiple_of(lax.axis_index("c") * width, width), width)
    pairs = [
        (named, named_held), (weights, weights_held), (context, packed.at[:, pl.ds(width, heads)]),
        (grads.at[:, columns], packed.at[:, pl.ds(0, width)]),
    ]
    copies = [pltpu.make_async_copy(*pair, sems.at[n]) for n, pair in enumerate(pairs)]
    for copy in copies:
        copy.start()
    copies[0].wait()
    copies[1].wait()
    rows = context.shape[0]
    expert = (lax.axis_index("hi") * 2 + lax.axis_index("y")) * 2 + lax.axis_index("c")
    row = jnp.sum(jnp.where(named_held[...] == expert, weights_held[...], 0.0), axis=0, keepdims=True)
    square = (rows, rows)
    diagonal = lax.broadcasted_iota(jnp.int32, square, 0) == lax.broadcasted_iota(jnp.int32, square, 1)
    gate = jnp.sum(jnp.where(diagonal, row, 0.0), axis=1, keepdims=True)
    lane = lax.broadcasted_iota(jnp.int32, (rows, LANES), 1)
    rest, block = jnp.broadcast_to(gate, (rows, LANES)), jnp.zeros((rows, LANES), F32)
    for term in range(TERMS):
        rounded = rest.astype(BF16).astype(F32)
        block = jnp.where(lane == term, rounded, block)
        rest = rest - rounded
    packed[:, width + heads :] = block.astype(BF16)
    copies[2].wait()
    copies[3].wait()


def unit_step(units):
    return STEP if units % STEP == 0 else units


def loop(count, body, unroll):
    if unroll:
        for step in range(count):
            body(step)
    else:
        def carried(step, carry):
            body(step)
            return carry

        lax.fori_loop(0, count, carried, 0)


def gates_of(packs):
    first = packs[0].shape[1] - LANES
    blocks = [pack[:, first : first + LANES].astype(F32) for pack in packs]
    gates = jnp.concatenate(blocks, axis=0)
    return gates[:, 0:1] + gates[:, 1:2] + gates[:, 2:3]


def half_columns(h, half):
    return pl.multiple_of((lax.axis_index("c") ^ h) * half, half)


def scaled_half(h, own, others, gain, scaled):
    half = scaled.shape[1]
    first, size = half_columns(h, half), 512 if len(others) < 2 else 128
    squares = 0.0
    for start in range(0, half, size):
        columns = pl.ds(pl.multiple_of(first + start, size), size)
        rows = [own[:, columns]] + [other[:, start : start + size] for other in others]
        value = jnp.concatenate([row.astype(F32) for row in rows], axis=0)
        squares = squares + folded(value * value)
        scaled[:, start : start + size] = (value * gain[:, columns]).astype(BF16)
    return squares


def hidden_first_kernel(n_dp, own, *refs):
    others = refs[: n_dp - 1]
    gain, w_gate, w_up, gate_sum, up_sum, square_sum, scaled = refs[n_dp - 1 :]
    half = scaled.shape[1]
    square_sum[...] = scaled_half(0, own, others, gain, scaled)
    size, rows = unit_step(w_gate.shape[1]), pl.ds(half_columns(0, half), half)

    def hidden_units(step):
        columns = pl.ds(place(step, size), size)
        gate_sum[:, columns] = dot(scaled[...], w_gate[rows, columns], ((1,), (0,)))
        up_sum[:, columns] = dot(scaled[...], w_up[rows, columns], ((1,), (0,)))

    loop(w_gate.shape[1] // size, hidden_units, scaled.shape[0] <= FEW_ROWS)


def hidden_rest_kernel(n_dp, own, *refs):
    others = refs[: n_dp - 1]
    gain, w_gate, w_up, gate_sum, up_sum, square_sum, pre_gate, pre_up, act, scales, scaled = refs[n_dp - 1 :]
    half = scaled.shape[1]
    squares = square_sum[...] + scaled_half(1, own, others, gain, scaled)
    scale = lax.rsqrt(jnp.sum(squares, axis=1, keepdims=True) / (2 * half) + EPSILON)
    scales[...] = jnp.broadcast_to(scale, scales.shape)
    size, rows = unit_step(w_gate.shape[1]), pl.ds(half_columns(1, half), half)

    def hidden_units(step):
        columns = pl.ds(place(step, size), size)
        gate_part = scale * (gate_sum[:, columns] + dot(scaled[...], w_gate[rows, columns], ((1,), (0,))))
        up_part = scale * (up_sum[:, columns] + dot(scaled[...], w_up[rows, columns], ((1,), (0,))))
        pre_gate[:, columns] = gate_part
        pre_up[:, columns] = up_part
        act[:, columns] = (gate_part * jax.nn.sigmoid(gate_part) * up_part).astype(BF16)

    loop(w_gate.shape[1] // size, hidden_units, scaled.shape[0] <= FEW_ROWS)


def outward_kernel(i, n_dp, *refs):
    smalls = refs[:n_dp]
    act, w_down, *_, target = refs[n_dp:]
    weight = gates_of(smalls)
    chunk = target.shape[3]
    few = act.shape[0] <= FEW_ROWS
    for j in range(2):
        first = own_columns(i, j, chunk)

        def outward(step):
            columns = pl.ds(pl.multiple_of(first + step * STEP, STEP), STEP)
            part = weight * dot(act[...], w_down[:, columns], ((1,), (0,)))
            store_blocks(target, j, pl.ds(place(step, STEP), STEP), part, n_dp)

        loop(chunk // STEP, outward, few)


def inward_part(i, n_dp, grad_refs, w_gate, w_up, target):
    chunk = target.shape[3]
    few = grad_refs[0].shape[0] <= FEW_ROWS
    for j in range(2):
        first = own_columns(i, j, chunk)

        def inward(step):
            columns = pl.ds(pl.multiple_of(first + step * STEP, STEP), STEP)
            part = 0.0
            for parity, weights in ((0, w_gate), (1, w_up)):
                start = 0
                for ref in grad_refs[parity::2]:
                    part = part + dot(ref[...], weights[columns, start : start + ref.shape[1]], ((1,), (1,)))
                    start += ref.shape[1]
            store_blocks(target, j, pl.ds(place(step, STEP), STEP), part, n_dp)

        loop(chunk // STEP, inward, few)


def gradients(first, weighted, pre_gate, pre_up, w_down, grad_gate, grad_up, few):
    size = unit_step(w_down.shape[0])

    def hidden_units(step):
        columns = pl.ds(place(step, size), size)
        units = pl.ds(first + step * size, size)
        back = dot(weighted[...], w_down[units, :], ((1,), (1,)))
        gate_part, up_part = pre_gate[:, units], pre_up[:, units]
        sig = jax.nn.sigmoid(gate_part)
        grad_gate[:, columns] = (back * up_part * sig * (1.0 + gate_part * (1.0 - sig))).astype(BF16)
        grad_up[:, columns] = (back * gate_part * sig).astype(BF16)

    loop(grad_gate.shape[1] // size, hidden_units, few or grad_gate.shape[1] == size)


def backward_first_kernel(n_dp, *refs):
    grads, smalls = refs[: 2 * n_dp - 1], refs[2 * n_dp - 1 : 3 * n_dp - 1]
    pre_gate, pre_up, w_down, waiting, grad_gate, grad_up, weighted, passed = refs[3 * n_dp - 1 :]
    passed[...] = waiting[...]
    weight = gates_of(smalls)
    few = weighted.shape[0] <= FEW_ROWS

    def weigh(columns, value):
        weighted[:, columns] = (weight * value).astype(BF16)

    both_halves([grads], weighted.shape[1], weigh)
    gradients(0, weighted, pre_gate, pre_up, w_down, grad_gate, grad_up, few)


def backward_rest_kernel(n_dp, weighted, pre_gate, pre_up, w_down, waiting, grad_gate, grad_up, passed):
    passed[...] = waiting[...]
    first = pre_gate.shape[1] - grad_gate.shape[1]
    gradients(first, weighted, pre_gate, pre_up, w_down, grad_gate, grad_up, True)


def inward_kernel(i, n_dp, *refs):
    w_gate, w_up, waiting, target, passed = refs[-5:]
    passed[...] = waiting[...]
    inward_part(i, n_dp, refs[:-5], w_gate, w_up, target)


def join_kernel(n_dp, in_keep, in_other, out_block, *refs):
    for t in range(2 * n_dp):
        k, j = t // 2, t % 2
        refs[t][...] = (in_keep[k, j].astype(F32) + in_other[k, j].astype(F32)).astype(BF16)
    refs[-1][...] = out_block[...]


def finish_kernel(n_dp, *refs):
    count = 2 * n_dp - 1
    hid, grads, smalls = refs[:count], refs[count : 2 * count], refs[2 * count : 2 * count + n_dp]
    refs = refs[2 * count + n_dp :]
    back, moe = refs[: 4 * n_dp], refs[4 * n_dp : 4 * n_dp + 2]
    refs = refs[4 * n_dp + 2 :]
    gain, scales, w_out, targets, held = refs[0], refs[1], refs[2], refs[3:7], refs[7:11]
    summed, d_all, sems = refs[11:]
    output, d_hidden, d_context, d_w_out = held
    copies = [pltpu.make_async_copy(held[n], targets[n], sems.at[n]) for n in range(3)]
    size = d_w_out.shape[1] // PIECES
    for piece in range(PIECES):
        block = (slice(None), pl.ds(piece * size, size))
        copies.append(pltpu.make_async_copy(d_w_out.at[block], targets[3].at[block], sems.at[3 + piece]))
    rows, width = hid[0].shape
    chunk = moe[0].shape[2]
    for i in range(2):
        for j in range(2):
            columns = pl.ds(pl.multiple_of(own_columns(i, j, chunk), chunk), chunk)
            for k in range(n_dp):
                piece = back[(i * n_dp + k) * 2 + j]
                summed[k * rows : (k + 1) * rows, columns] = piece[...].astype(F32) * gain[:, columns]
            output[:, columns] = (hid[0][:, columns].astype(F32) + moe[i][j].astype(F32)).astype(BF16)
    copies[0].start()

    few = rows * n_dp <= FEW_ROWS
    sums = [0.0]

    def products(columns, value):
        sums[0] = sums[0] + folded(value * summed[:, columns])

    both_halves([hid], width, products)
    scale = scales[:, :1]
    centre = scale * jnp.sum(sums[0], axis=1, keepdims=True) / width

    def total(columns, value, grad):
        result = grad + scale * (summed[:, columns] - value * scale * centre)
        d_all[:, columns] = result.astype(BF16)
        d_hidden[:, columns] = result[:rows].astype(BF16)

    both_halves([hid, grads], width, total)
    copies[1].start()
    heads = d_context.shape[1]
    part = width // n_dp
    lanes = slice(width // 2, width // 2 + heads)
    turned = jnp.concatenate([small[:, lanes].astype(F32) for small in smalls], axis=0).T.astype(BF16)
    size = part // PIECES
    for piece in range(PIECES):
        columns = pl.ds(pl.multiple_of(lax.axis_index("dp") * part + piece * size, LANES), size)
        block = pl.ds(piece * size, size)
        d_w_out[:, block] = dot(turned, d_all[:, columns], ((1,), (0,))).astype(BF16)
        copies[3 + piece].start()
    d_context[...] = dot(d_hidden[...], w_out[...], ((1,), (1,))).astype(BF16)
    copies[2].start()
    for copy in copies:
        copy.wait()


def run(kernel, n_dp, operands, outs, scratch, cost, name, far=(), out_space=pltpu.VMEM):
    spaces = [pltpu.HBM if n in far else pltpu.VMEM for n in range(len(operands))]
    held = [pltpu.with_memory_space_constraint(value, space) for value, space in zip(operands, spaces)]
    kinds = [out_space(shape, kind) for shape, kind in outs]
    return pl.pallas_call(
        functools.partial(kernel, n_dp),
        out_shape=kinds,
        in_specs=[pl.BlockSpec(memory_space=space) for space in spaces],
        out_specs=[pl.BlockSpec(memory_space=out_space)] * len(outs),
        scratch_shapes=scratch,
        compiler_params=pltpu.CompilerParams(vmem_limit_bytes=VMEM_LIMIT if n_dp <= 2 else VMEM_LIMIT_MANY),
        cost_estimate=pl.CostEstimate(flops=0, bytes_accessed=cost, transcendentals=0),
        name=name,
    )(*held)


def per_device(
    hidden_in, norm_gain, route_ids, route_gates, w_gate, w_up, w_down, context, w_out, grad_out
):
    n_dp, n_hi = lax.axis_size("dp"), lax.axis_size("hi")
    rows, width = hidden_in.shape
    top, heads = route_ids.shape[1], context.shape[1]
    all_rows, units, chunk = n_dp * rows, w_gate.shape[2], width // 4

    def swap(value, axes, turn, cross=True):
        count = 2
        for name in axes:
            count *= lax.axis_size(name)
        turn = 2 * turn + (parity(turn) if cross else 0)
        return lax.ppermute(value, axes + ("c",), [(i, i ^ turn) for i in range(count)])

    def other_core(value):
        return lax.ppermute(value, ("c",), [(0, 1), (1, 0)])

    weights = 2 * width * units
    shares = ((n_dp, 2, rows, chunk), BF16)
    wg, wu, wd, gain = w_gate[0], w_up[0], w_down[0], norm_gain.reshape(1, width)
    half = width // 2
    (hid_half,) = run(
        cut_kernel, n_dp, [hidden_in], [((rows, half), BF16)], [pltpu.SemaphoreType.DMA], rows * width, "cut", far=(0,)
    )
    (packed,) = run(
        gates_kernel, n_dp, [route_ids.T, route_gates.T, context, grad_out, wg, wu, wd],
        [((rows, half + heads + LANES), BF16)],
        [pltpu.VMEM((top, rows), jnp.int32), pltpu.VMEM((top, rows), F32), pltpu.SemaphoreType.DMA((4,))],
        4 * weights, "gates", far=range(7),
    )

    def others(value):
        here = [swap(value, ("dp",), k, False) for k in range(1, n_dp)]
        return here, [piece for one in here for piece in (one, other_core(one))]

    hid = [hidden_in] + others(hid_half)[1]
    packs, blocks = others(packed)
    smalls, grads = [packed] + packs, [grad_out] + blocks

    def add(one, other):
        return (one.astype(F32) + other.astype(F32)).astype(BF16)

    def total_of(pieces):
        total = pieces[0].astype(F32)
        for piece in pieces[1:]:
            total = total + piece.astype(F32)
        return total.astype(BF16)

    hidden_units, row_block = ((all_rows, units), F32), ((all_rows, LANES), F32)
    scaled = pltpu.VMEM((all_rows, half), BF16)
    gate_sum, up_sum, square_sum = run(
        hidden_first_kernel, n_dp, [hidden_in] + hid[1::2] + [gain, wg, wu],
        [hidden_units, hidden_units, row_block], [scaled], weights, "hidden_first",
    )
    pre_gate, pre_up, act, scales = run(
        hidden_rest_kernel, n_dp, [hidden_in] + hid[2::2] + [gain, wg, wu, gate_sum, up_sum, square_sum],
        [hidden_units, hidden_units, ((all_rows, units), BF16), row_block], [scaled], weights, "hidden_rest",
    )
    (out_send,) = run(
        functools.partial(outward_kernel, 1), n_dp, smalls + [act, wd], [shares], [],
        weights // 2, "outward_send",
    )
    out_other = other_core(out_send)
    (out_keep,) = run(
        functools.partial(outward_kernel, 0), n_dp, smalls + [act, wd, out_send], [shares], [],
        weights // 2, "outward_keep",
    )
    size = unit_step(units)
    first_units, rest_units = ((all_rows, size), BF16), ((all_rows, units - size), BF16)
    gate_first, up_first, weighted, out_keep = run(
        backward_first_kernel, n_dp, grads + smalls + [pre_gate, pre_up, wd, out_keep],
        [first_units, first_units, ((all_rows, width), BF16), shares], [], weights // 3, "backward_first",
    )
    back_grads = [gate_first, up_first]
    out_half = add(out_keep, out_other)
    out_blocks = [swap(out_half[k], ("dp",), k) for k in range(1, n_dp)]
    block, out_block = (shares[0][1:], BF16), out_half[0]
    if size < units:
        gate_rest, up_rest, out_block = run(
            backward_rest_kernel, n_dp, [weighted, pre_gate, pre_up, wd, out_block],
            [rest_units, rest_units, block], [], weights * 2 // 3, "backward_rest",
        )
        back_grads = back_grads + [gate_rest, up_rest]
    in_send, out_block = run(
        functools.partial(inward_kernel, 1), n_dp, back_grads + [wg, wu, out_block],
        [shares, block], [], weights, "inward_send",
    )
    in_other = other_core(in_send)
    out_block = total_of([out_block] + out_blocks)
    in_keep, out_block = run(
        functools.partial(inward_kernel, 0), n_dp, back_grads + [wg, wu, out_block], [shares, block], [],
        weights, "inward_keep",
    )
    *in_pieces, out_block = run(
        join_kernel, n_dp, [in_keep, in_other, out_block], [((rows, chunk), BF16)] * (2 * n_dp) + [block], [],
        rows * width, "join",
    )
    turns = [t for t in range(2 * n_dp - 1, 0, -1)]
    in_share = total_of([in_pieces[0]] + [swap(in_pieces[t], ("dp", "y"), t) for t in turns])
    out_total = add(out_block, swap(out_block, ("y",), 1)[::-1])
    in_total = total_of([in_share] + [swap(in_share, ("hi",), t) for t in range(1, n_hi)])
    turn = 1
    while turn < n_hi:
        out_total = add(out_total, swap(out_total, ("hi",), turn))
        turn = 2 * turn
    order = [t for t in turns if t < 2] + [t for t in turns if t >= 2]
    spread = {t: swap(in_total, ("dp", "y"), t) for t in order}
    back = [in_total] + [spread[t] for t in range(1, 2 * n_dp)]
    back = back + [other_core(piece) for piece in back]
    moe = [out_total, other_core(out_total)]
    outs = [((rows, width), BF16), ((rows, width), BF16), ((rows, heads), BF16), ((heads, width // n_dp), BF16)]
    return run(
        finish_kernel, n_dp, hid + grads + smalls + back + moe + [gain, scales, w_out], outs,
        [pltpu.VMEM(*out) for out in outs]
        + [pltpu.VMEM((all_rows, width), F32), pltpu.VMEM((all_rows, width), BF16), pltpu.SemaphoreType.DMA((3 + PIECES,))],
        weights, "finish", out_space=pltpu.HBM,
    )


def solution(mesh):
    n_dp, n_e = mesh.shape["dp"], mesh.shape["expert"]
    names = ("dp", "hi", "y", "c")
    mesh = jax.sharding.Mesh(mesh.devices.reshape(n_dp, n_e // 4, 2, 2), names)
    expert = names[1:]
    return jax.shard_map(
        per_device,
        mesh=mesh,
        in_specs=(
            P("dp", None),
            P(),
            P("dp", None),
            P("dp", None),
            P(expert, None, "dp"),
            P(expert, None, "dp"),
            P(expert, "dp", None),
            P("dp", expert),
            P(expert, None),
            P("dp", None),
        ),
        out_specs=(P("dp", None), P("dp", None), P("dp", expert), P(expert, "dp")),
        check_vma=False,
    )
```

```python
import functools

import jax
import jax.numpy as jnp
from jax import lax
from jax.experimental import pallas as pl
from jax.experimental.pallas import tpu as pltpu
from jax.sharding import PartitionSpec as P

EPSILON = 1e-06
F32 = jnp.float32
BF16 = jnp.bfloat16
STEP = 256
LANES = 128
TERMS = 3
PIECES = 2
LOAD_PIECES = 8
FEW_ROWS = 64
VMEM_LIMIT = 12 * 1024 * 1024
VMEM_LIMIT_MANY = 24 * 1024 * 1024


def dot(a, b, dims):
    return lax.dot_general(a, b, (dims, ((), ())), preferred_element_type=F32)


def place(step, count):
    return pl.multiple_of(step * count, count)


def parity(number):
    shift = 1
    while shift < 32:
        number = number ^ (number >> shift)
        shift = 2 * shift
    return number & 1


def own_half():
    chip = lax.axis_index("dp") ^ lax.axis_index("y") ^ lax.axis_index("hi")
    return lax.axis_index("c") ^ parity(chip)


def own_columns(i, j, width):
    return ((lax.axis_index("y") ^ j) * 2 + (own_half() ^ i)) * width


def folded(value):
    return sum(value[:, start : start + LANES] for start in range(0, value.shape[1], LANES))


def both_halves(refs, width, body):
    core, half = lax.axis_index("c"), width // 2
    size = 512 if len(refs[0]) <= 3 else 128
    for h in range(2):
        for step in range(half // size):
            columns = pl.ds(pl.multiple_of((core ^ h) * half + step * size, size), size)

            def rows_at(group):
                first = group[0][:, columns].astype(F32)
                others = [ref[:, step * size : (step + 1) * size].astype(F32) for ref in group[1 + h :: 2]]
                return jnp.concatenate([first] + others, axis=0)

            body(columns, *[rows_at(group) for group in refs])


def store_blocks(out_ref, j, columns, value, count):
    rows = value.shape[0] // count
    for k in range(count):
        out_ref[k, j, :, columns] = value[k * rows : (k + 1) * rows].astype(BF16)


def cut_kernel(n_dp, source, target, sem):
    width = target.shape[1]
    columns = pl.ds(pl.multiple_of(lax.axis_index("c") * width, width), width)
    copy = pltpu.make_async_copy(source.at[:, columns], target, sem)
    copy.start()
    copy.wait()


def gates_kernel(n_dp, named, weights, context, grads, w_gate, w_up, w_down, packed, named_held, weights_held, sems):
    width, heads = grads.shape[1] // 2, context.shape[1]
    columns = pl.ds(pl.multiple_of(lax.axis_index("c") * width, width), width)
    pairs = [
        (named, named_held), (weights, weights_held), (context, packed.at[:, pl.ds(width, heads)]),
        (grads.at[:, columns], packed.at[:, pl.ds(0, width)]),
    ]
    copies = [pltpu.make_async_copy(*pair, sems.at[n]) for n, pair in enumerate(pairs)]
    for copy in copies:
        copy.start()
    copies[0].wait()
    copies[1].wait()
    rows = context.shape[0]
    expert = (lax.axis_index("hi") * 2 + lax.axis_index("y")) * 2 + lax.axis_index("c")
    row = jnp.sum(jnp.where(named_held[...] == expert, weights_held[...], 0.0), axis=0, keepdims=True)
    square = (rows, rows)
    diagonal = lax.broadcasted_iota(jnp.int32, square, 0) == lax.broadcasted_iota(jnp.int32, square, 1)
    gate = jnp.sum(jnp.where(diagonal, row, 0.0), axis=1, keepdims=True)
    lane = lax.broadcasted_iota(jnp.int32, (rows, LANES), 1)
    rest, block = jnp.broadcast_to(gate, (rows, LANES)), jnp.zeros((rows, LANES), F32)
    for term in range(TERMS):
        rounded = rest.astype(BF16).astype(F32)
        block = jnp.where(lane == term, rounded, block)
        rest = rest - rounded
    packed[:, width + heads :] = block.astype(BF16)
    copies[2].wait()
    copies[3].wait()


def unit_step(units):
    return STEP if units % STEP == 0 else units


def loop(count, body, unroll):
    if unroll:
        for step in range(count):
            body(step)
    else:
        def carried(step, carry):
            body(step)
            return carry

        lax.fori_loop(0, count, carried, 0)


def gates_of(packs):
    first = packs[0].shape[1] - LANES
    blocks = [pack[:, first : first + LANES].astype(F32) for pack in packs]
    gates = jnp.concatenate(blocks, axis=0)
    return gates[:, 0:1] + gates[:, 1:2] + gates[:, 2:3]


def half_columns(h, half):
    return pl.multiple_of((lax.axis_index("c") ^ h) * half, half)


def scaled_half(h, own, others, gain, scaled):
    half = scaled.shape[1]
    first, size = half_columns(h, half), 512 if len(others) < 2 else 128
    squares = 0.0
    for start in range(0, half, size):
        columns = pl.ds(pl.multiple_of(first + start, size), size)
        rows = [own[:, columns]] + [other[:, start : start + size] for other in others]
        value = jnp.concatenate([row.astype(F32) for row in rows], axis=0)
        squares = squares + folded(value * value)
        scaled[:, start : start + size] = (value * gain[:, columns]).astype(BF16)
    return squares


def hidden_first_kernel(n_dp, own, *refs):
    others = refs[: n_dp - 1]
    gain, w_gate, w_up, gate_sum, up_sum, square_sum, scaled = refs[n_dp - 1 :]
    half = scaled.shape[1]
    square_sum[...] = scaled_half(0, own, others, gain, scaled)
    size, rows = unit_step(w_gate.shape[1]), pl.ds(half_columns(0, half), half)

    def hidden_units(step):
        columns = pl.ds(place(step, size), size)
        gate_sum[:, columns] = dot(scaled[...], w_gate[rows, columns], ((1,), (0,)))
        up_sum[:, columns] = dot(scaled[...], w_up[rows, columns], ((1,), (0,)))

    loop(w_gate.shape[1] // size, hidden_units, scaled.shape[0] <= FEW_ROWS)


def hidden_rest_kernel(n_dp, own, *refs):
    others = refs[: n_dp - 1]
    gain, w_gate, w_up, gate_sum, up_sum, square_sum, pre_gate, pre_up, act, scales, scaled = refs[n_dp - 1 :]
    half = scaled.shape[1]
    squares = square_sum[...] + scaled_half(1, own, others, gain, scaled)
    scale = lax.rsqrt(jnp.sum(squares, axis=1, keepdims=True) / (2 * half) + EPSILON)
    scales[...] = jnp.broadcast_to(scale, scales.shape)
    size, rows = unit_step(w_gate.shape[1]), pl.ds(half_columns(1, half), half)

    def hidden_units(step):
        columns = pl.ds(place(step, size), size)
        gate_part = scale * (gate_sum[:, columns] + dot(scaled[...], w_gate[rows, columns], ((1,), (0,))))
        up_part = scale * (up_sum[:, columns] + dot(scaled[...], w_up[rows, columns], ((1,), (0,))))
        pre_gate[:, columns] = gate_part
        pre_up[:, columns] = up_part
        act[:, columns] = (gate_part * jax.nn.sigmoid(gate_part) * up_part).astype(BF16)

    loop(w_gate.shape[1] // size, hidden_units, scaled.shape[0] <= FEW_ROWS)


def outward_kernel(i, n_dp, *refs):
    smalls = refs[:n_dp]
    act, w_down, *_, target = refs[n_dp:]
    weight = gates_of(smalls)
    chunk = target.shape[3]
    few = act.shape[0] <= FEW_ROWS
    for j in range(2):
        first = own_columns(i, j, chunk)

        def outward(step):
            columns = pl.ds(pl.multiple_of(first + step * STEP, STEP), STEP)
            part = weight * dot(act[...], w_down[:, columns], ((1,), (0,)))
            store_blocks(target, j, pl.ds(place(step, STEP), STEP), part, n_dp)

        loop(chunk // STEP, outward, few)


def inward_part(i, n_dp, grad_refs, w_gate, w_up, target):
    chunk = target.shape[3]
    few = grad_refs[0].shape[0] <= FEW_ROWS
    for j in range(2):
        first = own_columns(i, j, chunk)

        def inward(step):
            columns = pl.ds(pl.multiple_of(first + step * STEP, STEP), STEP)
            part = 0.0
            for parity, weights in ((0, w_gate), (1, w_up)):
                start = 0
                for ref in grad_refs[parity::2]:
                    part = part + dot(ref[...], weights[columns, start : start + ref.shape[1]], ((1,), (1,)))
                    start += ref.shape[1]
            store_blocks(target, j, pl.ds(place(step, STEP), STEP), part, n_dp)

        loop(chunk // STEP, inward, few)


def gradients(first, weighted, pre_gate, pre_up, w_down, grad_gate, grad_up, few):
    size = unit_step(w_down.shape[0])

    def hidden_units(step):
        columns = pl.ds(place(step, size), size)
        units = pl.ds(first + step * size, size)
        back = dot(weighted[...], w_down[units, :], ((1,), (1,)))
        gate_part, up_part = pre_gate[:, units], pre_up[:, units]
        sig = jax.nn.sigmoid(gate_part)
        grad_gate[:, columns] = (back * up_part * sig * (1.0 + gate_part * (1.0 - sig))).astype(BF16)
        grad_up[:, columns] = (back * gate_part * sig).astype(BF16)

    loop(grad_gate.shape[1] // size, hidden_units, few or grad_gate.shape[1] == size)


def backward_first_kernel(n_dp, *refs):
    grads, smalls = refs[: 2 * n_dp - 1], refs[2 * n_dp - 1 : 3 * n_dp - 1]
    pre_gate, pre_up, w_down, waiting, grad_gate, grad_up, weighted, passed = refs[3 * n_dp - 1 :]
    passed[...] = waiting[...]
    weight = gates_of(smalls)
    few = weighted.shape[0] <= FEW_ROWS

    def weigh(columns, value):
        weighted[:, columns] = (weight * value).astype(BF16)

    both_halves([grads], weighted.shape[1], weigh)
    gradients(0, weighted, pre_gate, pre_up, w_down, grad_gate, grad_up, few)


def backward_rest_kernel(n_dp, weighted, pre_gate, pre_up, w_down, waiting, grad_gate, grad_up, passed):
    passed[...] = waiting[...]
    first = pre_gate.shape[1] - grad_gate.shape[1]
    gradients(first, weighted, pre_gate, pre_up, w_down, grad_gate, grad_up, True)


def inward_kernel(i, n_dp, *refs):
    w_gate, w_up, waiting, target, passed = refs[-5:]
    passed[...] = waiting[...]
    inward_part(i, n_dp, refs[:-5], w_gate, w_up, target)


def join_kernel(n_dp, in_keep, in_other, out_block, *refs):
    for t in range(2 * n_dp):
        k, j = t // 2, t % 2
        total = (in_keep[k, j].astype(F32) + in_other[k, j].astype(F32)).astype(BF16)
        if t == 1:
            refs[t][0] = total
        else:
            refs[t][...] = total
    for j in range(2):
        refs[1][1 + j] = out_block[j]
    refs[-1][...] = out_block[...]


def flip_add_kernel(n_dp, own, arrived, target):
    for j in range(2):
        target[j] = (own[j].astype(F32) + arrived[2 - j].astype(F32)).astype(BF16)


def finish_kernel(n_dp, *refs):
    count = 2 * n_dp - 1
    hid, grads, smalls = refs[:count], refs[count : 2 * count], refs[2 * count : 2 * count + n_dp]
    refs = refs[2 * count + n_dp :]
    back, moe = refs[: 4 * n_dp], refs[4 * n_dp : 4 * n_dp + 2]
    refs = refs[4 * n_dp + 2 :]
    gain, scales, w_out, targets, held = refs[0], refs[1], refs[2], refs[3:7], refs[7:11]
    summed, d_all, sems = refs[11:]
    output, d_hidden, d_context, d_w_out = held
    copies = [pltpu.make_async_copy(held[n], targets[n], sems.at[n]) for n in range(3)]
    size = d_w_out.shape[1] // PIECES
    for piece in range(PIECES):
        block = (slice(None), pl.ds(piece * size, size))
        copies.append(pltpu.make_async_copy(d_w_out.at[block], targets[3].at[block], sems.at[3 + piece]))
    rows, width = hid[0].shape
    chunk = moe[0].shape[2]
    for i in range(2):
        for j in range(2):
            columns = pl.ds(pl.multiple_of(own_columns(i, j, chunk), chunk), chunk)
            for k in range(n_dp):
                piece = back[(i * n_dp + k) * 2 + j]
                summed[k * rows : (k + 1) * rows, columns] = piece[...].astype(F32) * gain[:, columns]
            output[:, columns] = (hid[0][:, columns].astype(F32) + moe[i][j].astype(F32)).astype(BF16)
    copies[0].start()

    few = rows * n_dp <= FEW_ROWS
    sums = [0.0]

    def products(columns, value):
        sums[0] = sums[0] + folded(value * summed[:, columns])

    both_halves([hid], width, products)
    scale = scales[:, :1]
    centre = scale * jnp.sum(sums[0], axis=1, keepdims=True) / width

    def total(columns, value, grad):
        result = grad + scale * (summed[:, columns] - value * scale * centre)
        d_all[:, columns] = result.astype(BF16)
        d_hidden[:, columns] = result[:rows].astype(BF16)

    both_halves([hid, grads], width, total)
    copies[1].start()
    heads = d_context.shape[1]
    part = width // n_dp
    lanes = slice(width // 2, width // 2 + heads)
    turned = jnp.concatenate([small[:, lanes].astype(F32) for small in smalls], axis=0).T.astype(BF16)
    size = part // PIECES
    for piece in range(PIECES):
        columns = pl.ds(pl.multiple_of(lax.axis_index("dp") * part + piece * size, LANES), size)
        block = pl.ds(piece * size, size)
        d_w_out[:, block] = dot(turned, d_all[:, columns], ((1,), (0,))).astype(BF16)
        copies[3 + piece].start()
    d_context[...] = dot(d_hidden[...], w_out[...], ((1,), (1,))).astype(BF16)
    copies[2].start()
    for copy in copies:
        copy.wait()


def run(kernel, n_dp, operands, outs, scratch, cost, name, far=(), out_space=pltpu.VMEM):
    spaces = [pltpu.HBM if n in far else pltpu.VMEM for n in range(len(operands))]
    held = [pltpu.with_memory_space_constraint(value, space) for value, space in zip(operands, spaces)]
    kinds = [out_space(shape, kind) for shape, kind in outs]
    return pl.pallas_call(
        functools.partial(kernel, n_dp),
        out_shape=kinds,
        in_specs=[pl.BlockSpec(memory_space=space) for space in spaces],
        out_specs=[pl.BlockSpec(memory_space=out_space)] * len(outs),
        scratch_shapes=scratch,
        compiler_params=pltpu.CompilerParams(vmem_limit_bytes=VMEM_LIMIT if n_dp <= 2 else VMEM_LIMIT_MANY),
        cost_estimate=pl.CostEstimate(flops=0, bytes_accessed=cost, transcendentals=0),
        name=name,
    )(*held)


def per_device(
    hidden_in, norm_gain, route_ids, route_gates, w_gate, w_up, w_down, context, w_out, grad_out
):
    n_dp, n_hi = lax.axis_size("dp"), lax.axis_size("hi")
    rows, width = hidden_in.shape
    top, heads = route_ids.shape[1], context.shape[1]
    all_rows, units, chunk = n_dp * rows, w_gate.shape[2], width // 4

    def swap(value, axes, turn, cross=True):
        count = 2
        for name in axes:
            count *= lax.axis_size(name)
        turn = 2 * turn + (parity(turn) if cross else 0)
        return lax.ppermute(value, axes + ("c",), [(i, i ^ turn) for i in range(count)])

    def other_core(value):
        return lax.ppermute(value, ("c",), [(0, 1), (1, 0)])

    weights = 2 * width * units
    shares = ((n_dp, 2, rows, chunk), BF16)
    wg, wu, wd, gain = w_gate[0], w_up[0], w_down[0], norm_gain.reshape(1, width)
    half = width // 2
    (hid_half,) = run(
        cut_kernel, n_dp, [hidden_in], [((rows, half), BF16)], [pltpu.SemaphoreType.DMA], rows * width, "cut", far=(0,)
    )
    (packed,) = run(
        gates_kernel, n_dp, [route_ids.T, route_gates.T, context, grad_out, wg, wu, wd],
        [((rows, half + heads + LANES), BF16)],
        [pltpu.VMEM((top, rows), jnp.int32), pltpu.VMEM((top, rows), F32), pltpu.SemaphoreType.DMA((4,))],
        4 * weights, "gates", far=range(7),
    )

    def others(value):
        here = [swap(value, ("dp",), k, False) for k in range(1, n_dp)]
        return here, [piece for one in here for piece in (one, other_core(one))]

    hid = [hidden_in] + others(hid_half)[1]
    packs, blocks = others(packed)
    smalls, grads = [packed] + packs, [grad_out] + blocks

    def add(one, other):
        return (one.astype(F32) + other.astype(F32)).astype(BF16)

    def total_of(pieces):
        total = pieces[0].astype(F32)
        for piece in pieces[1:]:
            total = total + piece.astype(F32)
        return total.astype(BF16)

    hidden_units, row_block = ((all_rows, units), F32), ((all_rows, LANES), F32)
    scaled = pltpu.VMEM((all_rows, half), BF16)
    gate_sum, up_sum, square_sum = run(
        hidden_first_kernel, n_dp, [hidden_in] + hid[1::2] + [gain, wg, wu],
        [hidden_units, hidden_units, row_block], [scaled], weights, "hidden_first",
    )
    pre_gate, pre_up, act, scales = run(
        hidden_rest_kernel, n_dp, [hidden_in] + hid[2::2] + [gain, wg, wu, gate_sum, up_sum, square_sum],
        [hidden_units, hidden_units, ((all_rows, units), BF16), row_block], [scaled], weights, "hidden_rest",
    )
    (out_send,) = run(
        functools.partial(outward_kernel, 1), n_dp, smalls + [act, wd], [shares], [],
        weights // 2, "outward_send",
    )
    out_other = other_core(out_send)
    (out_keep,) = run(
        functools.partial(outward_kernel, 0), n_dp, smalls + [act, wd, out_send], [shares], [],
        weights // 2, "outward_keep",
    )
    size = unit_step(units)
    first_units, rest_units = ((all_rows, size), BF16), ((all_rows, units - size), BF16)
    gate_first, up_first, weighted, out_keep = run(
        backward_first_kernel, n_dp, grads + smalls + [pre_gate, pre_up, wd, out_keep],
        [first_units, first_units, ((all_rows, width), BF16), shares], [], weights // 3, "backward_first",
    )
    back_grads = [gate_first, up_first]
    out_half = add(out_keep, out_other)
    out_blocks = [swap(out_half[k], ("dp",), k) for k in range(1, n_dp)]
    block, out_block = (shares[0][1:], BF16), out_half[0]
    if size < units:
        gate_rest, up_rest, out_block = run(
            backward_rest_kernel, n_dp, [weighted, pre_gate, pre_up, wd, out_block],
            [rest_units, rest_units, block], [], weights * 2 // 3, "backward_rest",
        )
        back_grads = back_grads + [gate_rest, up_rest]
    in_send, out_block = run(
        functools.partial(inward_kernel, 1), n_dp, back_grads + [wg, wu, out_block],
        [shares, block], [], weights, "inward_send",
    )
    in_other = other_core(in_send)
    out_block = total_of([out_block] + out_blocks)
    in_keep, out_block = run(
        functools.partial(inward_kernel, 0), n_dp, back_grads + [wg, wu, out_block], [shares, block], [],
        weights, "inward_keep",
    )
    piece, three = ((rows, chunk), BF16), ((3, rows, chunk), BF16)
    *in_pieces, out_block = run(
        join_kernel, n_dp, [in_keep, in_other, out_block],
        [three if t == 1 else piece for t in range(2 * n_dp)] + [block], [], rows * width, "join",
    )
    turns = [t for t in range(2 * n_dp - 1, 0, -1)]
    arrived = {t: swap(in_pieces[t], ("dp", "y"), t) for t in turns[::-1]}
    (out_total,) = run(flip_add_kernel, n_dp, [out_block, arrived[1]], [block], [], rows * width, "flip_add")
    in_share = total_of([in_pieces[0], arrived[1][0]] + [arrived[t] for t in turns[:-1]])
    in_total = total_of([in_share] + [swap(in_share, ("hi",), t) for t in range(1, n_hi)])
    turn = 1
    while turn < n_hi:
        out_total = add(out_total, swap(out_total, ("hi",), turn))
        turn = 2 * turn
    order = [t for t in turns if t < 2] + [t for t in turns if t >= 2]
    spread = {t: swap(in_total, ("dp", "y"), t) for t in order}
    back = [in_total] + [spread[t] for t in range(1, 2 * n_dp)]
    back = back + [other_core(piece) for piece in back]
    moe = [out_total, other_core(out_total)]
    outs = [((rows, width), BF16), ((rows, width), BF16), ((rows, heads), BF16), ((heads, width // n_dp), BF16)]
    return run(
        finish_kernel, n_dp, hid + grads + smalls + back + moe + [gain, scales, w_out], outs,
        [pltpu.VMEM(*out) for out in outs]
        + [pltpu.VMEM((all_rows, width), F32), pltpu.VMEM((all_rows, width), BF16), pltpu.SemaphoreType.DMA((3 + PIECES,))],
        weights, "finish", out_space=pltpu.HBM,
    )


def solution(mesh):
    n_dp, n_e = mesh.shape["dp"], mesh.shape["expert"]
    names = ("dp", "hi", "y", "c")
    mesh = jax.sharding.Mesh(mesh.devices.reshape(n_dp, n_e // 4, 2, 2), names)
    expert = names[1:]
    return jax.shard_map(
        per_device,
        mesh=mesh,
        in_specs=(
            P("dp", None),
            P(),
            P("dp", None),
            P("dp", None),
            P(expert, None, "dp"),
            P(expert, None, "dp"),
            P(expert, "dp", None),
            P("dp", expert),
            P(expert, None),
            P("dp", None),
        ),
        out_specs=(P("dp", None), P("dp", None), P("dp", expert), P(expert, "dp")),
        check_vma=False,
    )
```

```python
import functools

import jax
import jax.numpy as jnp
from jax import lax
from jax.experimental import pallas as pl
from jax.experimental.pallas import tpu as pltpu
from jax.sharding import PartitionSpec as P

EPSILON = 1e-06
F32 = jnp.float32
BF16 = jnp.bfloat16
STEP = 256
LANES = 128
TERMS = 3
PIECES = 2
LOAD_PIECES = 8
FEW_ROWS = 64
VMEM_LIMIT = 12 * 1024 * 1024
VMEM_LIMIT_MANY = 24 * 1024 * 1024


def dot(a, b, dims):
    return lax.dot_general(a, b, (dims, ((), ())), preferred_element_type=F32)


def place(step, count):
    return pl.multiple_of(step * count, count)


def parity(number):
    shift = 1
    while shift < 32:
        number = number ^ (number >> shift)
        shift = 2 * shift
    return number & 1


def own_half():
    chip = lax.axis_index("dp") ^ lax.axis_index("y") ^ lax.axis_index("hi")
    return lax.axis_index("c") ^ parity(chip)


def own_columns(i, j, width):
    return ((lax.axis_index("y") ^ j) * 2 + (own_half() ^ i)) * width


def folded(value):
    return sum(value[:, start : start + LANES] for start in range(0, value.shape[1], LANES))


def both_halves(refs, width, body):
    core, half = lax.axis_index("c"), width // 2
    size = 512 if len(refs[0]) <= 3 else 128
    for h in range(2):
        for step in range(half // size):
            columns = pl.ds(pl.multiple_of((core ^ h) * half + step * size, size), size)

            def rows_at(group):
                first = group[0][:, columns].astype(F32)
                others = [ref[:, step * size : (step + 1) * size].astype(F32) for ref in group[1 + h :: 2]]
                return jnp.concatenate([first] + others, axis=0)

            body(columns, *[rows_at(group) for group in refs])


def store_blocks(out_ref, j, columns, value, count):
    rows = value.shape[0] // count
    for k in range(count):
        out_ref[k, j, :, columns] = value[k * rows : (k + 1) * rows].astype(BF16)


def cut_kernel(n_dp, source, target, sem):
    width = target.shape[1]
    columns = pl.ds(pl.multiple_of(lax.axis_index("c") * width, width), width)
    copy = pltpu.make_async_copy(source.at[:, columns], target, sem)
    copy.start()
    copy.wait()


def gates_kernel(n_dp, named, weights, context, grads, w_gate, w_up, w_down, packed, named_held, weights_held, sems):
    width, heads = grads.shape[1] // 2, context.shape[1]
    columns = pl.ds(pl.multiple_of(lax.axis_index("c") * width, width), width)
    pairs = [
        (named, named_held), (weights, weights_held), (context, packed.at[:, pl.ds(width, heads)]),
        (grads.at[:, columns], packed.at[:, pl.ds(0, width)]),
    ]
    copies = [pltpu.make_async_copy(*pair, sems.at[n]) for n, pair in enumerate(pairs)]
    for copy in copies:
        copy.start()
    copies[0].wait()
    copies[1].wait()
    rows = context.shape[0]
    expert = (lax.axis_index("hi") * 2 + lax.axis_index("y")) * 2 + lax.axis_index("c")
    row = jnp.sum(jnp.where(named_held[...] == expert, weights_held[...], 0.0), axis=0, keepdims=True)
    square = (rows, rows)
    diagonal = lax.broadcasted_iota(jnp.int32, square, 0) == lax.broadcasted_iota(jnp.int32, square, 1)
    gate = jnp.sum(jnp.where(diagonal, row, 0.0), axis=1, keepdims=True)
    lane = lax.broadcasted_iota(jnp.int32, (rows, LANES), 1)
    rest, block = jnp.broadcast_to(gate, (rows, LANES)), jnp.zeros((rows, LANES), F32)
    for term in range(TERMS):
        rounded = rest.astype(BF16).astype(F32)
        block = jnp.where(lane == term, rounded, block)
        rest = rest - rounded
    packed[:, width + heads :] = block.astype(BF16)
    copies[2].wait()
    copies[3].wait()


def unit_step(units):
    return STEP if units % STEP == 0 else units


def loop(count, body, unroll):
    if unroll:
        for step in range(count):
            body(step)
    else:
        def carried(step, carry):
            body(step)
            return carry

        lax.fori_loop(0, count, carried, 0)


def gates_of(packs):
    first = packs[0].shape[1] - LANES
    blocks = [pack[:, first : first + LANES].astype(F32) for pack in packs]
    gates = jnp.concatenate(blocks, axis=0)
    return gates[:, 0:1] + gates[:, 1:2] + gates[:, 2:3]


def half_columns(h, half):
    return pl.multiple_of((lax.axis_index("c") ^ h) * half, half)


def scaled_half(h, own, others, gain, scaled):
    half = scaled.shape[1]
    first, size = half_columns(h, half), 512 if len(others) < 2 else 128
    squares = 0.0
    for start in range(0, half, size):
        columns = pl.ds(pl.multiple_of(first + start, size), size)
        rows = [own[:, columns]] + [other[:, start : start + size] for other in others]
        value = jnp.concatenate([row.astype(F32) for row in rows], axis=0)
        squares = squares + folded(value * value)
        scaled[:, start : start + size] = (value * gain[:, columns]).astype(BF16)
    return squares


def hidden_first_kernel(n_dp, own, *refs):
    others = refs[: n_dp - 1]
    gain, w_gate, w_up, gate_sum, up_sum, square_sum, scaled = refs[n_dp - 1 :]
    half = scaled.shape[1]
    square_sum[...] = scaled_half(0, own, others, gain, scaled)
    size, rows = unit_step(w_gate.shape[1]), pl.ds(half_columns(0, half), half)

    def hidden_units(step):
        columns = pl.ds(place(step, size), size)
        gate_sum[:, columns] = dot(scaled[...], w_gate[rows, columns], ((1,), (0,)))
        up_sum[:, columns] = dot(scaled[...], w_up[rows, columns], ((1,), (0,)))

    loop(w_gate.shape[1] // size, hidden_units, scaled.shape[0] <= FEW_ROWS)


def hidden_rest_kernel(n_dp, own, *refs):
    others = refs[: n_dp - 1]
    gain, w_gate, w_up, gate_sum, up_sum, square_sum, pre_gate, pre_up, act, scales, scaled = refs[n_dp - 1 :]
    half = scaled.shape[1]
    squares = square_sum[...] + scaled_half(1, own, others, gain, scaled)
    scale = lax.rsqrt(jnp.sum(squares, axis=1, keepdims=True) / (2 * half) + EPSILON)
    scales[...] = jnp.broadcast_to(scale, scales.shape)
    size, rows = unit_step(w_gate.shape[1]), pl.ds(half_columns(1, half), half)

    def hidden_units(step):
        columns = pl.ds(place(step, size), size)
        gate_part = scale * (gate_sum[:, columns] + dot(scaled[...], w_gate[rows, columns], ((1,), (0,))))
        up_part = scale * (up_sum[:, columns] + dot(scaled[...], w_up[rows, columns], ((1,), (0,))))
        pre_gate[:, columns] = gate_part
        pre_up[:, columns] = up_part
        act[:, columns] = (gate_part * jax.nn.sigmoid(gate_part) * up_part).astype(BF16)

    loop(w_gate.shape[1] // size, hidden_units, scaled.shape[0] <= FEW_ROWS)


def outward_kernel(i, n_dp, *refs):
    smalls = refs[:n_dp]
    act, w_down, *_, target = refs[n_dp:]
    weight = gates_of(smalls)
    chunk = target.shape[3]
    few = act.shape[0] <= FEW_ROWS
    for j in range(2):
        first = own_columns(i, j, chunk)

        def outward(step):
            columns = pl.ds(pl.multiple_of(first + step * STEP, STEP), STEP)
            part = weight * dot(act[...], w_down[:, columns], ((1,), (0,)))
            store_blocks(target, j, pl.ds(place(step, STEP), STEP), part, n_dp)

        loop(chunk // STEP, outward, few)


def inward_part(i, n_dp, grad_refs, w_gate, w_up, target):
    chunk = target.shape[3]
    few = grad_refs[0].shape[0] <= FEW_ROWS
    for j in range(2):
        first = own_columns(i, j, chunk)

        def inward(step):
            columns = pl.ds(pl.multiple_of(first + step * STEP, STEP), STEP)
            part = 0.0
            for parity, weights in ((0, w_gate), (1, w_up)):
                start = 0
                for ref in grad_refs[parity::2]:
                    part = part + dot(ref[...], weights[columns, start : start + ref.shape[1]], ((1,), (1,)))
                    start += ref.shape[1]
            store_blocks(target, j, pl.ds(place(step, STEP), STEP), part, n_dp)

        loop(chunk // STEP, inward, few)


def gradients(first, weighted, pre_gate, pre_up, w_down, grad_gate, grad_up, few):
    size = unit_step(w_down.shape[0])

    def hidden_units(step):
        columns = pl.ds(place(step, size), size)
        units = pl.ds(first + step * size, size)
        back = dot(weighted[...], w_down[units, :], ((1,), (1,)))
        gate_part, up_part = pre_gate[:, units], pre_up[:, units]
        sig = jax.nn.sigmoid(gate_part)
        grad_gate[:, columns] = (back * up_part * sig * (1.0 + gate_part * (1.0 - sig))).astype(BF16)
        grad_up[:, columns] = (back * gate_part * sig).astype(BF16)

    loop(grad_gate.shape[1] // size, hidden_units, few or grad_gate.shape[1] == size)


def backward_first_kernel(n_dp, *refs):
    grads, smalls = refs[: 2 * n_dp - 1], refs[2 * n_dp - 1 : 3 * n_dp - 1]
    pre_gate, pre_up, w_down, waiting, grad_gate, grad_up, weighted, passed = refs[3 * n_dp - 1 :]
    passed[...] = waiting[...]
    weight = gates_of(smalls)
    few = weighted.shape[0] <= FEW_ROWS

    def weigh(columns, value):
        weighted[:, columns] = (weight * value).astype(BF16)

    both_halves([grads], weighted.shape[1], weigh)
    gradients(0, weighted, pre_gate, pre_up, w_down, grad_gate, grad_up, few)


def backward_rest_kernel(n_dp, weighted, pre_gate, pre_up, w_down, waiting, grad_gate, grad_up, passed):
    passed[...] = waiting[...]
    first = pre_gate.shape[1] - grad_gate.shape[1]
    gradients(first, weighted, pre_gate, pre_up, w_down, grad_gate, grad_up, True)


def inward_kernel(i, n_dp, *refs):
    w_gate, w_up, waiting, target, passed = refs[-5:]
    passed[...] = waiting[...]
    inward_part(i, n_dp, refs[:-5], w_gate, w_up, target)


def join_kernel(n_dp, in_keep, in_other, out_block, *refs):
    for t in range(2 * n_dp):
        k, j = t // 2, t % 2
        refs[t][...] = (in_keep[k, j].astype(F32) + in_other[k, j].astype(F32)).astype(BF16)
    refs[-1][...] = out_block[...]


def own_rows_kernel(n_dp, hid, grads, *refs):
    back, gain, scales, w_out = refs[:4], refs[4], refs[5], refs[6]
    targets, d_half, held, summed, sems = refs[7:9], refs[9], refs[10:12], refs[12], refs[13]
    d_hidden, d_context = held
    copies = [pltpu.make_async_copy(held[n], targets[n], sems.at[n]) for n in range(2)]
    rows, width = hid.shape
    chunk = back[0].shape[1]
    products = 0.0
    for i in range(2):
        for j in range(2):
            columns = pl.ds(pl.multiple_of(own_columns(i, j, chunk), chunk), chunk)
            value = hid[:, columns].astype(F32)
            total = back[i * 2 + j][...].astype(F32) * gain[:, columns]
            summed[:, columns] = total
            products = products + folded(value * total)
    scale = scales[:rows, :1]
    centre = scale * jnp.sum(products, axis=1, keepdims=True) / width
    for start in range(0, width, 512):
        columns = slice(start, start + 512)
        value = summed[:, columns] - hid[:, columns].astype(F32) * scale * centre
        d_hidden[:, columns] = (grads[:, columns].astype(F32) + scale * value).astype(BF16)
    copies[0].start()
    part = width // n_dp
    d_half[...] = d_hidden[:, pl.ds(pl.multiple_of(lax.axis_index("dp") * part, part), part)]
    d_context[...] = dot(d_hidden[...], w_out[...], ((1,), (1,))).astype(BF16)
    copies[1].start()
    for copy in copies:
        copy.wait()


def far_rows_kernel(n_dp, *refs):
    count, far = 2 * (n_dp - 1), n_dp - 1
    hid, grads, packs = refs[:count], refs[count : 2 * count], refs[2 * count : 2 * count + n_dp]
    refs = refs[2 * count + n_dp :]
    back, refs = refs[: 4 * far], refs[4 * far :]
    own, moe, refs = refs[0], refs[1:3], refs[3:]
    d_half, gain, scales, out_target, target, output, held, summed, d_far, sems = refs
    rows, chunk = back[0].shape
    width = summed.shape[1]
    size = width // n_dp // PIECES
    copies = []
    for piece in range(PIECES):
        block = (slice(None), pl.ds(piece * size, size))
        copies.append(pltpu.make_async_copy(held.at[block], target.at[block], sems.at[piece]))
    copies.append(pltpu.make_async_copy(output, out_target, sems.at[PIECES]))
    for i in range(2):
        for j in range(2):
            columns = pl.ds(pl.multiple_of(own_columns(i, j, chunk), chunk), chunk)
            output[:, columns] = (own[:, columns].astype(F32) + moe[i][j].astype(F32)).astype(BF16)
            for k in range(far):
                piece = back[(i * far + k) * 2 + j][...].astype(F32)
                summed[k * rows : (k + 1) * rows, columns] = piece * gain[:, columns]
    copies[PIECES].start()
    half, step = width // 2, 512 if n_dp <= 2 else 128

    def over_halves(body):
        for h in range(2):
            for start in range(0, half, step):
                columns = pl.ds(pl.multiple_of(half_columns(h, half) + start, step), step)
                value, grad = [
                    jnp.concatenate([ref[:, start : start + step].astype(F32) for ref in group[h::2]], axis=0)
                    for group in (hid, grads)
                ]
                body(columns, value, grad)

    sums = [0.0]

    def products(columns, value, grad):
        sums[0] = sums[0] + folded(value * summed[:, columns])

    over_halves(products)
    scale = scales[rows:, :1]
    centre = scale * jnp.sum(sums[0], axis=1, keepdims=True) / width

    def total(columns, value, grad):
        d_far[:, columns] = grad + scale * (summed[:, columns] - value * scale * centre)

    over_halves(total)
    heads = held.shape[0]
    lanes = slice(half, half + heads)
    turned = jnp.concatenate([pack[:, lanes].astype(F32) for pack in packs], axis=0).T.astype(BF16)
    for piece in range(PIECES):
        first = lax.axis_index("dp") * (width // n_dp) + piece * size
        block = slice(piece * size, (piece + 1) * size)
        columns = pl.ds(pl.multiple_of(first, LANES), size)
        both = jnp.concatenate([d_half[:, block].astype(F32), d_far[:, columns]], axis=0).astype(BF16)
        held[:, block] = dot(turned, both, ((1,), (0,))).astype(BF16)
        copies[piece].start()
    for copy in copies:
        copy.wait()


def run(kernel, n_dp, operands, outs, scratch, cost, name, far=(), out_space=pltpu.VMEM):
    spaces = [pltpu.HBM if n in far else pltpu.VMEM for n in range(len(operands))]
    held = [pltpu.with_memory_space_constraint(value, space) for value, space in zip(operands, spaces)]
    places = out_space if isinstance(out_space, list) else [out_space] * len(outs)
    kinds = [place_of(shape, kind) for place_of, (shape, kind) in zip(places, outs)]
    return pl.pallas_call(
        functools.partial(kernel, n_dp),
        out_shape=kinds,
        in_specs=[pl.BlockSpec(memory_space=space) for space in spaces],
        out_specs=[pl.BlockSpec(memory_space=space) for space in places],
        scratch_shapes=scratch,
        compiler_params=pltpu.CompilerParams(vmem_limit_bytes=VMEM_LIMIT if n_dp <= 2 else VMEM_LIMIT_MANY),
        cost_estimate=pl.CostEstimate(flops=0, bytes_accessed=cost, transcendentals=0),
        name=name,
    )(*held)


def per_device(
    hidden_in, norm_gain, route_ids, route_gates, w_gate, w_up, w_down, context, w_out, grad_out
):
    n_dp, n_hi = lax.axis_size("dp"), lax.axis_size("hi")
    rows, width = hidden_in.shape
    top, heads = route_ids.shape[1], context.shape[1]
    all_rows, units, chunk = n_dp * rows, w_gate.shape[2], width // 4

    def swap(value, axes, turn, cross=True):
        count = 2
        for name in axes:
            count *= lax.axis_size(name)
        turn = 2 * turn + (parity(turn) if cross else 0)
        return lax.ppermute(value, axes + ("c",), [(i, i ^ turn) for i in range(count)])

    def other_core(value):
        return lax.ppermute(value, ("c",), [(0, 1), (1, 0)])

    weights = 2 * width * units
    shares = ((n_dp, 2, rows, chunk), BF16)
    wg, wu, wd, gain = w_gate[0], w_up[0], w_down[0], norm_gain.reshape(1, width)
    half = width // 2
    (hid_half,) = run(
        cut_kernel, n_dp, [hidden_in], [((rows, half), BF16)], [pltpu.SemaphoreType.DMA], rows * width, "cut", far=(0,)
    )
    (packed,) = run(
        gates_kernel, n_dp, [route_ids.T, route_gates.T, context, grad_out, wg, wu, wd],
        [((rows, half + heads + LANES), BF16)],
        [pltpu.VMEM((top, rows), jnp.int32), pltpu.VMEM((top, rows), F32), pltpu.SemaphoreType.DMA((4,))],
        4 * weights, "gates", far=range(7),
    )

    def others(value):
        here = [swap(value, ("dp",), k, False) for k in range(1, n_dp)]
        return here, [piece for one in here for piece in (one, other_core(one))]

    hid = [hidden_in] + others(hid_half)[1]
    packs, blocks = others(packed)
    smalls, grads = [packed] + packs, [grad_out] + blocks

    def add(one, other):
        return (one.astype(F32) + other.astype(F32)).astype(BF16)

    def total_of(pieces):
        total = pieces[0].astype(F32)
        for piece in pieces[1:]:
            total = total + piece.astype(F32)
        return total.astype(BF16)

    hidden_units, row_block = ((all_rows, units), F32), ((all_rows, LANES), F32)
    scaled = pltpu.VMEM((all_rows, half), BF16)
    gate_sum, up_sum, square_sum = run(
        hidden_first_kernel, n_dp, [hidden_in] + hid[1::2] + [gain, wg, wu],
        [hidden_units, hidden_units, row_block], [scaled], weights, "hidden_first",
    )
    pre_gate, pre_up, act, scales = run(
        hidden_rest_kernel, n_dp, [hidden_in] + hid[2::2] + [gain, wg, wu, gate_sum, up_sum, square_sum],
        [hidden_units, hidden_units, ((all_rows, units), BF16), row_block], [scaled], weights, "hidden_rest",
    )
    (out_send,) = run(
        functools.partial(outward_kernel, 1), n_dp, smalls + [act, wd], [shares], [],
        weights // 2, "outward_send",
    )
    out_other = other_core(out_send)
    (out_keep,) = run(
        functools.partial(outward_kernel, 0), n_dp, smalls + [act, wd, out_send], [shares], [],
        weights // 2, "outward_keep",
    )
    size = unit_step(units)
    first_units, rest_units = ((all_rows, size), BF16), ((all_rows, units - size), BF16)
    gate_first, up_first, weighted, out_keep = run(
        backward_first_kernel, n_dp, grads + smalls + [pre_gate, pre_up, wd, out_keep],
        [first_units, first_units, ((all_rows, width), BF16), shares], [], weights // 3, "backward_first",
    )
    back_grads = [gate_first, up_first]
    out_half = add(out_keep, out_other)
    out_blocks = [swap(out_half[k], ("dp",), k) for k in range(1, n_dp)]
    block, out_block = (shares[0][1:], BF16), out_half[0]
    if size < units:
        gate_rest, up_rest, out_block = run(
            backward_rest_kernel, n_dp, [weighted, pre_gate, pre_up, wd, out_block],
            [rest_units, rest_units, block], [], weights * 2 // 3, "backward_rest",
        )
        back_grads = back_grads + [gate_rest, up_rest]
    in_send, out_block = run(
        functools.partial(inward_kernel, 1), n_dp, back_grads + [wg, wu, out_block],
        [shares, block], [], weights, "inward_send",
    )
    in_other = other_core(in_send)
    out_block = total_of([out_block] + out_blocks)
    in_keep, out_block = run(
        functools.partial(inward_kernel, 0), n_dp, back_grads + [wg, wu, out_block], [shares, block], [],
        weights, "inward_keep",
    )
    *in_pieces, out_block = run(
        join_kernel, n_dp, [in_keep, in_other, out_block], [((rows, chunk), BF16)] * (2 * n_dp) + [block], [],
        rows * width, "join",
    )
    turns = [t for t in range(2 * n_dp - 1, 0, -1)]
    in_share = total_of([in_pieces[0]] + [swap(in_pieces[t], ("dp", "y"), t) for t in turns])
    out_total = add(out_block, swap(out_block, ("y",), 1)[::-1])
    in_total = total_of([in_share] + [swap(in_share, ("hi",), t) for t in range(1, n_hi)])
    turn = 1
    while turn < n_hi:
        out_total = add(out_total, swap(out_total, ("hi",), turn))
        turn = 2 * turn
    spread = {t: swap(in_total, ("dp", "y"), t) for t in turns}
    back = [in_total] + [spread[t] for t in range(1, 2 * n_dp)]
    crossed = [other_core(one) for one in back]
    moe = [out_total, other_core(out_total)]
    part, far_rows = width // n_dp, all_rows - rows
    whole, context_out, weight_out = ((rows, width), BF16), ((rows, heads), BF16), ((heads, part), BF16)
    d_hidden, d_context, d_half = run(
        own_rows_kernel, n_dp, [hidden_in, grad_out] + back[:2] + crossed[:2] + [gain, scales, w_out],
        [whole, context_out, ((rows, part), BF16)],
        [pltpu.VMEM(*whole), pltpu.VMEM(*context_out), pltpu.VMEM((rows, width), F32), pltpu.SemaphoreType.DMA((2,))],
        weights // 2, "own_rows", out_space=[pltpu.HBM] * 2 + [pltpu.VMEM],
    )
    output, d_w_out = run(
        far_rows_kernel, n_dp,
        hid[1:] + grads[1:] + smalls + back[2:] + crossed[2:] + [hidden_in] + moe + [d_half, gain, scales],
        [whole, weight_out],
        [pltpu.VMEM(*whole), pltpu.VMEM(*weight_out), pltpu.VMEM((far_rows, width), F32),
         pltpu.VMEM((far_rows, width), F32), pltpu.SemaphoreType.DMA((PIECES + 1,))],
        weights // 2, "far_rows", out_space=pltpu.HBM,
    )
    return output, d_hidden, d_context, d_w_out


def solution(mesh):
    n_dp, n_e = mesh.shape["dp"], mesh.shape["expert"]
    names = ("dp", "hi", "y", "c")
    mesh = jax.sharding.Mesh(mesh.devices.reshape(n_dp, n_e // 4, 2, 2), names)
    expert = names[1:]
    return jax.shard_map(
        per_device,
        mesh=mesh,
        in_specs=(
            P("dp", None),
            P(),
            P("dp", None),
            P("dp", None),
            P(expert, None, "dp"),
            P(expert, None, "dp"),
            P(expert, "dp", None),
            P("dp", expert),
            P(expert, None),
            P("dp", None),
        ),
        out_specs=(P("dp", None), P("dp", None), P("dp", expert), P(expert, "dp")),
        check_vma=False,
    )
```

```python
import functools

import jax
import jax.numpy as jnp
from jax import lax
from jax.experimental import pallas as pl
from jax.experimental.pallas import tpu as pltpu
from jax.sharding import PartitionSpec as P

EPSILON = 1e-06
F32 = jnp.float32
BF16 = jnp.bfloat16
STEP = 256
LANES = 128
TERMS = 3
PIECES = 2
LOAD_PIECES = 8
FEW_ROWS = 64
VMEM_LIMIT = 12 * 1024 * 1024
VMEM_LIMIT_MANY = 24 * 1024 * 1024


def dot(a, b, dims):
    return lax.dot_general(a, b, (dims, ((), ())), preferred_element_type=F32)


def place(step, count):
    return pl.multiple_of(step * count, count)


def parity(number):
    shift = 1
    while shift < 32:
        number = number ^ (number >> shift)
        shift = 2 * shift
    return number & 1


def own_half():
    chip = lax.axis_index("dp") ^ lax.axis_index("y") ^ lax.axis_index("hi")
    return lax.axis_index("c") ^ parity(chip)


def own_columns(i, j, width):
    return ((lax.axis_index("y") ^ j) * 2 + (own_half() ^ i)) * width


def folded(value):
    return sum(value[:, start : start + LANES] for start in range(0, value.shape[1], LANES))


def both_halves(refs, width, body):
    core, half = lax.axis_index("c"), width // 2
    size = 512 if len(refs[0]) <= 3 else 128
    for h in range(2):
        for step in range(half // size):
            columns = pl.ds(pl.multiple_of((core ^ h) * half + step * size, size), size)

            def rows_at(group):
                first = group[0][:, columns].astype(F32)
                others = [ref[:, step * size : (step + 1) * size].astype(F32) for ref in group[1 + h :: 2]]
                return jnp.concatenate([first] + others, axis=0)

            body(columns, *[rows_at(group) for group in refs])


def store_blocks(out_ref, j, columns, value, count):
    rows = value.shape[0] // count
    for k in range(count):
        out_ref[k, j, :, columns] = value[k * rows : (k + 1) * rows].astype(BF16)


def cut_kernel(n_dp, source, target, sem):
    width = target.shape[1]
    columns = pl.ds(pl.multiple_of(lax.axis_index("c") * width, width), width)
    copy = pltpu.make_async_copy(source.at[:, columns], target, sem)
    copy.start()
    copy.wait()


def gates_kernel(n_dp, named, weights, context, grads, w_gate, w_up, w_down, packed, named_held, weights_held, sems):
    width, heads = grads.shape[1] // 2, context.shape[1]
    columns = pl.ds(pl.multiple_of(lax.axis_index("c") * width, width), width)
    pairs = [
        (named, named_held), (weights, weights_held), (context, packed.at[:, pl.ds(width, heads)]),
        (grads.at[:, columns], packed.at[:, pl.ds(0, width)]),
    ]
    copies = [pltpu.make_async_copy(*pair, sems.at[n]) for n, pair in enumerate(pairs)]
    for copy in copies:
        copy.start()
    copies[0].wait()
    copies[1].wait()
    rows = context.shape[0]
    expert = (lax.axis_index("hi") * 2 + lax.axis_index("y")) * 2 + lax.axis_index("c")
    row = jnp.sum(jnp.where(named_held[...] == expert, weights_held[...], 0.0), axis=0, keepdims=True)
    square = (rows, rows)
    diagonal = lax.broadcasted_iota(jnp.int32, square, 0) == lax.broadcasted_iota(jnp.int32, square, 1)
    gate = jnp.sum(jnp.where(diagonal, row, 0.0), axis=1, keepdims=True)
    lane = lax.broadcasted_iota(jnp.int32, (rows, LANES), 1)
    rest, block = jnp.broadcast_to(gate, (rows, LANES)), jnp.zeros((rows, LANES), F32)
    for term in range(TERMS):
        rounded = rest.astype(BF16).astype(F32)
        block = jnp.where(lane == term, rounded, block)
        rest = rest - rounded
    packed[:, width + heads :] = block.astype(BF16)
    copies[2].wait()
    copies[3].wait()


def unit_step(units):
    return STEP if units % STEP == 0 else units


def loop(count, body, unroll):
    if unroll:
        for step in range(count):
            body(step)
    else:
        def carried(step, carry):
            body(step)
            return carry

        lax.fori_loop(0, count, carried, 0)


def gates_of(packs):
    first = packs[0].shape[1] - LANES
    blocks = [pack[:, first : first + LANES].astype(F32) for pack in packs]
    gates = jnp.concatenate(blocks, axis=0)
    return gates[:, 0:1] + gates[:, 1:2] + gates[:, 2:3]


def half_columns(h, half):
    return pl.multiple_of((lax.axis_index("c") ^ h) * half, half)


def scaled_half(h, own, others, gain, scaled):
    half = scaled.shape[1]
    first, size = half_columns(h, half), 512 if len(others) < 2 else 128
    squares = 0.0
    for start in range(0, half, size):
        columns = pl.ds(pl.multiple_of(first + start, size), size)
        rows = [own[:, columns]] + [other[:, start : start + size] for other in others]
        value = jnp.concatenate([row.astype(F32) for row in rows], axis=0)
        squares = squares + folded(value * value)
        scaled[:, start : start + size] = (value * gain[:, columns]).astype(BF16)
    return squares


def hidden_first_kernel(n_dp, own, *refs):
    others = refs[: n_dp - 1]
    gain, w_gate, w_up, gate_sum, up_sum, square_sum, scaled = refs[n_dp - 1 :]
    half = scaled.shape[1]
    square_sum[...] = scaled_half(0, own, others, gain, scaled)
    size, rows = unit_step(w_gate.shape[1]), pl.ds(half_columns(0, half), half)

    def hidden_units(step):
        columns = pl.ds(place(step, size), size)
        gate_sum[:, columns] = dot(scaled[...], w_gate[rows, columns], ((1,), (0,)))
        up_sum[:, columns] = dot(scaled[...], w_up[rows, columns], ((1,), (0,)))

    loop(w_gate.shape[1] // size, hidden_units, scaled.shape[0] <= FEW_ROWS)


def hidden_rest_kernel(n_dp, own, *refs):
    others = refs[: n_dp - 1]
    gain, w_gate, w_up, gate_sum, up_sum, square_sum, pre_gate, pre_up, act, scales, scaled = refs[n_dp - 1 :]
    half = scaled.shape[1]
    squares = square_sum[...] + scaled_half(1, own, others, gain, scaled)
    scale = lax.rsqrt(jnp.sum(squares, axis=1, keepdims=True) / (2 * half) + EPSILON)
    scales[...] = jnp.broadcast_to(scale, scales.shape)
    size, rows = unit_step(w_gate.shape[1]), pl.ds(half_columns(1, half), half)

    def hidden_units(step):
        columns = pl.ds(place(step, size), size)
        gate_part = scale * (gate_sum[:, columns] + dot(scaled[...], w_gate[rows, columns], ((1,), (0,))))
        up_part = scale * (up_sum[:, columns] + dot(scaled[...], w_up[rows, columns], ((1,), (0,))))
        pre_gate[:, columns] = gate_part
        pre_up[:, columns] = up_part
        act[:, columns] = (gate_part * jax.nn.sigmoid(gate_part) * up_part).astype(BF16)

    loop(w_gate.shape[1] // size, hidden_units, scaled.shape[0] <= FEW_ROWS)


def outward_kernel(i, n_dp, *refs):
    smalls = refs[:n_dp]
    act, w_down, *_, target = refs[n_dp:]
    weight = gates_of(smalls)
    chunk = target.shape[3]
    few = act.shape[0] <= FEW_ROWS
    for j in range(2):
        first = own_columns(i, j, chunk)

        def outward(step):
            columns = pl.ds(pl.multiple_of(first + step * STEP, STEP), STEP)
            part = weight * dot(act[...], w_down[:, columns], ((1,), (0,)))
            store_blocks(target, j, pl.ds(place(step, STEP), STEP), part, n_dp)

        loop(chunk // STEP, outward, few)


def inward_part(i, n_dp, grad_refs, w_gate, w_up, target):
    chunk = target.shape[3]
    few = grad_refs[0].shape[0] <= FEW_ROWS
    for j in range(2):
        first = own_columns(i, j, chunk)

        def inward(step):
            columns = pl.ds(pl.multiple_of(first + step * STEP, STEP), STEP)
            part = 0.0
            for parity, weights in ((0, w_gate), (1, w_up)):
                start = 0
                for ref in grad_refs[parity::2]:
                    part = part + dot(ref[...], weights[columns, start : start + ref.shape[1]], ((1,), (1,)))
                    start += ref.shape[1]
            store_blocks(target, j, pl.ds(place(step, STEP), STEP), part, n_dp)

        loop(chunk // STEP, inward, few)


def gradients(first, weighted, pre_gate, pre_up, w_down, grad_gate, grad_up, few):
    size = unit_step(w_down.shape[0])

    def hidden_units(step):
        columns = pl.ds(place(step, size), size)
        units = pl.ds(first + step * size, size)
        back = dot(weighted[...], w_down[units, :], ((1,), (1,)))
        gate_part, up_part = pre_gate[:, units], pre_up[:, units]
        sig = jax.nn.sigmoid(gate_part)
        grad_gate[:, columns] = (back * up_part * sig * (1.0 + gate_part * (1.0 - sig))).astype(BF16)
        grad_up[:, columns] = (back * gate_part * sig).astype(BF16)

    loop(grad_gate.shape[1] // size, hidden_units, few or grad_gate.shape[1] == size)


def backward_first_kernel(n_dp, *refs):
    grads, smalls = refs[: 2 * n_dp - 1], refs[2 * n_dp - 1 : 3 * n_dp - 1]
    pre_gate, pre_up, w_down, waiting, grad_gate, grad_up, weighted, passed = refs[3 * n_dp - 1 :]
    passed[...] = waiting[...]
    weight = gates_of(smalls)
    few = weighted.shape[0] <= FEW_ROWS

    def weigh(columns, value):
        weighted[:, columns] = (weight * value).astype(BF16)

    both_halves([grads], weighted.shape[1], weigh)
    gradients(0, weighted, pre_gate, pre_up, w_down, grad_gate, grad_up, few)


def backward_rest_kernel(n_dp, weighted, pre_gate, pre_up, w_down, waiting, grad_gate, grad_up, passed):
    passed[...] = waiting[...]
    first = pre_gate.shape[1] - grad_gate.shape[1]
    gradients(first, weighted, pre_gate, pre_up, w_down, grad_gate, grad_up, True)


def inward_kernel(i, n_dp, *refs):
    w_gate, w_up, waiting, target, passed = refs[-5:]
    passed[...] = waiting[...]
    inward_part(i, n_dp, refs[:-5], w_gate, w_up, target)


def join_kernel(n_dp, in_keep, in_other, out_block, *refs):
    for t in range(2 * n_dp):
        k, j = t // 2, t % 2
        refs[t][...] = (in_keep[k, j].astype(F32) + in_other[k, j].astype(F32)).astype(BF16)
    refs[-1][...] = out_block[...]


def own_rows_kernel(n_dp, hid, grads, *refs):
    back, gain, scales, w_out = refs[:4], refs[4], refs[5], refs[6]
    targets, d_half, held, summed, sems = refs[7:9], refs[9], refs[10:12], refs[12], refs[13]
    d_hidden, d_context = held
    copies = [pltpu.make_async_copy(held[n], targets[n], sems.at[n]) for n in range(2)]
    rows, width = hid.shape
    chunk = back[0].shape[1]
    products = 0.0
    for i in range(2):
        for j in range(2):
            columns = pl.ds(pl.multiple_of(own_columns(i, j, chunk), chunk), chunk)
            value = hid[:, columns].astype(F32)
            total = back[i * 2 + j][...].astype(F32) * gain[:, columns]
            summed[:, columns] = total
            products = products + folded(value * total)
    scale = scales[:rows, :1]
    centre = scale * jnp.sum(products, axis=1, keepdims=True) / width
    for start in range(0, width, 512):
        columns = slice(start, start + 512)
        value = summed[:, columns] - hid[:, columns].astype(F32) * scale * centre
        d_hidden[:, columns] = (grads[:, columns].astype(F32) + scale * value).astype(BF16)
    copies[0].start()
    part = width // n_dp
    d_half[...] = d_hidden[:, pl.ds(pl.multiple_of(lax.axis_index("dp") * part, part), part)]
    d_context[...] = dot(d_hidden[...], w_out[...], ((1,), (1,))).astype(BF16)
    copies[1].start()
    for copy in copies:
        copy.wait()


def far_rows_kernel(n_dp, *refs):
    count, far = 2 * (n_dp - 1), n_dp - 1
    hid, grads, packs = refs[:count], refs[count : 2 * count], refs[2 * count : 2 * count + n_dp]
    refs = refs[2 * count + n_dp :]
    back, refs = refs[: 4 * far], refs[4 * far :]
    own, moe, refs = refs[0], refs[1:3], refs[3:]
    d_half, gain, scales, out_target, target, output, held, summed, d_far, sems = refs
    rows, chunk = back[0].shape
    width = summed.shape[1]
    size = width // n_dp // PIECES
    copies = []
    for piece in range(PIECES):
        block = (slice(None), pl.ds(piece * size, size))
        copies.append(pltpu.make_async_copy(held.at[block], target.at[block], sems.at[piece]))
    copies.append(pltpu.make_async_copy(output, out_target, sems.at[PIECES]))
    for i in range(2):
        for j in range(2):
            columns = pl.ds(pl.multiple_of(own_columns(i, j, chunk), chunk), chunk)
            output[:, columns] = (own[:, columns].astype(F32) + moe[i][j].astype(F32)).astype(BF16)
            for k in range(far):
                piece = back[(i * far + k) * 2 + j][...].astype(F32)
                summed[k * rows : (k + 1) * rows, columns] = piece * gain[:, columns]
    copies[PIECES].start()
    half, step = width // 2, 512 if n_dp <= 2 else 128

    def over_halves(body):
        for h in range(2):
            for start in range(0, half, step):
                columns = pl.ds(pl.multiple_of(half_columns(h, half) + start, step), step)
                value, grad = [
                    jnp.concatenate([ref[:, start : start + step].astype(F32) for ref in group[h::2]], axis=0)
                    for group in (hid, grads)
                ]
                body(columns, value, grad)

    sums = [0.0]

    def products(columns, value, grad):
        sums[0] = sums[0] + folded(value * summed[:, columns])

    over_halves(products)
    scale = scales[rows:, :1]
    centre = scale * jnp.sum(sums[0], axis=1, keepdims=True) / width

    def total(columns, value, grad):
        d_far[:, columns] = grad + scale * (summed[:, columns] - value * scale * centre)

    over_halves(total)
    heads = held.shape[0]
    lanes = slice(half, half + heads)
    turned = jnp.concatenate([pack[:, lanes].astype(F32) for pack in packs], axis=0).T.astype(BF16)
    for piece in range(PIECES):
        first = lax.axis_index("dp") * (width // n_dp) + piece * size
        block = slice(piece * size, (piece + 1) * size)
        columns = pl.ds(pl.multiple_of(first, LANES), size)
        both = jnp.concatenate([d_half[:, block].astype(F32), d_far[:, columns]], axis=0).astype(BF16)
        held[:, block] = dot(turned, both, ((1,), (0,))).astype(BF16)
        copies[piece].start()
    for copy in copies:
        copy.wait()


def run(kernel, n_dp, operands, outs, scratch, cost, name, far=(), out_space=pltpu.VMEM):
    spaces = [pltpu.HBM if n in far else pltpu.VMEM for n in range(len(operands))]
    held = [pltpu.with_memory_space_constraint(value, space) for value, space in zip(operands, spaces)]
    places = out_space if isinstance(out_space, list) else [out_space] * len(outs)
    kinds = [place_of(shape, kind) for place_of, (shape, kind) in zip(places, outs)]
    return pl.pallas_call(
        functools.partial(kernel, n_dp),
        out_shape=kinds,
        in_specs=[pl.BlockSpec(memory_space=space) for space in spaces],
        out_specs=[pl.BlockSpec(memory_space=space) for space in places],
        scratch_shapes=scratch,
        compiler_params=pltpu.CompilerParams(vmem_limit_bytes=VMEM_LIMIT if n_dp <= 2 else VMEM_LIMIT_MANY),
        cost_estimate=pl.CostEstimate(flops=0, bytes_accessed=cost, transcendentals=0),
        name=name,
    )(*held)


def per_device(
    hidden_in, norm_gain, route_ids, route_gates, w_gate, w_up, w_down, context, w_out, grad_out
):
    n_dp, n_hi = lax.axis_size("dp"), lax.axis_size("hi")
    rows, width = hidden_in.shape
    top, heads = route_ids.shape[1], context.shape[1]
    all_rows, units, chunk = n_dp * rows, w_gate.shape[2], width // 4

    def swap(value, axes, turn, cross=True):
        count = 2
        for name in axes:
            count *= lax.axis_size(name)
        turn = 2 * turn + (parity(turn) if cross else 0)
        return lax.ppermute(value, axes + ("c",), [(i, i ^ turn) for i in range(count)])

    def other_core(value):
        return lax.ppermute(value, ("c",), [(0, 1), (1, 0)])

    weights = 2 * width * units
    shares = ((n_dp, 2, rows, chunk), BF16)
    wg, wu, wd, gain = w_gate[0], w_up[0], w_down[0], norm_gain.reshape(1, width)
    half = width // 2
    (hid_half,) = run(
        cut_kernel, n_dp, [hidden_in], [((rows, half), BF16)], [pltpu.SemaphoreType.DMA], rows * width, "cut", far=(0,)
    )
    (packed,) = run(
        gates_kernel, n_dp, [route_ids.T, route_gates.T, context, grad_out, wg, wu, wd],
        [((rows, half + heads + LANES), BF16)],
        [pltpu.VMEM((top, rows), jnp.int32), pltpu.VMEM((top, rows), F32), pltpu.SemaphoreType.DMA((4,))],
        4 * weights, "gates", far=range(7),
    )

    def others(value):
        here = [swap(value, ("dp",), k, False) for k in range(1, n_dp)]
        return here, [piece for one in here for piece in (one, other_core(one))]

    hid = [hidden_in] + others(hid_half)[1]
    packs, blocks = others(packed)
    smalls, grads = [packed] + packs, [grad_out] + blocks

    def add(one, other):
        return (one.astype(F32) + other.astype(F32)).astype(BF16)

    def total_of(pieces):
        total = pieces[0].astype(F32)
        for piece in pieces[1:]:
            total = total + piece.astype(F32)
        return total.astype(BF16)

    hidden_units, row_block = ((all_rows, units), F32), ((all_rows, LANES), F32)
    scaled = pltpu.VMEM((all_rows, half), BF16)
    gate_sum, up_sum, square_sum = run(
        hidden_first_kernel, n_dp, [hidden_in] + hid[1::2] + [gain, wg, wu],
        [hidden_units, hidden_units, row_block], [scaled], weights, "hidden_first",
    )
    pre_gate, pre_up, act, scales = run(
        hidden_rest_kernel, n_dp, [hidden_in] + hid[2::2] + [gain, wg, wu, gate_sum, up_sum, square_sum],
        [hidden_units, hidden_units, ((all_rows, units), BF16), row_block], [scaled], weights, "hidden_rest",
    )
    (out_send,) = run(
        functools.partial(outward_kernel, 1), n_dp, smalls + [act, wd], [shares], [],
        weights // 2, "outward_send",
    )
    out_other = other_core(out_send)
    (out_keep,) = run(
        functools.partial(outward_kernel, 0), n_dp, smalls + [act, wd, out_send], [shares], [],
        weights // 2, "outward_keep",
    )
    size = unit_step(units)
    first_units, rest_units = ((all_rows, size), BF16), ((all_rows, units - size), BF16)
    gate_first, up_first, weighted, out_keep = run(
        backward_first_kernel, n_dp, grads + smalls + [pre_gate, pre_up, wd, out_keep],
        [first_units, first_units, ((all_rows, width), BF16), shares], [], weights // 3, "backward_first",
    )
    back_grads = [gate_first, up_first]
    out_half = add(out_keep, out_other)
    out_blocks = [swap(out_half[k], ("dp",), k) for k in range(1, n_dp)]
    block, out_block = (shares[0][1:], BF16), out_half[0]
    if size < units:
        gate_rest, up_rest, out_block = run(
            backward_rest_kernel, n_dp, [weighted, pre_gate, pre_up, wd, out_block],
            [rest_units, rest_units, block], [], weights * 2 // 3, "backward_rest",
        )
        back_grads = back_grads + [gate_rest, up_rest]
    in_send, out_block = run(
        functools.partial(inward_kernel, 1), n_dp, back_grads + [wg, wu, out_block],
        [shares, block], [], weights, "inward_send",
    )
    in_other = other_core(in_send)
    out_block = total_of([out_block] + out_blocks)
    in_keep, out_block = run(
        functools.partial(inward_kernel, 0), n_dp, back_grads + [wg, wu, out_block], [shares, block], [],
        weights, "inward_keep",
    )
    *in_pieces, out_block = run(
        join_kernel, n_dp, [in_keep, in_other, out_block], [((rows, chunk), BF16)] * (2 * n_dp) + [block], [],
        rows * width, "join",
    )
    turns = [t for t in range(2 * n_dp - 1, 0, -1)]
    in_share = total_of([in_pieces[0]] + [swap(in_pieces[t], ("dp", "y"), t) for t in turns])
    out_total = out_block
    in_total = total_of([in_share] + [swap(in_share, ("hi",), t) for t in range(1, n_hi)])
    turn = 1
    while turn < n_hi:
        out_total = add(out_total, swap(out_total, ("hi",), turn))
        turn = 2 * turn
    out_total = add(out_total, swap(out_total, ("y",), 1)[::-1])
    spread = {t: swap(in_total, ("dp", "y"), t) for t in turns}
    back = [in_total] + [spread[t] for t in range(1, 2 * n_dp)]
    crossed = [other_core(one) for one in back]
    moe = [out_total, other_core(out_total)]
    part, far_rows = width // n_dp, all_rows - rows
    whole, context_out, weight_out = ((rows, width), BF16), ((rows, heads), BF16), ((heads, part), BF16)
    d_hidden, d_context, d_half = run(
        own_rows_kernel, n_dp, [hidden_in, grad_out] + back[:2] + crossed[:2] + [gain, scales, w_out],
        [whole, context_out, ((rows, part), BF16)],
        [pltpu.VMEM(*whole), pltpu.VMEM(*context_out), pltpu.VMEM((rows, width), F32), pltpu.SemaphoreType.DMA((2,))],
        weights // 2, "own_rows", out_space=[pltpu.HBM] * 2 + [pltpu.VMEM],
    )
    output, d_w_out = run(
        far_rows_kernel, n_dp,
        hid[1:] + grads[1:] + smalls + back[2:] + crossed[2:] + [hidden_in] + moe + [d_half, gain, scales],
        [whole, weight_out],
        [pltpu.VMEM(*whole), pltpu.VMEM(*weight_out), pltpu.VMEM((far_rows, width), F32),
         pltpu.VMEM((far_rows, width), F32), pltpu.SemaphoreType.DMA((PIECES + 1,))],
        weights // 2, "far_rows", out_space=pltpu.HBM,
    )
    return output, d_hidden, d_context, d_w_out


def solution(mesh):
    n_dp, n_e = mesh.shape["dp"], mesh.shape["expert"]
    names = ("dp", "hi", "y", "c")
    mesh = jax.sharding.Mesh(mesh.devices.reshape(n_dp, n_e // 4, 2, 2), names)
    expert = names[1:]
    return jax.shard_map(
        per_device,
        mesh=mesh,
        in_specs=(
            P("dp", None),
            P(),
            P("dp", None),
            P("dp", None),
            P(expert, None, "dp"),
            P(expert, None, "dp"),
            P(expert, "dp", None),
            P("dp", expert),
            P(expert, None),
            P("dp", None),
        ),
        out_specs=(P("dp", None), P("dp", None), P("dp", expert), P(expert, "dp")),
        check_vma=False,
    )
```

```python
import functools

import jax
import jax.numpy as jnp
from jax import lax
from jax.experimental import pallas as pl
from jax.experimental.pallas import tpu as pltpu
from jax.sharding import PartitionSpec as P

EPSILON = 1e-06
F32 = jnp.float32
BF16 = jnp.bfloat16
STEP = 256
LANES = 128
TERMS = 3
PIECES = 2
LOAD_PIECES = 8
FEW_ROWS = 64
VMEM_LIMIT = 12 * 1024 * 1024
VMEM_LIMIT_MANY = 24 * 1024 * 1024


def dot(a, b, dims):
    return lax.dot_general(a, b, (dims, ((), ())), preferred_element_type=F32)


def place(step, count):
    return pl.multiple_of(step * count, count)


def parity(number):
    shift = 1
    while shift < 32:
        number = number ^ (number >> shift)
        shift = 2 * shift
    return number & 1


def own_half():
    chip = lax.axis_index("dp") ^ lax.axis_index("y") ^ lax.axis_index("hi")
    return lax.axis_index("c") ^ parity(chip)


def own_columns(i, j, width):
    return ((lax.axis_index("y") ^ j) * 2 + (own_half() ^ i)) * width


def folded(value):
    return sum(value[:, start : start + LANES] for start in range(0, value.shape[1], LANES))


def both_halves(refs, width, body):
    core, half = lax.axis_index("c"), width // 2
    size = 512 if len(refs[0]) <= 3 else 128
    for h in range(2):
        for step in range(half // size):
            columns = pl.ds(pl.multiple_of((core ^ h) * half + step * size, size), size)

            def rows_at(group):
                first = group[0][:, columns].astype(F32)
                others = [ref[:, step * size : (step + 1) * size].astype(F32) for ref in group[1 + h :: 2]]
                return jnp.concatenate([first] + others, axis=0)

            body(columns, *[rows_at(group) for group in refs])


def store_blocks(out_ref, j, columns, value, count):
    rows = value.shape[0] // count
    for k in range(count):
        out_ref[k, j, :, columns] = value[k * rows : (k + 1) * rows].astype(BF16)


def cut_kernel(n_dp, source, target, sem):
    width = target.shape[1]
    columns = pl.ds(pl.multiple_of(lax.axis_index("c") * width, width), width)
    copy = pltpu.make_async_copy(source.at[:, columns], target, sem)
    copy.start()
    copy.wait()


def gates_kernel(n_dp, named, weights, context, grads, w_gate, w_up, w_down, packed, named_held, weights_held, sems):
    width, heads = grads.shape[1] // 2, context.shape[1]
    columns = pl.ds(pl.multiple_of(lax.axis_index("c") * width, width), width)
    pairs = [
        (named, named_held), (weights, weights_held), (context, packed.at[:, pl.ds(width, heads)]),
        (grads.at[:, columns], packed.at[:, pl.ds(0, width)]),
    ]
    copies = [pltpu.make_async_copy(*pair, sems.at[n]) for n, pair in enumerate(pairs)]
    for copy in copies:
        copy.start()
    copies[0].wait()
    copies[1].wait()
    rows = context.shape[0]
    expert = (lax.axis_index("hi") * 2 + lax.axis_index("y")) * 2 + lax.axis_index("c")
    row = jnp.sum(jnp.where(named_held[...] == expert, weights_held[...], 0.0), axis=0, keepdims=True)
    square = (rows, rows)
    diagonal = lax.broadcasted_iota(jnp.int32, square, 0) == lax.broadcasted_iota(jnp.int32, square, 1)
    gate = jnp.sum(jnp.where(diagonal, row, 0.0), axis=1, keepdims=True)
    lane = lax.broadcasted_iota(jnp.int32, (rows, LANES), 1)
    rest, block = jnp.broadcast_to(gate, (rows, LANES)), jnp.zeros((rows, LANES), F32)
    for term in range(TERMS):
        rounded = rest.astype(BF16).astype(F32)
        block = jnp.where(lane == term, rounded, block)
        rest = rest - rounded
    packed[:, width + heads :] = block.astype(BF16)
    copies[2].wait()
    copies[3].wait()


def unit_step(units):
    return STEP if units % STEP == 0 else units


def loop(count, body, unroll):
    if unroll:
        for step in range(count):
            body(step)
    else:
        def carried(step, carry):
            body(step)
            return carry

        lax.fori_loop(0, count, carried, 0)


def gates_of(packs):
    first = packs[0].shape[1] - LANES
    blocks = [pack[:, first : first + LANES].astype(F32) for pack in packs]
    gates = jnp.concatenate(blocks, axis=0)
    return gates[:, 0:1] + gates[:, 1:2] + gates[:, 2:3]


def half_columns(h, half):
    return pl.multiple_of((lax.axis_index("c") ^ h) * half, half)


def scaled_half(h, own, others, gain, scaled):
    half = scaled.shape[1]
    first, size = half_columns(h, half), 512 if len(others) < 2 else 128
    squares = 0.0
    for start in range(0, half, size):
        columns = pl.ds(pl.multiple_of(first + start, size), size)
        rows = [own[:, columns]] + [other[:, start : start + size] for other in others]
        value = jnp.concatenate([row.astype(F32) for row in rows], axis=0)
        squares = squares + folded(value * value)
        scaled[:, start : start + size] = (value * gain[:, columns]).astype(BF16)
    return squares


def hidden_first_kernel(n_dp, own, *refs):
    others = refs[: n_dp - 1]
    gain, w_gate, w_up, gate_sum, up_sum, square_sum, scaled = refs[n_dp - 1 :]
    half = scaled.shape[1]
    square_sum[...] = scaled_half(0, own, others, gain, scaled)
    size, rows = unit_step(w_gate.shape[1]), pl.ds(half_columns(0, half), half)

    def hidden_units(step):
        columns = pl.ds(place(step, size), size)
        gate_sum[:, columns] = dot(scaled[...], w_gate[rows, columns], ((1,), (0,)))
        up_sum[:, columns] = dot(scaled[...], w_up[rows, columns], ((1,), (0,)))

    loop(w_gate.shape[1] // size, hidden_units, scaled.shape[0] <= FEW_ROWS)


def hidden_rest_kernel(n_dp, own, *refs):
    others = refs[: n_dp - 1]
    gain, w_gate, w_up, gate_sum, up_sum, square_sum, pre_gate, pre_up, act, scales, scaled = refs[n_dp - 1 :]
    half = scaled.shape[1]
    squares = square_sum[...] + scaled_half(1, own, others, gain, scaled)
    scale = lax.rsqrt(jnp.sum(squares, axis=1, keepdims=True) / (2 * half) + EPSILON)
    scales[...] = jnp.broadcast_to(scale, scales.shape)
    size, rows = unit_step(w_gate.shape[1]), pl.ds(half_columns(1, half), half)

    def hidden_units(step):
        columns = pl.ds(place(step, size), size)
        gate_part = scale * (gate_sum[:, columns] + dot(scaled[...], w_gate[rows, columns], ((1,), (0,))))
        up_part = scale * (up_sum[:, columns] + dot(scaled[...], w_up[rows, columns], ((1,), (0,))))
        pre_gate[:, columns] = gate_part
        pre_up[:, columns] = up_part
        act[:, columns] = (gate_part * jax.nn.sigmoid(gate_part) * up_part).astype(BF16)

    loop(w_gate.shape[1] // size, hidden_units, scaled.shape[0] <= FEW_ROWS)


def outward_kernel(i, n_dp, *refs):
    smalls = refs[:n_dp]
    act, w_down, *_, target = refs[n_dp:]
    weight = gates_of(smalls)
    chunk = target.shape[3]
    few = act.shape[0] <= FEW_ROWS
    for j in range(2):
        first = own_columns(i, j, chunk)

        def outward(step):
            columns = pl.ds(pl.multiple_of(first + step * STEP, STEP), STEP)
            part = weight * dot(act[...], w_down[:, columns], ((1,), (0,)))
            store_blocks(target, j, pl.ds(place(step, STEP), STEP), part, n_dp)

        loop(chunk // STEP, outward, few)


def inward_part(i, n_dp, grad_refs, w_gate, w_up, target):
    chunk = target.shape[3]
    few = grad_refs[0].shape[0] <= FEW_ROWS
    for j in range(2):
        first = own_columns(i, j, chunk)

        def inward(step):
            columns = pl.ds(pl.multiple_of(first + step * STEP, STEP), STEP)
            part = 0.0
            for parity, weights in ((0, w_gate), (1, w_up)):
                start = 0
                for ref in grad_refs[parity::2]:
                    part = part + dot(ref[...], weights[columns, start : start + ref.shape[1]], ((1,), (1,)))
                    start += ref.shape[1]
            store_blocks(target, j, pl.ds(place(step, STEP), STEP), part, n_dp)

        loop(chunk // STEP, inward, few)


def gradients(first, weighted, pre_gate, pre_up, w_down, grad_gate, grad_up, few):
    size = unit_step(w_down.shape[0])

    def hidden_units(step):
        columns = pl.ds(place(step, size), size)
        units = pl.ds(first + step * size, size)
        back = dot(weighted[...], w_down[units, :], ((1,), (1,)))
        gate_part, up_part = pre_gate[:, units], pre_up[:, units]
        sig = jax.nn.sigmoid(gate_part)
        grad_gate[:, columns] = (back * up_part * sig * (1.0 + gate_part * (1.0 - sig))).astype(BF16)
        grad_up[:, columns] = (back * gate_part * sig).astype(BF16)

    loop(grad_gate.shape[1] // size, hidden_units, few or grad_gate.shape[1] == size)


def backward_first_kernel(n_dp, *refs):
    grads, smalls = refs[: 2 * n_dp - 1], refs[2 * n_dp - 1 : 3 * n_dp - 1]
    pre_gate, pre_up, w_down, waiting, grad_gate, grad_up, weighted, passed = refs[3 * n_dp - 1 :]
    passed[...] = waiting[...]
    weight = gates_of(smalls)
    few = weighted.shape[0] <= FEW_ROWS

    def weigh(columns, value):
        weighted[:, columns] = (weight * value).astype(BF16)

    both_halves([grads], weighted.shape[1], weigh)
    gradients(0, weighted, pre_gate, pre_up, w_down, grad_gate, grad_up, few)


def backward_rest_kernel(n_dp, weighted, pre_gate, pre_up, w_down, waiting, grad_gate, grad_up, passed):
    passed[...] = waiting[...]
    first = pre_gate.shape[1] - grad_gate.shape[1]
    gradients(first, weighted, pre_gate, pre_up, w_down, grad_gate, grad_up, True)


def inward_kernel(i, n_dp, *refs):
    w_gate, w_up, waiting, target, passed = refs[-5:]
    passed[...] = waiting[...]
    inward_part(i, n_dp, refs[:-5], w_gate, w_up, target)


def join_kernel(n_dp, in_keep, in_other, out_block, *refs):
    for t in range(2 * n_dp):
        k, j = t // 2, t % 2
        refs[t][...] = (in_keep[k, j].astype(F32) + in_other[k, j].astype(F32)).astype(BF16)
    refs[-1][...] = out_block[...]


def own_rows_kernel(n_dp, hid, grads, *refs):
    back, gain, scales, w_out = refs[:4], refs[4], refs[5], refs[6]
    targets, d_half, held, summed, sems = refs[7:9], refs[9], refs[10:12], refs[12], refs[13]
    d_hidden, d_context = held
    copies = [pltpu.make_async_copy(held[n], targets[n], sems.at[n]) for n in range(2)]
    rows, width = hid.shape
    chunk = back[0].shape[1]
    products = 0.0
    for i in range(2):
        for j in range(2):
            columns = pl.ds(pl.multiple_of(own_columns(i, j, chunk), chunk), chunk)
            value = hid[:, columns].astype(F32)
            total = back[i * 2 + j][...].astype(F32) * gain[:, columns]
            summed[:, columns] = total
            products = products + folded(value * total)
    scale = scales[:rows, :1]
    centre = scale * jnp.sum(products, axis=1, keepdims=True) / width
    for start in range(0, width, 512):
        columns = slice(start, start + 512)
        value = summed[:, columns] - hid[:, columns].astype(F32) * scale * centre
        d_hidden[:, columns] = (grads[:, columns].astype(F32) + scale * value).astype(BF16)
    copies[0].start()
    part = width // n_dp
    d_half[...] = d_hidden[:, pl.ds(pl.multiple_of(lax.axis_index("dp") * part, part), part)]
    d_context[...] = dot(d_hidden[...], w_out[...], ((1,), (1,))).astype(BF16)
    copies[1].start()
    for copy in copies:
        copy.wait()


def far_rows_kernel(n_dp, *refs):
    count, far = 2 * (n_dp - 1), n_dp - 1
    hid, grads, packs = refs[:count], refs[count : 2 * count], refs[2 * count : 2 * count + n_dp]
    refs = refs[2 * count + n_dp :]
    back, refs = refs[: 4 * far], refs[4 * far :]
    own, moe, refs = refs[0], refs[1:3], refs[3:]
    d_half, gain, scales, out_target, target, output, held, summed, d_far, sems = refs
    rows, chunk = back[0].shape
    width = summed.shape[1]
    size = width // n_dp // PIECES
    copies = []
    for piece in range(PIECES):
        block = (slice(None), pl.ds(piece * size, size))
        copies.append(pltpu.make_async_copy(held.at[block], target.at[block], sems.at[piece]))
    copies.append(pltpu.make_async_copy(output, out_target, sems.at[PIECES]))
    for i in range(2):
        for j in range(2):
            columns = pl.ds(pl.multiple_of(own_columns(i, j, chunk), chunk), chunk)
            output[:, columns] = (own[:, columns].astype(F32) + moe[i][j].astype(F32)).astype(BF16)
            for k in range(far):
                piece = back[(i * far + k) * 2 + j][...].astype(F32)
                summed[k * rows : (k + 1) * rows, columns] = piece * gain[:, columns]
    copies[PIECES].start()
    half, step = width // 2, 512 if n_dp <= 2 else 128

    def over_halves(body):
        for h in range(2):
            for start in range(0, half, step):
                columns = pl.ds(pl.multiple_of(half_columns(h, half) + start, step), step)
                value, grad = [
                    jnp.concatenate([ref[:, start : start + step].astype(F32) for ref in group[h::2]], axis=0)
                    for group in (hid, grads)
                ]
                body(columns, value, grad)

    sums = [0.0]

    def products(columns, value, grad):
        sums[0] = sums[0] + folded(value * summed[:, columns])

    over_halves(products)
    scale = scales[rows:, :1]
    centre = scale * jnp.sum(sums[0], axis=1, keepdims=True) / width

    def total(columns, value, grad):
        d_far[:, columns] = grad + scale * (summed[:, columns] - value * scale * centre)

    over_halves(total)
    heads = held.shape[0]
    lanes = slice(half, half + heads)
    turned = jnp.concatenate([pack[:, lanes].astype(F32) for pack in packs], axis=0).T.astype(BF16)
    for piece in range(PIECES):
        first = lax.axis_index("dp") * (width // n_dp) + piece * size
        block = slice(piece * size, (piece + 1) * size)
        columns = pl.ds(pl.multiple_of(first, LANES), size)
        both = jnp.concatenate([d_half[:, block].astype(F32), d_far[:, columns]], axis=0).astype(BF16)
        held[:, block] = dot(turned, both, ((1,), (0,))).astype(BF16)
        copies[piece].start()
    for copy in copies:
        copy.wait()


def run(kernel, n_dp, operands, outs, scratch, cost, name, far=(), out_space=pltpu.VMEM):
    spaces = [pltpu.HBM if n in far else pltpu.VMEM for n in range(len(operands))]
    held = [pltpu.with_memory_space_constraint(value, space) for value, space in zip(operands, spaces)]
    places = out_space if isinstance(out_space, list) else [out_space] * len(outs)
    kinds = [place_of(shape, kind) for place_of, (shape, kind) in zip(places, outs)]
    return pl.pallas_call(
        functools.partial(kernel, n_dp),
        out_shape=kinds,
        in_specs=[pl.BlockSpec(memory_space=space) for space in spaces],
        out_specs=[pl.BlockSpec(memory_space=space) for space in places],
        scratch_shapes=scratch,
        compiler_params=pltpu.CompilerParams(vmem_limit_bytes=VMEM_LIMIT if n_dp <= 2 else VMEM_LIMIT_MANY),
        cost_estimate=pl.CostEstimate(flops=0, bytes_accessed=cost, transcendentals=0),
        name=name,
    )(*held)


def per_device(
    hidden_in, norm_gain, route_ids, route_gates, w_gate, w_up, w_down, context, w_out, grad_out
):
    n_dp, n_hi = lax.axis_size("dp"), lax.axis_size("hi")
    rows, width = hidden_in.shape
    top, heads = route_ids.shape[1], context.shape[1]
    all_rows, units, chunk = n_dp * rows, w_gate.shape[2], width // 4

    def swap(value, axes, turn, cross=True):
        count = 2
        for name in axes:
            count *= lax.axis_size(name)
        turn = 2 * turn + (parity(turn) if cross else 0)
        return lax.ppermute(value, axes + ("c",), [(i, i ^ turn) for i in range(count)])

    def other_core(value):
        return lax.ppermute(value, ("c",), [(0, 1), (1, 0)])

    weights = 2 * width * units
    shares = ((n_dp, 2, rows, chunk), BF16)
    wg, wu, wd, gain = w_gate[0], w_up[0], w_down[0], norm_gain.reshape(1, width)
    half = width // 2
    (hid_half,) = run(
        cut_kernel, n_dp, [hidden_in], [((rows, half), BF16)], [pltpu.SemaphoreType.DMA], rows * width, "cut", far=(0,)
    )
    (packed,) = run(
        gates_kernel, n_dp, [route_ids.T, route_gates.T, context, grad_out, wg, wu, wd],
        [((rows, half + heads + LANES), BF16)],
        [pltpu.VMEM((top, rows), jnp.int32), pltpu.VMEM((top, rows), F32), pltpu.SemaphoreType.DMA((4,))],
        4 * weights, "gates", far=range(7),
    )

    def others(value):
        here = [swap(value, ("dp",), k, False) for k in range(1, n_dp)]
        return here, [piece for one in here for piece in (one, other_core(one))]

    hid = [hidden_in] + others(hid_half)[1]
    packs, blocks = others(packed)
    smalls, grads = [packed] + packs, [grad_out] + blocks

    def add(one, other):
        return (one.astype(F32) + other.astype(F32)).astype(BF16)

    def total_of(pieces):
        total = pieces[0].astype(F32)
        for piece in pieces[1:]:
            total = total + piece.astype(F32)
        return total.astype(BF16)

    hidden_units, row_block = ((all_rows, units), F32), ((all_rows, LANES), F32)
    scaled = pltpu.VMEM((all_rows, half), BF16)
    gate_sum, up_sum, square_sum = run(
        hidden_first_kernel, n_dp, [hidden_in] + hid[1::2] + [gain, wg, wu],
        [hidden_units, hidden_units, row_block], [scaled], weights, "hidden_first",
    )
    pre_gate, pre_up, act, scales = run(
        hidden_rest_kernel, n_dp, [hidden_in] + hid[2::2] + [gain, wg, wu, gate_sum, up_sum, square_sum],
        [hidden_units, hidden_units, ((all_rows, units), BF16), row_block], [scaled], weights, "hidden_rest",
    )
    (out_send,) = run(
        functools.partial(outward_kernel, 1), n_dp, smalls + [act, wd], [shares], [],
        weights // 2, "outward_send",
    )
    out_other = other_core(out_send)
    (out_keep,) = run(
        functools.partial(outward_kernel, 0), n_dp, smalls + [act, wd, out_send], [shares], [],
        weights // 2, "outward_keep",
    )
    size = unit_step(units)
    first_units, rest_units = ((all_rows, size), BF16), ((all_rows, units - size), BF16)
    gate_first, up_first, weighted, out_keep = run(
        backward_first_kernel, n_dp, grads + smalls + [pre_gate, pre_up, wd, out_keep],
        [first_units, first_units, ((all_rows, width), BF16), shares], [], weights // 3, "backward_first",
    )
    back_grads = [gate_first, up_first]
    out_half = add(out_keep, out_other)
    out_blocks = [swap(out_half[k], ("dp",), k) for k in range(1, n_dp)]
    block, out_block = (shares[0][1:], BF16), out_half[0]
    if size < units:
        gate_rest, up_rest, out_block = run(
            backward_rest_kernel, n_dp, [weighted, pre_gate, pre_up, wd, out_block],
            [rest_units, rest_units, block], [], weights * 2 // 3, "backward_rest",
        )
        back_grads = back_grads + [gate_rest, up_rest]
    in_send, out_block = run(
        functools.partial(inward_kernel, 1), n_dp, back_grads + [wg, wu, out_block],
        [shares, block], [], weights, "inward_send",
    )
    in_other = other_core(in_send)
    out_block = total_of([out_block] + out_blocks)
    in_keep, out_block = run(
        functools.partial(inward_kernel, 0), n_dp, back_grads + [wg, wu, out_block], [shares, block], [],
        weights, "inward_keep",
    )
    *in_pieces, out_block = run(
        join_kernel, n_dp, [in_keep, in_other, out_block], [((rows, chunk), BF16)] * (2 * n_dp) + [block], [],
        rows * width, "join",
    )
    turns = [t for t in range(2 * n_dp - 1, 0, -1)]
    in_share = total_of([in_pieces[0]] + [swap(in_pieces[t], ("dp", "y"), t) for t in turns])
    out_total = out_block
    in_total = total_of([in_share] + [swap(in_share, ("hi",), t) for t in range(1, n_hi)])
    turn = 1
    while turn < n_hi:
        out_total = add(out_total, swap(out_total, ("hi",), turn))
        if turn == 1:
            out_total = add(out_total, swap(out_total, ("y",), 1)[::-1])
        turn = 2 * turn
    spread = {t: swap(in_total, ("dp", "y"), t) for t in turns}
    back = [in_total] + [spread[t] for t in range(1, 2 * n_dp)]
    crossed = [other_core(one) for one in back]
    moe = [out_total, other_core(out_total)]
    part, far_rows = width // n_dp, all_rows - rows
    whole, context_out, weight_out = ((rows, width), BF16), ((rows, heads), BF16), ((heads, part), BF16)
    d_hidden, d_context, d_half = run(
        own_rows_kernel, n_dp, [hidden_in, grad_out] + back[:2] + crossed[:2] + [gain, scales, w_out],
        [whole, context_out, ((rows, part), BF16)],
        [pltpu.VMEM(*whole), pltpu.VMEM(*context_out), pltpu.VMEM((rows, width), F32), pltpu.SemaphoreType.DMA((2,))],
        weights // 2, "own_rows", out_space=[pltpu.HBM] * 2 + [pltpu.VMEM],
    )
    output, d_w_out = run(
        far_rows_kernel, n_dp,
        hid[1:] + grads[1:] + smalls + back[2:] + crossed[2:] + [hidden_in] + moe + [d_half, gain, scales],
        [whole, weight_out],
        [pltpu.VMEM(*whole), pltpu.VMEM(*weight_out), pltpu.VMEM((far_rows, width), F32),
         pltpu.VMEM((far_rows, width), F32), pltpu.SemaphoreType.DMA((PIECES + 1,))],
        weights // 2, "far_rows", out_space=pltpu.HBM,
    )
    return output, d_hidden, d_context, d_w_out


def solution(mesh):
    n_dp, n_e = mesh.shape["dp"], mesh.shape["expert"]
    names = ("dp", "hi", "y", "c")
    mesh = jax.sharding.Mesh(mesh.devices.reshape(n_dp, n_e // 4, 2, 2), names)
    expert = names[1:]
    return jax.shard_map(
        per_device,
        mesh=mesh,
        in_specs=(
            P("dp", None),
            P(),
            P("dp", None),
            P("dp", None),
            P(expert, None, "dp"),
            P(expert, None, "dp"),
            P(expert, "dp", None),
            P("dp", expert),
            P(expert, None),
            P("dp", None),
        ),
        out_specs=(P("dp", None), P("dp", None), P("dp", expert), P(expert, "dp")),
        check_vma=False,
    )
```

```python
import functools

import jax
import jax.numpy as jnp
from jax import lax
from jax.experimental import pallas as pl
from jax.experimental.pallas import tpu as pltpu
from jax.sharding import PartitionSpec as P

EPSILON = 1e-06
F32 = jnp.float32
BF16 = jnp.bfloat16
STEP = 256
LANES = 128
TERMS = 3
PIECES = 2
LOAD_PIECES = 8
FEW_ROWS = 64
VMEM_LIMIT = 12 * 1024 * 1024
VMEM_LIMIT_MANY = 24 * 1024 * 1024


def dot(a, b, dims):
    return lax.dot_general(a, b, (dims, ((), ())), preferred_element_type=F32)


def place(step, count):
    return pl.multiple_of(step * count, count)


def parity(number):
    shift = 1
    while shift < 32:
        number = number ^ (number >> shift)
        shift = 2 * shift
    return number & 1


def own_half():
    chip = lax.axis_index("dp") ^ lax.axis_index("y") ^ lax.axis_index("hi")
    return lax.axis_index("c") ^ parity(chip)


def own_columns(i, j, width):
    return ((lax.axis_index("y") ^ j) * 2 + (own_half() ^ i)) * width


def folded(value):
    return sum(value[:, start : start + LANES] for start in range(0, value.shape[1], LANES))


def both_halves(refs, width, body):
    core, half = lax.axis_index("c"), width // 2
    size = 512 if len(refs[0]) <= 3 else 128
    for h in range(2):
        for step in range(half // size):
            columns = pl.ds(pl.multiple_of((core ^ h) * half + step * size, size), size)

            def rows_at(group):
                first = group[0][:, columns].astype(F32)
                others = [ref[:, step * size : (step + 1) * size].astype(F32) for ref in group[1 + h :: 2]]
                return jnp.concatenate([first] + others, axis=0)

            body(columns, *[rows_at(group) for group in refs])


def store_blocks(out_ref, j, columns, value, count):
    rows = value.shape[0] // count
    for k in range(count):
        out_ref[k, j, :, columns] = value[k * rows : (k + 1) * rows].astype(BF16)


def cut_kernel(n_dp, source, target, sem):
    width = target.shape[1]
    columns = pl.ds(pl.multiple_of(lax.axis_index("c") * width, width), width)
    copy = pltpu.make_async_copy(source.at[:, columns], target, sem)
    copy.start()
    copy.wait()


def gates_kernel(n_dp, named, weights, context, grads, w_gate, w_up, w_down, packed, named_held, weights_held, sems):
    width, heads = grads.shape[1] // 2, context.shape[1]
    columns = pl.ds(pl.multiple_of(lax.axis_index("c") * width, width), width)
    pairs = [
        (named, named_held), (weights, weights_held), (context, packed.at[:, pl.ds(width, heads)]),
        (grads.at[:, columns], packed.at[:, pl.ds(0, width)]),
    ]
    copies = [pltpu.make_async_copy(*pair, sems.at[n]) for n, pair in enumerate(pairs)]
    for copy in copies:
        copy.start()
    copies[0].wait()
    copies[1].wait()
    rows = context.shape[0]
    expert = (lax.axis_index("hi") * 2 + lax.axis_index("y")) * 2 + lax.axis_index("c")
    row = jnp.sum(jnp.where(named_held[...] == expert, weights_held[...], 0.0), axis=0, keepdims=True)
    square = (rows, rows)
    diagonal = lax.broadcasted_iota(jnp.int32, square, 0) == lax.broadcasted_iota(jnp.int32, square, 1)
    gate = jnp.sum(jnp.where(diagonal, row, 0.0), axis=1, keepdims=True)
    lane = lax.broadcasted_iota(jnp.int32, (rows, LANES), 1)
    rest, block = jnp.broadcast_to(gate, (rows, LANES)), jnp.zeros((rows, LANES), F32)
    for term in range(TERMS):
        rounded = rest.astype(BF16).astype(F32)
        block = jnp.where(lane == term, rounded, block)
        rest = rest - rounded
    packed[:, width + heads :] = block.astype(BF16)
    copies[2].wait()
    copies[3].wait()


def unit_step(units):
    return STEP if units % STEP == 0 else units


def loop(count, body, unroll):
    if unroll:
        for step in range(count):
            body(step)
    else:
        def carried(step, carry):
            body(step)
            return carry

        lax.fori_loop(0, count, carried, 0)


def gates_of(packs):
    first = packs[0].shape[1] - LANES
    blocks = [pack[:, first : first + LANES].astype(F32) for pack in packs]
    gates = jnp.concatenate(blocks, axis=0)
    return gates[:, 0:1] + gates[:, 1:2] + gates[:, 2:3]


def half_columns(h, half):
    return pl.multiple_of((lax.axis_index("c") ^ h) * half, half)


def scaled_half(h, own, others, gain, scaled):
    half = scaled.shape[1]
    first, size = half_columns(h, half), 512 if len(others) < 2 else 128
    squares = 0.0
    for start in range(0, half, size):
        columns = pl.ds(pl.multiple_of(first + start, size), size)
        rows = [own[:, columns]] + [other[:, start : start + size] for other in others]
        value = jnp.concatenate([row.astype(F32) for row in rows], axis=0)
        squares = squares + folded(value * value)
        scaled[:, start : start + size] = (value * gain[:, columns]).astype(BF16)
    return squares


def hidden_first_kernel(n_dp, own, *refs):
    others = refs[: n_dp - 1]
    gain, w_gate, w_up, gate_sum, up_sum, square_sum, scaled = refs[n_dp - 1 :]
    half = scaled.shape[1]
    square_sum[...] = scaled_half(0, own, others, gain, scaled)
    size, rows = unit_step(w_gate.shape[1]), pl.ds(half_columns(0, half), half)

    def hidden_units(step):
        columns = pl.ds(place(step, size), size)
        gate_sum[:, columns] = dot(scaled[...], w_gate[rows, columns], ((1,), (0,)))
        up_sum[:, columns] = dot(scaled[...], w_up[rows, columns], ((1,), (0,)))

    loop(w_gate.shape[1] // size, hidden_units, scaled.shape[0] <= FEW_ROWS)


def hidden_rest_kernel(n_dp, own, *refs):
    others = refs[: n_dp - 1]
    gain, w_gate, w_up, gate_sum, up_sum, square_sum, pre_gate, pre_up, act, scales, scaled = refs[n_dp - 1 :]
    half = scaled.shape[1]
    squares = square_sum[...] + scaled_half(1, own, others, gain, scaled)
    scale = lax.rsqrt(jnp.sum(squares, axis=1, keepdims=True) / (2 * half) + EPSILON)
    scales[...] = jnp.broadcast_to(scale, scales.shape)
    size, rows = unit_step(w_gate.shape[1]), pl.ds(half_columns(1, half), half)

    def hidden_units(step):
        columns = pl.ds(place(step, size), size)
        gate_part = scale * (gate_sum[:, columns] + dot(scaled[...], w_gate[rows, columns], ((1,), (0,))))
        up_part = scale * (up_sum[:, columns] + dot(scaled[...], w_up[rows, columns], ((1,), (0,))))
        pre_gate[:, columns] = gate_part
        pre_up[:, columns] = up_part
        act[:, columns] = (gate_part * jax.nn.sigmoid(gate_part) * up_part).astype(BF16)

    loop(w_gate.shape[1] // size, hidden_units, scaled.shape[0] <= FEW_ROWS)


def outward_kernel(i, n_dp, *refs):
    smalls = refs[:n_dp]
    act, w_down, *_, target = refs[n_dp:]
    weight = gates_of(smalls)
    chunk = target.shape[3]
    few = act.shape[0] <= FEW_ROWS
    for j in range(2):
        first = own_columns(i, j, chunk)

        def outward(step):
            columns = pl.ds(pl.multiple_of(first + step * STEP, STEP), STEP)
            part = weight * dot(act[...], w_down[:, columns], ((1,), (0,)))
            store_blocks(target, j, pl.ds(place(step, STEP), STEP), part, n_dp)

        loop(chunk // STEP, outward, few)


def inward_part(i, n_dp, grad_refs, w_gate, w_up, target):
    chunk = target.shape[3]
    few = grad_refs[0].shape[0] <= FEW_ROWS
    for j in range(2):
        first = own_columns(i, j, chunk)

        def inward(step):
            columns = pl.ds(pl.multiple_of(first + step * STEP, STEP), STEP)
            part = 0.0
            for parity, weights in ((0, w_gate), (1, w_up)):
                start = 0
                for ref in grad_refs[parity::2]:
                    part = part + dot(ref[...], weights[columns, start : start + ref.shape[1]], ((1,), (1,)))
                    start += ref.shape[1]
            store_blocks(target, j, pl.ds(place(step, STEP), STEP), part, n_dp)

        loop(chunk // STEP, inward, few)


def gradients(first, weighted, pre_gate, pre_up, w_down, grad_gate, grad_up, few):
    size = unit_step(w_down.shape[0])

    def hidden_units(step):
        columns = pl.ds(place(step, size), size)
        units = pl.ds(first + step * size, size)
        back = dot(weighted[...], w_down[units, :], ((1,), (1,)))
        gate_part, up_part = pre_gate[:, units], pre_up[:, units]
        sig = jax.nn.sigmoid(gate_part)
        grad_gate[:, columns] = (back * up_part * sig * (1.0 + gate_part * (1.0 - sig))).astype(BF16)
        grad_up[:, columns] = (back * gate_part * sig).astype(BF16)

    loop(grad_gate.shape[1] // size, hidden_units, few or grad_gate.shape[1] == size)


def backward_first_kernel(n_dp, *refs):
    grads, smalls = refs[: 2 * n_dp - 1], refs[2 * n_dp - 1 : 3 * n_dp - 1]
    pre_gate, pre_up, w_down, waiting, grad_gate, grad_up, weighted, passed = refs[3 * n_dp - 1 :]
    passed[...] = waiting[...]
    weight = gates_of(smalls)
    few = weighted.shape[0] <= FEW_ROWS

    def weigh(columns, value):
        weighted[:, columns] = (weight * value).astype(BF16)

    both_halves([grads], weighted.shape[1], weigh)
    gradients(0, weighted, pre_gate, pre_up, w_down, grad_gate, grad_up, few)


def backward_rest_kernel(n_dp, weighted, pre_gate, pre_up, w_down, waiting, grad_gate, grad_up, passed):
    passed[...] = waiting[...]
    first = pre_gate.shape[1] - grad_gate.shape[1]
    gradients(first, weighted, pre_gate, pre_up, w_down, grad_gate, grad_up, True)


def inward_kernel(i, n_dp, *refs):
    w_gate, w_up, waiting, target, passed = refs[-5:]
    passed[...] = waiting[...]
    inward_part(i, n_dp, refs[:-5], w_gate, w_up, target)


def join_kernel(n_dp, in_keep, in_other, out_block, *refs):
    for t in range(2 * n_dp):
        k, j = t // 2, t % 2
        refs[t][...] = (in_keep[k, j].astype(F32) + in_other[k, j].astype(F32)).astype(BF16)
    refs[-1][...] = out_block[...]


def finish_kernel(n_dp, *refs):
    count = 2 * n_dp - 1
    hid, grads, smalls = refs[:count], refs[count : 2 * count], refs[2 * count : 2 * count + n_dp]
    refs = refs[2 * count + n_dp :]
    back, moe = refs[: 4 * n_dp], refs[4 * n_dp : 4 * n_dp + 2]
    refs = refs[4 * n_dp + 2 :]
    gain, scales, w_out, targets, held = refs[0], refs[1], refs[2], refs[3:7], refs[7:11]
    summed, d_all, sems = refs[11:]
    output, d_hidden, d_context, d_w_out = held
    copies = [pltpu.make_async_copy(held[n], targets[n], sems.at[n]) for n in range(3)]
    size = d_w_out.shape[1] // PIECES
    for piece in range(PIECES):
        block = (slice(None), pl.ds(piece * size, size))
        copies.append(pltpu.make_async_copy(d_w_out.at[block], targets[3].at[block], sems.at[3 + piece]))
    rows, width = hid[0].shape
    chunk = moe[0].shape[2]
    for i in range(2):
        for j in range(2):
            columns = pl.ds(pl.multiple_of(own_columns(i, j, chunk), chunk), chunk)
            for k in range(n_dp):
                piece = back[(i * n_dp + k) * 2 + j]
                summed[k * rows : (k + 1) * rows, columns] = piece[...].astype(F32) * gain[:, columns]
            output[:, columns] = (hid[0][:, columns].astype(F32) + moe[i][j].astype(F32)).astype(BF16)
    copies[0].start()

    few = rows * n_dp <= FEW_ROWS
    sums = [0.0]

    def products(columns, value):
        sums[0] = sums[0] + folded(value * summed[:, columns])

    both_halves([hid], width, products)
    scale = scales[:, :1]
    centre = scale * jnp.sum(sums[0], axis=1, keepdims=True) / width

    def total(columns, value, grad):
        result = grad + scale * (summed[:, columns] - value * scale * centre)
        d_all[:, columns] = result.astype(BF16)
        d_hidden[:, columns] = result[:rows].astype(BF16)

    both_halves([hid, grads], width, total)
    copies[1].start()
    heads = d_context.shape[1]
    part = width // n_dp
    lanes = slice(width // 2, width // 2 + heads)
    turned = jnp.concatenate([small[:, lanes].astype(F32) for small in smalls], axis=0).T.astype(BF16)
    size = part // PIECES
    for piece in range(PIECES):
        columns = pl.ds(pl.multiple_of(lax.axis_index("dp") * part + piece * size, LANES), size)
        block = pl.ds(piece * size, size)
        d_w_out[:, block] = dot(turned, d_all[:, columns], ((1,), (0,))).astype(BF16)
        copies[3 + piece].start()
    d_context[...] = dot(d_hidden[...], w_out[...], ((1,), (1,))).astype(BF16)
    copies[2].start()
    for copy in copies:
        copy.wait()


def run(kernel, n_dp, operands, outs, scratch, cost, name, far=(), out_space=pltpu.VMEM):
    spaces = [pltpu.HBM if n in far else pltpu.VMEM for n in range(len(operands))]
    held = [pltpu.with_memory_space_constraint(value, space) for value, space in zip(operands, spaces)]
    kinds = [out_space(shape, kind) for shape, kind in outs]
    return pl.pallas_call(
        functools.partial(kernel, n_dp),
        out_shape=kinds,
        in_specs=[pl.BlockSpec(memory_space=space) for space in spaces],
        out_specs=[pl.BlockSpec(memory_space=out_space)] * len(outs),
        scratch_shapes=scratch,
        compiler_params=pltpu.CompilerParams(vmem_limit_bytes=VMEM_LIMIT if n_dp <= 2 else VMEM_LIMIT_MANY),
        cost_estimate=pl.CostEstimate(flops=0, bytes_accessed=cost, transcendentals=0),
        name=name,
    )(*held)


def per_device(
    hidden_in, norm_gain, route_ids, route_gates, w_gate, w_up, w_down, context, w_out, grad_out
):
    n_dp, n_hi = lax.axis_size("dp"), lax.axis_size("hi")
    rows, width = hidden_in.shape
    top, heads = route_ids.shape[1], context.shape[1]
    all_rows, units, chunk = n_dp * rows, w_gate.shape[2], width // 4

    def swap(value, axes, turn, cross=True):
        count = 2
        for name in axes:
            count *= lax.axis_size(name)
        turn = 2 * turn + (parity(turn) if cross else 0)
        return lax.ppermute(value, axes + ("c",), [(i, i ^ turn) for i in range(count)])

    def other_core(value):
        return lax.ppermute(value, ("c",), [(0, 1), (1, 0)])

    weights = 2 * width * units
    shares = ((n_dp, 2, rows, chunk), BF16)
    wg, wu, wd, gain = w_gate[0], w_up[0], w_down[0], norm_gain.reshape(1, width)
    half = width // 2
    (hid_half,) = run(
        cut_kernel, n_dp, [hidden_in], [((rows, half), BF16)], [pltpu.SemaphoreType.DMA], rows * width, "cut", far=(0,)
    )
    (packed,) = run(
        gates_kernel, n_dp, [route_ids.T, route_gates.T, context, grad_out, wg, wu, wd],
        [((rows, half + heads + LANES), BF16)],
        [pltpu.VMEM((top, rows), jnp.int32), pltpu.VMEM((top, rows), F32), pltpu.SemaphoreType.DMA((4,))],
        4 * weights, "gates", far=range(7),
    )

    def others(value):
        here = [swap(value, ("dp",), k, False) for k in range(1, n_dp)]
        return here, [piece for one in here for piece in (one, other_core(one))]

    hid = [hidden_in] + others(hid_half)[1]
    packs, blocks = others(packed)
    smalls, grads = [packed] + packs, [grad_out] + blocks

    def add(one, other):
        return (one.astype(F32) + other.astype(F32)).astype(BF16)

    def total_of(pieces):
        total = pieces[0].astype(F32)
        for piece in pieces[1:]:
            total = total + piece.astype(F32)
        return total.astype(BF16)

    hidden_units, row_block = ((all_rows, units), F32), ((all_rows, LANES), F32)
    scaled = pltpu.VMEM((all_rows, half), BF16)
    gate_sum, up_sum, square_sum = run(
        hidden_first_kernel, n_dp, [hidden_in] + hid[1::2] + [gain, wg, wu],
        [hidden_units, hidden_units, row_block], [scaled], weights, "hidden_first",
    )
    pre_gate, pre_up, act, scales = run(
        hidden_rest_kernel, n_dp, [hidden_in] + hid[2::2] + [gain, wg, wu, gate_sum, up_sum, square_sum],
        [hidden_units, hidden_units, ((all_rows, units), BF16), row_block], [scaled], weights, "hidden_rest",
    )
    (out_send,) = run(
        functools.partial(outward_kernel, 1), n_dp, smalls + [act, wd], [shares], [],
        weights // 2, "outward_send",
    )
    out_other = other_core(out_send)
    (out_keep,) = run(
        functools.partial(outward_kernel, 0), n_dp, smalls + [act, wd, out_send], [shares], [],
        weights // 2, "outward_keep",
    )
    size = unit_step(units)
    first_units, rest_units = ((all_rows, size), BF16), ((all_rows, units - size), BF16)
    gate_first, up_first, weighted, out_keep = run(
        backward_first_kernel, n_dp, grads + smalls + [pre_gate, pre_up, wd, out_keep],
        [first_units, first_units, ((all_rows, width), BF16), shares], [], weights // 3, "backward_first",
    )
    back_grads = [gate_first, up_first]
    out_half = add(out_keep, out_other)
    out_blocks = [swap(out_half[k], ("dp",), k) for k in range(1, n_dp)]
    block, out_block = (shares[0][1:], BF16), out_half[0]
    if size < units:
        gate_rest, up_rest, out_block = run(
            backward_rest_kernel, n_dp, [weighted, pre_gate, pre_up, wd, out_block],
            [rest_units, rest_units, block], [], weights * 2 // 3, "backward_rest",
        )
        back_grads = back_grads + [gate_rest, up_rest]
    in_send, out_block = run(
        functools.partial(inward_kernel, 1), n_dp, back_grads + [wg, wu, out_block],
        [shares, block], [], weights, "inward_send",
    )
    in_other = other_core(in_send)
    out_block = total_of([out_block] + out_blocks)
    in_keep, out_block = run(
        functools.partial(inward_kernel, 0), n_dp, back_grads + [wg, wu, out_block], [shares, block], [],
        weights, "inward_keep",
    )
    *in_pieces, out_block = run(
        join_kernel, n_dp, [in_keep, in_other, out_block], [((rows, chunk), BF16)] * (2 * n_dp) + [block], [],
        rows * width, "join",
    )
    turns = [t for t in range(2 * n_dp - 1, 0, -1)]
    in_share = total_of([in_pieces[0]] + [swap(in_pieces[t], ("dp", "y"), t) for t in turns])
    out_total = out_block
    in_total = total_of([in_share] + [swap(in_share, ("hi",), t) for t in range(1, n_hi)])
    turn = 1
    while turn < n_hi:
        out_total = add(out_total, swap(out_total, ("hi",), turn))
        if turn == 1:
            out_total = add(out_total, swap(out_total, ("y",), 1)[::-1])
        turn = 2 * turn
    order = [t for t in turns if t < 2] + [t for t in turns if t >= 2]
    spread = {t: swap(in_total, ("dp", "y"), t) for t in order}
    back = [in_total] + [spread[t] for t in range(1, 2 * n_dp)]
    back = back + [other_core(piece) for piece in back]
    moe = [out_total, other_core(out_total)]
    outs = [((rows, width), BF16), ((rows, width), BF16), ((rows, heads), BF16), ((heads, width // n_dp), BF16)]
    return run(
        finish_kernel, n_dp, hid + grads + smalls + back + moe + [gain, scales, w_out], outs,
        [pltpu.VMEM(*out) for out in outs]
        + [pltpu.VMEM((all_rows, width), F32), pltpu.VMEM((all_rows, width), BF16), pltpu.SemaphoreType.DMA((3 + PIECES,))],
        weights, "finish", out_space=pltpu.HBM,
    )


def solution(mesh):
    n_dp, n_e = mesh.shape["dp"], mesh.shape["expert"]
    names = ("dp", "hi", "y", "c")
    mesh = jax.sharding.Mesh(mesh.devices.reshape(n_dp, n_e // 4, 2, 2), names)
    expert = names[1:]
    return jax.shard_map(
        per_device,
        mesh=mesh,
        in_specs=(
            P("dp", None),
            P(),
            P("dp", None),
            P("dp", None),
            P(expert, None, "dp"),
            P(expert, None, "dp"),
            P(expert, "dp", None),
            P("dp", expert),
            P(expert, None),
            P("dp", None),
        ),
        out_specs=(P("dp", None), P("dp", None), P("dp", expert), P(expert, "dp")),
        check_vma=False,
    )
```
